128 devices in a mesh: group: 16 (over z, y), head: 8 (over x, core).
Axes of the slice: x: 4, y: 4, z: 4, core: 2. Of those that a mesh axis runs over, the one named last changes fastest.
Arguments:
- hidden_in: bfloat16 [512, 4, 2048], P('group'), may hold values from -6 to 6
- w_query: bfloat16 [2048, 2048], P(None, 'head'), may hold values from -0.125 to 0.125
- w_key: bfloat16 [2048, 2048], P(None, 'head'), may hold values from -0.125 to 0.125
- w_value: bfloat16 [2048, 4096], P(None, 'head'), may hold values from -0.125 to 0.125
- w_gate_z: bfloat16 [2048, 4096], P(None, 'head'), may hold values from -0.125 to 0.125
- w_write: bfloat16 [2048, 32], P(None, 'head'), may hold values from -0.125 to 0.125
- w_decay: bfloat16 [2048, 32], P(None, 'head'), may hold values from -0.125 to 0.125
- conv_query: bfloat16 [4, 2048], P(None, 'head'), may hold values from -3 to 3
- conv_key: bfloat16 [4, 2048], P(None, 'head'), may hold values from -3 to 3
- conv_value: bfloat16 [4, 4096], P(None, 'head'), may hold values from -3 to 3
- decay_rate: float32 [32], P('head'), may hold values from 0.02 to 1.5
- dt_bias: float32 [32], P('head'), may hold values from -1 to 1
- norm_gain: float32 [128], replicated, may hold values from 0.1 to 1.9
- w_out: bfloat16 [4096, 2048], P('head'), may hold values from -0.125 to 0.125
- states: float32 [512, 32, 128, 128], P('group', 'head'), may hold values from -3 to 3
- tail_query: float32 [512, 3, 2048], P('group', None, 'head'), may hold values from -6 to 6
- tail_key: float32 [512, 3, 2048], P('group', None, 'head'), may hold values from -6 to 6
- tail_value: float32 [512, 3, 4096], P('group', None, 'head'), may hold values from -6 to 6
- send_slot: int32 [16, 16, 2], P('group'), may hold values from -1 to 31, as said below
- recv_slot: int32 [16, 16, 2], P('group'), may hold values from -1 to 31, as said below
- live_count: int32 [16], P('group'), may hold values from 8 to 32, as said below
Outputs:
- layer_out: bfloat16 [512, 4, 2048], P('group', None, 'head')
- new_states: float32 [512, 32, 128, 128], P('group', 'head')
- new_tail_query: float32 [512, 3, 2048], P('group', None, 'head')
- new_tail_key: float32 [512, 3, 2048], P('group', None, 'head')
- new_tail_value: float32 [512, 3, 4096], P('group', None, 'head')
The draws below stay inside these ranges and needn't reach their ends.
Inputs may be any that keep to these rules, and one draw needn't show every extreme that they name: `send_slot`: no group sends to itself; the slots named by one group's entries are distinct; one pair carries at most 2 requests, and every draw has a group that receives 2 from every other group. recv_slot[h, g, c] is -1 exactly where send_slot[g, h, c] is -1; the slots named by one receiving group are distinct. `live_count`: some group is full in every draw.
All inputs are finite; a program needn't handle non-finite values.
Results may differ from the reference program's by a relative error of at most 0.0049.
Values sent between devices are 32-bit elements; how exact they have to be, the bound alone decides.
No kernel may reach another device: no remote copies, remote signals or barrier semaphores. Data moves between devices by JAX's collectives and lax.ppermute only.
A program may use at most 128 MiB of HBM per device.

```python
import math
import jax
import jax.numpy as jnp
from jax import lax

D = 2048
HV = 32
HK = 16
DK = 128
DV = 128
CONV = 4
SLOTS = 32
STEPS = 4
CAP = 2
GROUPS = 16
REQS = 512


def migration_tables(key):
    key_active, key_send, key_recv, key_full, key_hub = jax.random.split(key, 5)
    active = jax.random.randint(key_active, (GROUPS, GROUPS, CAP), 0, 5) < 3
    source_ids = jnp.arange(GROUPS, dtype=jnp.int32)
    hub = jax.random.randint(key_hub, (), 0, GROUPS)
    favourite = (source_ids + 1 + jax.random.randint(key_full, (GROUPS,), 0, GROUPS - 1)) % GROUPS
    forced = (source_ids[None, :] == favourite[:, None]) | (source_ids[None, :] == hub)
    active = active | forced[:, :, None]
    no_self = source_ids[:, None] != source_ids[None, :]
    active = active & no_self[:, :, None]
    send_perm = jax.vmap(lambda sub: jax.random.permutation(sub, SLOTS))(jax.random.split(key_send, GROUPS))
    recv_perm = jax.vmap(lambda sub: jax.random.permutation(sub, SLOTS))(jax.random.split(key_recv, GROUPS))
    send_view = send_perm[:, :GROUPS * CAP].reshape(GROUPS, GROUPS, CAP).astype(jnp.int32)
    recv_view = recv_perm[:, :GROUPS * CAP].reshape(GROUPS, GROUPS, CAP).astype(jnp.int32)
    send_table = jnp.where(active, send_view, -1).astype(jnp.int32)
    recv_active = jnp.transpose(active, (1, 0, 2))
    recv_table = jnp.where(recv_active, recv_view, -1).astype(jnp.int32)
    return (send_table, recv_table)


def draw_send_slot(key, part):
    return migration_tables(key)[0]


def draw_recv_slot(key, part):
    return migration_tables(key)[1]


def draw_live_count(key, part):
    key = jax.random.fold_in(key, 7)
    key_counts, key_full, key_low = jax.random.split(key, 3)
    counts = jax.random.randint(key_counts, (GROUPS,), SLOTS // 4, SLOTS + 1)
    full_group = jax.random.randint(key_full, (), 0, GROUPS)
    low_group = (full_group + 1 + jax.random.randint(key_low, (), 0, GROUPS - 1)) % GROUPS
    counts = counts.at[full_group].set(SLOTS)
    counts = counts.at[low_group].set(SLOTS // 4)
    return counts.astype(jnp.int32)


def spiked(array, key, source, target, parts, factor):
    owner, partner = [(jnp.arange(array.shape[position]) // (array.shape[position] // parts)).reshape([-1 if axis == position else 1 for axis in range(array.ndim)]) for position in (source, target)]
    chosen = jax.random.permutation(key, parts)[partner]
    strong = (owner == chosen) | (owner == (partner + parts // 2) % parts)
    return jnp.where(strong, factor * array, array)


def block_scale(own_key, dims, cuts, low, top_value):
    level = 1.0
    for axis_at, blocks in cuts:
        draws = jax.random.uniform(jax.random.fold_in(jax.random.fold_in(own_key, 6), axis_at), (blocks,), jnp.float32, low / len(cuts), top_value / len(cuts))
        level = level * jnp.repeat(jnp.exp(draws), dims[axis_at] // blocks).reshape((-1,) + (1,) * (len(dims) - 1 - axis_at))
    return level


def scatter_about(rng, extent, scale, most, shards=(), kind=jnp.bfloat16):
    loudness = block_scale(rng, extent, shards, -0.22, 0.18) if shards else 1.0
    values = jax.random.normal(rng, extent, jnp.float32) * scale * loudness
    return jnp.minimum(jnp.maximum(values, -most), most).astype(kind)


def bell_draw_with(key, dims, width, most, cuts, heavy, kind=jnp.bfloat16):
    drawn = width * jax.random.normal(key, dims, jnp.float32)
    if cuts:
        drawn = drawn * block_scale(key, dims, cuts, -0.22, 0.18)
    return jnp.clip(spiked(drawn, jax.random.fold_in(key, 3), *heavy), -most, most).astype(kind)


def setup_inputs(seed: int = 0) -> dict:
    key_list = jax.random.split(jax.random.key(seed), 22)
    hidden_in = scatter_about(key_list[0], (REQS, STEPS, D), 1.0, 6.0, ((0, 16),))
    w_query = scatter_about(key_list[1], (D, HK * DK), D ** -0.5, 0.125, ((1, 8),))
    w_key = scatter_about(key_list[2], (D, HK * DK), D ** -0.5, 0.125, ((1, 8),))
    w_value = scatter_about(key_list[3], (D, HV * DV), D ** -0.5, 0.125, ((1, 8),))
    w_gate_z = scatter_about(key_list[4], (D, HV * DV), D ** -0.5, 0.125, ((1, 8),))
    w_write = scatter_about(key_list[5], (D, HV), D ** -0.5, 0.125, ((1, 8),))
    w_decay = scatter_about(key_list[6], (D, HV), D ** -0.5, 0.125, ((1, 8),))
    conv_query = scatter_about(key_list[7], (CONV, HK * DK), CONV ** -0.5, 3.0, ((1, 8),))
    conv_key = scatter_about(key_list[8], (CONV, HK * DK), CONV ** -0.5, 3.0, ((1, 8),))
    conv_value = scatter_about(key_list[9], (CONV, HV * DV), CONV ** -0.5, 3.0, ((1, 8),))
    decay_rate = jnp.clip(jnp.exp(math.log(1.5) - 4.317488 * jax.random.uniform(key_list[10], (HV,), jnp.float32) ** block_scale(key_list[10], (HV,), ((0, 8),), -0.2, 0.2)), 0.02, 1.5)
    dt_bias = jnp.clip(jax.random.uniform(key_list[11], (HV,), jnp.float32, -1.0, 1.0) * block_scale(key_list[11], (HV,), ((0, 8),), -0.4, 0.0), -1.0, 1.0)
    norm_gain = jnp.clip(1.0 + 0.18 * jax.random.normal(key_list[12], (DV,), jnp.float32), 0.1, 1.9)
    w_out = bell_draw_with(key_list[13], (HV * DV, D), (HV * DV) ** -0.5, 0.125, ((0, 8),), (0, 1, 8, 2.0))
    states = scatter_about(key_list[14], (REQS, HV, DK, DV), 0.3, 3.0, ((0, 16), (1, 8)), jnp.float32)
    tail_query = scatter_about(key_list[15], (REQS, CONV - 1, HK * DK), 1.0, 6.0, ((0, 16), (2, 8)), jnp.float32)
    tail_key = scatter_about(key_list[16], (REQS, CONV - 1, HK * DK), 1.0, 6.0, ((0, 16), (2, 8)), jnp.float32)
    tail_value = scatter_about(key_list[17], (REQS, CONV - 1, HV * DV), 1.0, 6.0, ((0, 16), (2, 8)), jnp.float32)
    send_slot = draw_send_slot(jax.random.fold_in(key_list[21], 71), 0)
    recv_slot = draw_recv_slot(jax.random.fold_in(key_list[21], 71), 0)
    live_count = draw_live_count(jax.random.fold_in(key_list[21], 71), 0)
    return dict(hidden_in=hidden_in, w_query=w_query, w_key=w_key, w_value=w_value, w_gate_z=w_gate_z, w_write=w_write, w_decay=w_decay, conv_query=conv_query, conv_key=conv_key, conv_value=conv_value, decay_rate=decay_rate, dt_bias=dt_bias, norm_gain=norm_gain, w_out=w_out, states=states, tail_query=tail_query, tail_key=tail_key, tail_value=tail_value, send_slot=send_slot, recv_slot=recv_slot, live_count=live_count)


def unit_norm(vector):
    return vector / jnp.sqrt(lax.optimization_barrier(jnp.sum(vector * vector, -1, keepdims=True)) + 1e-06)

def short_conv(tail_rows, projected, kernel):
    window = jnp.concatenate([tail_rows, projected], axis=1)
    count = projected.shape[1]
    taps = kernel.astype(jnp.float32)
    mixed = window[:, 0:count] * taps[0]
    for offset in range(1, taps.shape[0]):
        mixed = mixed + window[:, offset:offset + count] * taps[offset]
    return (jax.nn.silu(mixed), window[:, count:])

def decode_block(memory, tail_query, tail_key, tail_value, proj_query, proj_key, proj_value, proj_gate, proj_write, proj_decay, conv_query, conv_key, conv_value, decay_rate, dt_bias, norm_gain):
    num_req = proj_query.shape[0]
    step_count = proj_query.shape[1]
    value_heads = memory.shape[1]
    key_dim = memory.shape[2]
    value_dim = memory.shape[3]
    conv_q, new_tq = short_conv(tail_query, proj_query, conv_query)
    conv_k, new_tk = short_conv(tail_key, proj_key, conv_key)
    conv_v, new_tv = short_conv(tail_value, proj_value, conv_value)
    key_heads = conv_q.shape[2] // key_dim
    head_ratio = value_heads // key_heads
    queries = unit_norm(conv_q.reshape(num_req, step_count, key_heads, key_dim)) * key_dim ** (-0.5)
    keys_unit = unit_norm(conv_k.reshape(num_req, step_count, key_heads, key_dim))
    queries = jnp.repeat(queries, head_ratio, axis=2)
    keys_unit = jnp.repeat(keys_unit, head_ratio, axis=2)
    values = conv_v.reshape(num_req, step_count, value_heads, value_dim)
    write_rate = jax.nn.sigmoid(proj_write)
    log_decay = -decay_rate * jax.nn.softplus(proj_decay + dt_bias)
    readouts = []
    for step in range(step_count):
        memory = memory * jnp.exp(log_decay[:, step])[:, :, None, None]
        key_now = keys_unit[:, step][:, :, :, None]
        recalled = lax.optimization_barrier(jnp.sum(memory * key_now, axis=2))
        correction = (values[:, step] - recalled) * write_rate[:, step][:, :, None]
        memory = memory + key_now * correction[:, :, None, :]
        readouts.append(lax.optimization_barrier(jnp.sum(memory * queries[:, step][:, :, :, None], axis=2)))
    readout = jnp.stack(readouts, axis=1)
    gate_rows = proj_gate.reshape(num_req, step_count, value_heads, value_dim)
    normed = readout * lax.rsqrt(lax.optimization_barrier(jnp.mean(readout * readout, -1, keepdims=True)) + 1e-06)
    normed = normed * norm_gain * jax.nn.silu(gate_rows)
    normed = normed.reshape(num_req, step_count, value_heads * value_dim).astype(jnp.bfloat16)
    return (normed, memory, new_tq, new_tk, new_tv)

def reference(hidden_in, w_query, w_key, w_value, w_gate_z, w_write, w_decay, conv_query, conv_key, conv_value, decay_rate, dt_bias, norm_gain, w_out, states, tail_query, tail_key, tail_value, send_slot, recv_slot, live_count):
    flat_rows = hidden_in.reshape(GROUPS * SLOTS * STEPS, D)

    def project(weight):
        product = jnp.dot(flat_rows, weight, preferred_element_type=jnp.float32)
        return product.reshape(GROUPS, SLOTS, STEPS, weight.shape[1])
    proj_query = project(w_query)
    proj_key = project(w_key)
    proj_value = project(w_value)
    proj_gate = project(w_gate_z)
    proj_write = project(w_write)
    proj_decay = project(w_decay)
    group_base = jnp.arange(GROUPS, dtype=jnp.int32) * SLOTS
    sender = jnp.transpose(send_slot, (1, 0, 2))
    source = (group_base[None, :, None] + sender).astype(jnp.int32)
    target = jnp.where(recv_slot >= 0, group_base[:, None, None] + recv_slot, GROUPS * SLOTS).astype(jnp.int32)
    source_index = jnp.arange(GROUPS * SLOTS, dtype=jnp.int32).at[target.reshape(-1)].set(source.reshape(-1), mode='drop')
    is_live = jnp.arange(SLOTS, dtype=jnp.int32)[None, :] < live_count[:, None]

    def one_group(block):
        slot_index, part_q, part_k, part_v, part_g, part_w, part_d, live_rows = block
        moved = states[slot_index]
        moved_tq = tail_query[slot_index]
        moved_tk = tail_key[slot_index]
        moved_tv = tail_value[slot_index]
        normed, memory, new_tq, new_tk, new_tv = decode_block(moved, moved_tq, moved_tk, moved_tv, part_q, part_k, part_v, part_g, part_w, part_d, conv_query, conv_key, conv_value, decay_rate, dt_bias, norm_gain)
        result = jnp.dot(normed.reshape(SLOTS * STEPS, HV * DV), w_out, preferred_element_type=jnp.float32)
        result = result.astype(jnp.bfloat16).reshape(SLOTS, STEPS, D)
        result = jnp.where(live_rows[:, None, None], result, jnp.zeros_like(result))
        memory = jnp.where(live_rows[:, None, None, None], memory, moved)
        new_tq = jnp.where(live_rows[:, None, None], new_tq, moved_tq)
        new_tk = jnp.where(live_rows[:, None, None], new_tk, moved_tk)
        new_tv = jnp.where(live_rows[:, None, None], new_tv, moved_tv)
        return (result, memory, new_tq, new_tk, new_tv)
    blocks = (source_index.reshape(GROUPS, SLOTS), proj_query, proj_key, proj_value, proj_gate, proj_write, proj_decay, is_live)
    layer_out, new_states, new_tq, new_tk, new_tv = lax.map(one_group, blocks)
    return (layer_out.reshape(GROUPS * SLOTS, STEPS, D), new_states.reshape(GROUPS * SLOTS, HV, DK, DV), new_tq.reshape(GROUPS * SLOTS, CONV - 1, HK * DK), new_tk.reshape(GROUPS * SLOTS, CONV - 1, HK * DK), new_tv.reshape(GROUPS * SLOTS, CONV - 1, HV * DV))
```

```python
import functools

import jax
import jax.numpy as jnp
from jax import lax
from jax.experimental import pallas as pl
from jax.experimental.pallas import tpu as pltpu
from jax.sharding import PartitionSpec as P

SMEM = pl.BlockSpec(memory_space=pltpu.SMEM)
VMEM = pl.BlockSpec(memory_space=pltpu.VMEM)
ANY = pl.BlockSpec(memory_space=pl.ANY)
LANES = 128


def params(mib):
    return pltpu.CompilerParams(vmem_limit_bytes=mib * 1024 * 1024)


def cost(flops, moved):
    return pl.CostEstimate(flops=flops, bytes_accessed=moved, transcendentals=0)


def pack_first(send, ids, states, tq, tk, tv, out, rows, sem, tail_sem):
    count, slots = send.shape[0], states.shape[0]
    half = states.shape[1] // 2
    extra = rows.shape[1]

    def copy(i, carry):
        pltpu.make_async_copy(
            states.at[send[i], pl.ds(0, half)], out.at[i, pl.ds(0, half)], sem
        ).start()
        return carry

    lax.fori_loop(0, count, copy, 0, unroll=8)
    pick = lax.broadcasted_iota(jnp.int32, (count, slots), 1) == ids[...]
    pick = pick.astype(jnp.float32)
    at = 0
    for j in range(tq.shape[0]):
        for ref in (tq, tk, tv):
            chosen = jnp.dot(
                pick, ref[j], precision=lax.Precision.HIGHEST, preferred_element_type=jnp.float32
            )
            for g in range(ref.shape[2] // LANES):
                rows[:, at, :] = chosen[:, g * LANES : (g + 1) * LANES]
                at += 1
    tail_copy = pltpu.make_async_copy(rows, out.at[:, pl.ds(half, extra)], tail_sem)
    tail_copy.start()
    pltpu.make_async_copy(
        states.at[:, pl.ds(0, half)], out.at[:, pl.ds(0, half)], sem
    ).wait()
    tail_copy.wait()


def pack_second(send, states, out, sem):
    count = send.shape[0]
    half = states.shape[1] // 2

    def copy(i, carry):
        pltpu.make_async_copy(
            states.at[send[i], pl.ds(half, half)], out.at[i], sem
        ).start()
        return carry

    lax.fori_loop(0, count, copy, 0, unroll=8)
    pltpu.make_async_copy(states.at[:, pl.ds(half, half)], out, sem).wait()


def prepare(
    recv, live, rows, tq, tk, tv, pq, pk, pv, cq, ck, cv,
    x_ref, v_ref, ntq, ntk, ntv,
):
    taps, slots = tq.shape[0], tq.shape[1]
    count = recv.shape[1]
    put = lax.broadcasted_iota(jnp.int32, (slots, count), 0) == recv[...]
    put = put.astype(jnp.float32)
    arrived = jnp.sum(put, axis=1, keepdims=True) > 0.0
    moved = {ref: [] for ref in range(3)}
    at = 0
    for j in range(taps):
        for n, ref in enumerate((tq, tk, tv)):
            groups = ref.shape[2] // LANES
            sent = jnp.concatenate([rows[:, at + g, :] for g in range(groups)], axis=1)
            at += groups
            sent = jnp.dot(
                put, sent, precision=lax.Precision.HIGHEST, preferred_element_type=jnp.float32
            )
            moved[n].append(jnp.where(arrived, sent, ref[j]))
    steps = pq.shape[0]
    is_live = lax.broadcasted_iota(jnp.int32, (slots, 1), 0) < live[0]

    def conv(moved, proj, kernel, new):
        window = [moved[j] for j in range(taps)] + [proj[t] for t in range(steps)]
        outs = []
        for t in range(steps):
            mixed = window[t] * kernel[0:1, :]
            for j in range(1, taps + 1):
                mixed = mixed + window[t + j] * kernel[j : j + 1, :]
            outs.append(mixed * jax.nn.sigmoid(mixed))
        for j in range(taps):
            new[j] = jnp.where(is_live, window[steps + j], window[j])
        return outs

    def unit(v, scale):
        parts = []
        for h in range(v.shape[1] // LANES):
            part = v[:, h * LANES : (h + 1) * LANES]
            total = jnp.sum(part * part, axis=1, keepdims=True)
            parts.append(part * (lax.rsqrt(total + 1e-06) * scale))
        return jnp.concatenate(parts, axis=1)

    outs = conv(moved[0], pq, cq, ntq)
    for t in range(steps):
        x_ref[steps + t] = unit(outs[t], LANES**-0.5)
    outs = conv(moved[1], pk, ck, ntk)
    for t in range(steps):
        x_ref[t] = unit(outs[t], 1.0)
    outs = conv(moved[2], pv, cv, ntv)
    for t in range(steps):
        v_ref[t] = outs[t]


def fetch(src, r, states, recv, row, size, dst, sem):
    @pl.when(src[r] >= 0)
    def _():
        pltpu.make_async_copy(recv.at[src[r], pl.ds(0, size)], dst, sem).start()

    @pl.when(src[r] < 0)
    def _():
        pltpu.make_async_copy(states.at[r, pl.ds(row, size)], dst, sem).start()


def split(v):
    high = v.astype(jnp.bfloat16)
    return high, (v - high.astype(jnp.float32)).astype(jnp.bfloat16)


def read_heads(
    half, src, live, states, recv, xs, xt, v_ref, gate, decay, write, gain,
    normed, u_ref, buf, pr, sems,
):
    slots = states.shape[0]
    size = buf.shape[1]
    dim = LANES
    steps = v_ref.shape[0]
    key_lanes = pl.ds(half * dim, dim)

    def start(r, carry):
        fetch(src, r, states, recv, half * size, size, buf.at[r], sems.at[r])
        return carry

    lax.fori_loop(0, slots, start, 0)

    def project(r, carry):
        pltpu.make_async_copy(states.at[0, pl.ds(0, size)], buf.at[r], sems.at[r]).wait()
        state = jnp.concatenate([buf[r, 0:dim, :], buf[r, dim : 2 * dim, :]], axis=1)
        high, low = split(state)
        x_high, x_low = split(xs[r, :, key_lanes])
        both = jnp.concatenate([x_high, x_low], axis=0)
        a = jnp.dot(both, high, preferred_element_type=jnp.float32)
        b = jnp.dot(both, low, preferred_element_type=jnp.float32)
        n = 2 * steps
        pr[r] = a[0:n] + a[n : 2 * n] + b[0:n] + b[n : 2 * n]
        return carry

    lax.fori_loop(0, slots, project, 0, unroll=4)

    is_live = lax.broadcasted_iota(jnp.int32, (slots, 1), 0) < live[0]
    keys = [xt[t, :, key_lanes] for t in range(steps)]
    queries = [xt[steps + t, :, key_lanes] for t in range(steps)]
    inner = lambda a, b: jnp.sum(a * b, axis=1, keepdims=True)
    kk = {(s, t): inner(keys[s], keys[t]) for t in range(steps) for s in range(t)}
    kq = {(s, t): inner(keys[s], queries[t]) for t in range(steps) for s in range(t + 1)}
    for h in range(2):
        head = 2 * half + h
        lanes = pl.ds(h * dim, dim)
        wide = pl.ds(head * dim, dim)
        fall = [decay[t, :, head : head + 1] for t in range(steps)]
        rate = [write[t, :, head : head + 1] for t in range(steps)]
        ratio = {}
        for s in range(steps):
            ratio[s, s] = None
            for t in range(s + 1, steps):
                ratio[s, t] = fall[t] if t == s + 1 else ratio[s, t - 1] * fall[t]
        total = [fall[0]]
        for t in range(1, steps):
            total.append(total[-1] * fall[t])
        us = []
        for t in range(steps):
            gap = v_ref[t, :, wide] - total[t] * pr[:, t, lanes]
            for s in range(t):
                gap = gap - (ratio[s, t] * kk[s, t]) * us[s]
            us.append(gap * rate[t])
            out = total[t] * pr[:, steps + t, lanes]
            for s in range(t + 1):
                weight = kq[s, t] if s == t else ratio[s, t] * kq[s, t]
                out = out + weight * us[s]
            mean = jnp.mean(out * out, axis=1, keepdims=True)
            z = gate[t, :, wide]
            out = out * lax.rsqrt(mean + 1e-06) * gain[...] * (z * jax.nn.sigmoid(z))
            normed[t, :, lanes] = out.astype(normed.dtype)
        for s in range(steps):
            last = us[s] if s == steps - 1 else ratio[s, steps - 1] * us[s]
            u_ref[:, s, lanes] = jnp.where(is_live, last, 0.0)
        u_ref[:, steps, lanes] = jnp.broadcast_to(
            jnp.where(is_live, total[-1], 1.0), (slots, dim)
        )


def update(
    src, states, recv1, recv2, xs, u1, u2, out, buf, in_sems, out_sems
):
    slots = states.shape[0]
    size = states.shape[1] // 2
    dim = LANES
    steps = xs.shape[1] // 2

    def start(r, carry):
        fetch(src, r, states, recv1, 0, size, buf.at[r, pl.ds(0, size)], in_sems.at[r])
        fetch(src, r, states, recv2, size, size, buf.at[r, pl.ds(size, size)], in_sems.at[r])
        return carry

    lax.fori_loop(0, slots, start, 0)

    def one(r, carry):
        pltpu.make_async_copy(states.at[0], buf.at[r], in_sems.at[r]).wait()
        for half, u in enumerate((u1, u2)):
            k_high, k_low = split(xs[r, 0:steps, pl.ds(half * dim, dim)])
            rows = u[r]
            u_high, u_low = split(rows[0:steps])
            wide = lambda v: v.astype(jnp.float32)
            left = jnp.concatenate([wide(k_high), wide(k_high), wide(k_low), wide(k_low)], axis=0)
            right = jnp.concatenate([wide(u_high), wide(u_low), wide(u_high), wide(u_low)], axis=0)
            change = lax.dot_general(
                left.T.astype(jnp.bfloat16),
                right.astype(jnp.bfloat16),
                (((1,), (0,)), ((), ())),
                preferred_element_type=jnp.float32,
            )
            for h in range(2):
                at = pl.ds(half * size + h * dim, dim)
                lanes = slice(h * dim, (h + 1) * dim)
                scale = rows[steps : steps + 1, lanes]
                buf[r, at, :] = buf[r, at, :] * scale + change[:, lanes]
        pltpu.make_async_copy(buf.at[r], out.at[r], out_sems.at[r]).start()
        return carry

    lax.fori_loop(0, slots, one, 0, unroll=2)

    def finish(r, carry):
        pltpu.make_async_copy(buf.at[r], out.at[r], out_sems.at[r]).wait()
        return carry

    lax.fori_loop(0, slots, finish, 0)


def shards(
    hidden_in, w_query, w_key, w_value, w_gate_z, w_write, w_decay,
    conv_query, conv_key, conv_value, decay_rate, dt_bias, norm_gain, w_out,
    states, tail_query, tail_key, tail_value, send_slot, recv_slot, live_count,
):
    slots, steps, width = hidden_in.shape
    heads, dim = states.shape[1], states.shape[2]
    f32 = jnp.float32
    rows = heads * dim
    half = rows // 2
    flat_states = states.reshape(slots, rows, dim)
    tails = [jnp.transpose(t, (1, 0, 2)) for t in (tail_query, tail_key, tail_value)]
    taps = tails[0].shape[0]
    extra = taps * sum(t.shape[2] for t in tails) // LANES
    send = jnp.maximum(send_slot.reshape(-1), 0)
    recv = recv_slot.reshape(-1)
    count = send.shape[0]
    place = jnp.arange(slots, dtype=jnp.int32)
    order = jnp.arange(count, dtype=jnp.int32)
    src = jnp.max(jnp.where(recv[None, :] == place[:, None], order[None, :], -1), axis=1)

    first = pl.pallas_call(
        pack_first,
        out_shape=jax.ShapeDtypeStruct((count, half + extra, LANES), f32),
        in_specs=[SMEM, VMEM, ANY, VMEM, VMEM, VMEM],
        out_specs=ANY,
        scratch_shapes=[
            pltpu.VMEM((count, extra, LANES), f32),
            pltpu.SemaphoreType.DMA,
            pltpu.SemaphoreType.DMA,
        ],
        compiler_params=params(16),
        cost_estimate=cost(0, 2 * count * half * LANES * 4),
        name="pack_first",
    )(send, send.reshape(count, 1), flat_states, *tails)
    second = pl.pallas_call(
        pack_second,
        out_shape=jax.ShapeDtypeStruct((count, half, LANES), f32),
        in_specs=[SMEM, ANY],
        out_specs=ANY,
        scratch_shapes=[pltpu.SemaphoreType.DMA],
        compiler_params=params(16),
        cost_estimate=cost(0, 2 * count * half * LANES * 4),
        name="pack_second",
    )(send, flat_states)
    recv1 = lax.all_to_all(first, "group", split_axis=0, concat_axis=0, tiled=True)
    recv2 = lax.all_to_all(second, "group", split_axis=0, concat_axis=0, tiled=True)

    flat_hidden = jnp.transpose(hidden_in, (1, 0, 2)).reshape(steps * slots, width)

    def project(weight):
        product = jnp.dot(flat_hidden, weight, preferred_element_type=f32)
        return product.reshape(steps, slots, weight.shape[1])

    pq, pk, pv, pg = (project(w) for w in (w_query, w_key, w_value, w_gate_z))
    write = jax.nn.sigmoid(project(w_write))
    decay = jnp.exp(-decay_rate * jax.nn.softplus(project(w_decay) + dt_bias))

    small = recv1[:, half:, :]
    kernels = [c.astype(f32) for c in (conv_query, conv_key, conv_value)]
    tail_shapes = [jax.ShapeDtypeStruct(t.shape, f32) for t in tails]
    xt, values, ntq, ntk, ntv = pl.pallas_call(
        prepare,
        out_shape=[
            jax.ShapeDtypeStruct((2 * steps, slots, pq.shape[2]), f32),
            jax.ShapeDtypeStruct(pv.shape, f32),
            *tail_shapes,
        ],
        in_specs=[VMEM, SMEM] + [VMEM] * 10,
        out_specs=[VMEM] * 5,
        compiler_params=params(24),
        cost_estimate=cost(2_000_000, 3_000_000),
        name="prepare",
    )(recv.reshape(1, count), live_count, small, *tails, pq, pk, pv, *kernels)
    xs = jnp.transpose(xt, (1, 0, 2))

    def read(index, arrived):
        return pl.pallas_call(
            functools.partial(read_heads, index),
            out_shape=[
                jax.ShapeDtypeStruct((steps, slots, 2 * dim), jnp.bfloat16),
                jax.ShapeDtypeStruct((slots, 2 * steps, 2 * dim), f32),
            ],
            in_specs=[SMEM, SMEM, ANY, ANY] + [VMEM] * 7,
            out_specs=[VMEM] * 2,
            scratch_shapes=[
                pltpu.VMEM((slots, half, dim), f32),
                pltpu.VMEM((slots, 2 * steps, 2 * dim), f32),
                pltpu.SemaphoreType.DMA((slots,)),
            ],
            compiler_params=params(32),
            cost_estimate=cost(64_000_000, 6_000_000),
            name="read_heads",
        )(
            src, live_count, flat_states, arrived, xs, xt, values, pg, decay, write,
            norm_gain.reshape(1, dim),
        )

    normed1, u1 = read(0, recv1)
    normed2, u2 = read(1, recv2)
    normed = jnp.concatenate([normed1, normed2], axis=2).reshape(steps * slots, rows)
    partial = jnp.dot(normed, w_out, preferred_element_type=f32)
    parts = lax.axis_size("head")
    pieces = jnp.transpose(
        partial.reshape(steps * slots, parts, width // parts), (1, 0, 2)
    )
    shared = lax.all_to_all(pieces, "head", split_axis=0, concat_axis=0, tiled=True)

    new_states = pl.pallas_call(
        update,
        out_shape=jax.ShapeDtypeStruct((slots, rows, dim), f32),
        in_specs=[SMEM] + [ANY] * 3 + [VMEM] * 3,
        out_specs=ANY,
        scratch_shapes=[
            pltpu.VMEM((slots, rows, dim), f32),
            pltpu.SemaphoreType.DMA((slots,)),
            pltpu.SemaphoreType.DMA((slots,)),
        ],
        compiler_params=params(32),
        cost_estimate=cost(64_000_000, 2 * slots * rows * dim * 4),
        name="update",
    )(src, flat_states, recv1, recv2, xs, u1, u2)

    summed = jnp.sum(shared, axis=0).reshape(steps, slots, width // parts)
    is_live = place < live_count[0]
    layer_out = jnp.where(is_live[None, :, None], summed, 0.0).astype(jnp.bfloat16)
    back = lambda v: jnp.transpose(v, (1, 0, 2))
    return (
        back(layer_out),
        new_states.reshape(states.shape),
        back(ntq),
        back(ntk),
        back(ntv),
    )


def solution(mesh):
    by_head = P(None, "head")
    by_both = P("group", None, "head")
    return jax.shard_map(
        shards,
        mesh=mesh,
        in_specs=(
            P("group", None, None),
            *([by_head] * 9),
            P("head"),
            P("head"),
            P(),
            P("head", None),
            P("group", "head", None, None),
            by_both,
            by_both,
            by_both,
            P("group", None, None),
            P("group", None, None),
            P("group"),
        ),
        out_specs=(
            by_both,
            P("group", "head", None, None),
            by_both,
            by_both,
            by_both,
        ),
        check_vma=False,
    )
```

```python
import functools

import jax
import jax.numpy as jnp
from jax import lax
from jax.experimental import pallas as pl
from jax.experimental.pallas import tpu as pltpu
from jax.sharding import PartitionSpec as P

SMEM = pl.BlockSpec(memory_space=pltpu.SMEM)
VMEM = pl.BlockSpec(memory_space=pltpu.VMEM)
HBM = pl.BlockSpec(memory_space=pltpu.HBM)
LANES = 128


def params(mib):
    return pltpu.CompilerParams(vmem_limit_bytes=mib * 1024 * 1024)


def cost(flops, moved):
    return pl.CostEstimate(flops=flops, bytes_accessed=moved, transcendentals=0)


def in_hbm(v):
    return pltpu.with_memory_space_constraint(v, pltpu.HBM)


def wait_all(ref, sem):
    pltpu.make_async_copy(ref, ref, sem).wait()


def exact(a, b):
    return jnp.dot(a, b, precision=lax.Precision.HIGHEST, preferred_element_type=jnp.float32)


def exact_t(a, b):
    return lax.dot_general(
        a, b, (((0,), (0,)), ((), ())),
        precision=lax.Precision.HIGHEST, preferred_element_type=jnp.float32,
    )


def one_hot(slots, ids):
    hit = lax.broadcasted_iota(jnp.int32, (slots, ids.shape[1]), 0) == ids
    return hit.astype(jnp.float32)


def split(v):
    high = v.astype(jnp.bfloat16)
    return high, (v - high.astype(jnp.float32)).astype(jnp.bfloat16)


def pack(
    send, ids, states, tq, tk, tv, out1, out2,
    buf, bq, bk, bv, rows, in_sems, tail_sems, sems,
):
    groups, slots, size = send.shape[1], states.shape[0], states.shape[1]
    rest = out2.shape[1]
    upper = size - rest
    extra = rows.shape[1]
    tails = (tq, tk, tv)
    held = (bq, bk, bv)
    for n in range(3):
        pltpu.make_async_copy(tails[n], held[n], tail_sems.at[n]).start()
    for c in range(2):

        def start(g, carry, c=c):
            slot = jnp.maximum(send[c, g], 0)
            pltpu.make_async_copy(
                states.at[slot], buf.at[c * groups + g], in_sems.at[c * groups + g]
            ).start()
            return carry

        lax.fori_loop(0, groups, start, 0, unroll=8)
    for n in range(3):
        pltpu.make_async_copy(tails[n], held[n], tail_sems.at[n]).wait()
    for c in range(2):
        pick = one_hot(slots, ids[c : c + 1, :])
        at = c * (extra // 2)
        for j in range(tq.shape[0]):
            for ref in held:
                chosen = exact_t(pick, ref[j])
                for g in range(ref.shape[2] // LANES):
                    rows[:, at, :] = chosen[:, g * LANES : (g + 1) * LANES]
                    at += 1
    pltpu.make_async_copy(rows, out1.at[:, pl.ds(size + upper, extra)], sems.at[0]).start()

    def first(g, carry):
        pltpu.make_async_copy(states.at[0], buf.at[g], in_sems.at[g]).wait()
        pltpu.make_async_copy(buf.at[g], out1.at[g, pl.ds(0, size)], sems.at[0]).start()
        return carry

    lax.fori_loop(0, groups, first, 0, unroll=4)

    def second(g, carry):
        e = g + groups
        pltpu.make_async_copy(states.at[0], buf.at[e], in_sems.at[e]).wait()
        pltpu.make_async_copy(
            buf.at[e, pl.ds(0, upper)], out1.at[g, pl.ds(size, upper)], sems.at[0]
        ).start()
        pltpu.make_async_copy(buf.at[e, pl.ds(upper, rest)], out2.at[g], sems.at[1]).start()
        return carry

    lax.fori_loop(0, groups, second, 0, unroll=4)
    wait_all(out1, sems.at[0])
    wait_all(out2, sems.at[1])


def prepare(
    ids, live, rows, tq, tk, tv, pq, pk, pv, pg, rates, cq, ck, cv,
    xt, xs, v_ref, xt_late, xs_late, v_late, g_late, rates_late, live_late, ntq, ntk, ntv,
):
    taps, slots = tq.shape[0], tq.shape[1]
    puts = [one_hot(slots, ids[c : c + 1, :]) for c in range(2)]
    put = jnp.concatenate(puts, axis=1)
    arrived = jnp.sum(put, axis=1, keepdims=True) > 0.0
    late = puts[1]
    moved = {n: [] for n in range(3)}
    extra = rows.shape[1] // 2
    at = 0
    for j in range(taps):
        for n, ref in enumerate((tq, tk, tv)):
            groups = ref.shape[2] // LANES
            sent = [
                jnp.concatenate([rows[:, at + c + g, :] for g in range(groups)], axis=1)
                for c in (0, extra)
            ]
            at += groups
            sent = exact(put, jnp.concatenate(sent, axis=0))
            moved[n].append(jnp.where(arrived, sent, ref[j]))
    steps = pq.shape[0]
    is_live = lax.broadcasted_iota(jnp.int32, (slots, 1), 0) < live[0]

    def conv(before, proj, kernel, new):
        window = before + [proj[t] for t in range(steps)]
        outs = []
        for t in range(steps):
            mixed = window[t] * kernel[0:1, :]
            for j in range(1, taps + 1):
                mixed = mixed + window[t + j] * kernel[j : j + 1, :]
            outs.append(mixed * jax.nn.sigmoid(mixed))
        for j in range(taps):
            new[j] = jnp.where(is_live, window[steps + j], window[j])
        return outs

    def unit(v, scale):
        parts = []
        for h in range(v.shape[1] // LANES):
            part = v[:, h * LANES : (h + 1) * LANES]
            total = jnp.sum(part * part, axis=1, keepdims=True)
            parts.append(part * (lax.rsqrt(total + 1e-06) * scale))
        return jnp.concatenate(parts, axis=1)

    queries = [unit(v, LANES**-0.5) for v in conv(moved[0], pq, cq, ntq)]
    keys = [unit(v, 1.0) for v in conv(moved[1], pk, ck, ntk)]
    for n, v in enumerate(keys + queries):
        xt[n] = v
        xs[:, n, :] = v
        v = exact_t(late, v)
        xt_late[n] = v
        xs_late[:, n, :] = v
    for t, v in enumerate(conv(moved[2], pv, cv, ntv)):
        v_ref[t] = v
        v_late[t] = exact_t(late, v)
    for t in range(steps):
        g_late[t] = exact_t(late, pg[t])
        rates_late[t] = exact_t(late, rates[t])
    live_late[...] = exact_t(
        late, jnp.broadcast_to(is_live.astype(jnp.float32), (slots, LANES))
    )


def solve(halves, is_live, xt, v_ref, gate, rates, gain, normed, u_ref, pr):
    dim = LANES
    steps = v_ref.shape[0]
    slots = v_ref.shape[1]
    heads = rates.shape[2] // 2
    inner = lambda a, b: jnp.sum(a * b, axis=1, keepdims=True)
    for n, half in enumerate(halves):
        key_lanes = pl.ds(half * dim, dim)
        keys = [xt[t, :, key_lanes] for t in range(steps)]
        queries = [xt[steps + t, :, key_lanes] for t in range(steps)]
        kk = {(s, t): inner(keys[s], keys[t]) for t in range(steps) for s in range(t)}
        kq = {(s, t): inner(keys[s], queries[t]) for t in range(steps) for s in range(t + 1)}
        for h in range(2):
            head = 2 * half + h
            lanes = pl.ds((2 * n + h) * dim, dim)
            wide = pl.ds(head * dim, dim)
            fall = [rates[t, :, head : head + 1] for t in range(steps)]
            rate = [rates[t, :, heads + head : heads + head + 1] for t in range(steps)]
            ratio = {}
            for s in range(steps):
                for t in range(s + 1, steps):
                    ratio[s, t] = fall[t] if t == s + 1 else ratio[s, t - 1] * fall[t]
            total = [fall[0]]
            for t in range(1, steps):
                total.append(total[-1] * fall[t])
            us = []
            for t in range(steps):
                gap = v_ref[t, :, wide] - total[t] * pr[:, t, lanes]
                for s in range(t):
                    gap = gap - (ratio[s, t] * kk[s, t]) * us[s]
                us.append(gap * rate[t])
                out = total[t] * pr[:, steps + t, lanes]
                for s in range(t + 1):
                    weight = kq[s, t] if s == t else ratio[s, t] * kq[s, t]
                    out = out + weight * us[s]
                mean = jnp.mean(out * out, axis=1, keepdims=True)
                z = gate[t, :, wide]
                out = out * lax.rsqrt(mean + 1e-06) * gain[...] * (z * jax.nn.sigmoid(z))
                normed[t, :, lanes] = out.astype(normed.dtype)
            for s in range(steps):
                last = us[s] if s == steps - 1 else ratio[s, steps - 1] * us[s]
                u_ref[:, s, lanes] = jnp.where(is_live, last, 0.0)
            u_ref[:, steps, lanes] = jnp.broadcast_to(
                jnp.where(is_live, total[-1], 1.0), (slots, dim)
            )


def products(halves, xs, buf, pr, wait):
    dim = LANES

    def one(r, carry):
        wait(r)
        for n, half in enumerate(halves):
            state = jnp.concatenate(
                [buf[r, pl.ds((2 * n + h) * dim, dim), :] for h in range(2)], axis=1
            )
            high, low = split(state)
            both = jnp.concatenate(split(xs[r, :, pl.ds(half * dim, dim)]), axis=0)
            a = jnp.dot(both, high, preferred_element_type=jnp.float32)
            b = jnp.dot(both, low, preferred_element_type=jnp.float32)
            a = a + b
            rows = both.shape[0] // 2
            pr[r, :, pl.ds(2 * n * dim, 2 * dim)] = a[0:rows] + a[rows:]
        return carry

    lax.fori_loop(0, buf.shape[0], one, 0, unroll=4)


def read_early(
    src, live, states, recv1, xs, xt, v_ref, gate, rates, gain, normed, u_ref, buf, pr, sems
):
    slots, size = states.shape[0], states.shape[1]
    halves = tuple(range(size // (2 * LANES)))

    def start(r, carry):
        @pl.when(src[r] >= 0)
        def _():
            pltpu.make_async_copy(
                recv1.at[src[r], pl.ds(0, size)], buf.at[r], sems.at[r]
            ).start()

        @pl.when(src[r] < 0)
        def _():
            pltpu.make_async_copy(states.at[r], buf.at[r], sems.at[r]).start()

        return carry

    lax.fori_loop(0, slots, start, 0)
    wait = lambda r: pltpu.make_async_copy(states.at[0], buf.at[r], sems.at[r]).wait()
    products(halves, xs, buf, pr, wait)
    is_live = lax.broadcasted_iota(jnp.int32, (slots, 1), 0) < live[0]
    solve(halves, is_live, xt, v_ref, gate, rates, gain, normed, u_ref, pr)


def read_late(
    half, offset, recv, xs, xt, v_ref, gate, rates, live, gain, normed, u_ref, buf, pr, sems
):
    count, size = buf.shape[0], buf.shape[1]

    def copy(i):
        return pltpu.make_async_copy(
            recv.at[i, pl.ds(offset, size)], buf.at[i], sems.at[i]
        )

    def start(i, carry):
        copy(i).start()
        return carry

    lax.fori_loop(0, count, start, 0, unroll=8)
    products((half,), xs, buf, pr, lambda i: copy(i).wait())
    is_live = live[:, 0:1] > 0.5
    solve((half,), is_live, xt, v_ref, gate, rates, gain, normed, u_ref, pr)


def renew(xs, us, buf, r):
    dim = LANES
    steps = xs.shape[1] // 2
    wide = lambda v: v.astype(jnp.float32)
    for half, (u, at) in enumerate(us):
        k_high, k_low = split(xs[r, 0:steps, pl.ds(half * dim, dim)])
        rows = u[r, :, pl.ds(at, 2 * dim)]
        u_high, u_low = split(rows[0:steps])
        left = jnp.concatenate([wide(k_high), wide(k_high), wide(k_low), wide(k_low)], axis=0)
        right = jnp.concatenate([wide(u_high), wide(u_low), wide(u_high), wide(u_low)], axis=0)
        change = jnp.dot(
            left.T.astype(jnp.bfloat16),
            right.astype(jnp.bfloat16),
            preferred_element_type=jnp.float32,
        )
        for h in range(2):
            place = pl.ds((2 * half + h) * dim, dim)
            lanes = slice(h * dim, (h + 1) * dim)
            buf[r, place, :] = buf[r, place, :] * rows[steps : steps + 1, lanes] + change[:, lanes]


def update_early(src, states, recv1, xs, u, out, buf, in_sems, out_sems):
    slots, size = states.shape[0], states.shape[1]
    us = [(u, half * 2 * LANES) for half in range(size // (2 * LANES))]

    def start(r, carry):
        @pl.when(src[r] >= 0)
        def _():
            pltpu.make_async_copy(
                recv1.at[src[r], pl.ds(0, size)], buf.at[r], in_sems.at[r]
            ).start()

        @pl.when(src[r] == -1)
        def _():
            pltpu.make_async_copy(states.at[r], buf.at[r], in_sems.at[r]).start()

        return carry

    lax.fori_loop(0, slots, start, 0)

    def one(r, carry):
        @pl.when(src[r] >= -1)
        def _():
            pltpu.make_async_copy(states.at[0], buf.at[r], in_sems.at[r]).wait()
            renew(xs, us, buf, r)
            pltpu.make_async_copy(buf.at[r], out.at[r], out_sems.at[r]).start()

        return carry

    lax.fori_loop(0, slots, one, 0)

    def finish(r, carry):
        @pl.when(src[r] >= -1)
        def _():
            pltpu.make_async_copy(buf.at[r], out.at[r], out_sems.at[r]).wait()

        return carry

    lax.fori_loop(0, slots, finish, 0)


def update_late(ids, recv1, recv2, xs, u1, u2, before, out, buf, in_sems, out_sems):
    count, size = buf.shape[0], buf.shape[1]
    rest = recv2.shape[1]
    upper = size - rest

    def start(i, carry):
        pltpu.make_async_copy(
            recv1.at[i, pl.ds(size, upper)], buf.at[i, pl.ds(0, upper)], in_sems.at[0, i]
        ).start()
        pltpu.make_async_copy(
            recv2.at[i], buf.at[i, pl.ds(upper, rest)], in_sems.at[1, i]
        ).start()
        return carry

    lax.fori_loop(0, count, start, 0, unroll=4)

    def one(i, carry):
        pltpu.make_async_copy(
            recv1.at[i, pl.ds(size, upper)], buf.at[i, pl.ds(0, upper)], in_sems.at[0, i]
        ).wait()
        pltpu.make_async_copy(
            recv2.at[i], buf.at[i, pl.ds(upper, rest)], in_sems.at[1, i]
        ).wait()
        renew(xs, ((u1, 0), (u2, 0)), buf, i)

        @pl.when(ids[1, i] >= 0)
        def _():
            pltpu.make_async_copy(buf.at[i], out.at[ids[1, i]], out_sems.at[i]).start()

        return carry

    lax.fori_loop(0, count, one, 0, unroll=2)

    def finish(i, carry):
        @pl.when(ids[1, i] >= 0)
        def _():
            pltpu.make_async_copy(buf.at[i], out.at[0], out_sems.at[i]).wait()

        return carry

    lax.fori_loop(0, count, finish, 0)


def finish_rows(ids, live, early, shared, out):
    steps, slots = early.shape[0], early.shape[1]
    put = one_hot(slots, ids[1:2, :])
    arrived = jnp.sum(put, axis=1, keepdims=True) > 0.0
    is_live = lax.broadcasted_iota(jnp.int32, (slots, 1), 0) < live[0]
    for t in range(steps):
        total = shared[0, t]
        for p in range(1, shared.shape[0]):
            total = total + shared[p, t]
        value = jnp.where(arrived, exact(put, total), early[t])
        out[t] = jnp.where(is_live, value, 0.0).astype(out.dtype)


def shards(
    hidden_in, w_query, w_key, w_value, w_gate_z, w_write, w_decay,
    conv_query, conv_key, conv_value, decay_rate, dt_bias, norm_gain, w_out,
    states, tail_query, tail_key, tail_value, send_slot, recv_slot, live_count,
):
    slots, steps, width = hidden_in.shape
    heads, dim = states.shape[1], states.shape[2]
    f32 = jnp.float32
    shape = jax.ShapeDtypeStruct
    size = heads * dim
    half = size // 2
    old = in_hbm(states.reshape(slots, size, dim))
    step_major = lambda v: jnp.transpose(v, (1, 0, 2))
    tails = [step_major(t) for t in (tail_query, tail_key, tail_value)]
    taps = tails[0].shape[0]
    extra = 2 * taps * sum(t.shape[2] for t in tails) // LANES
    send = jnp.transpose(send_slot[0], (1, 0))
    groups = send.shape[1]
    upper, rest = half, half

    out1, out2 = pl.pallas_call(
        pack,
        out_shape=[
            pltpu.HBM((groups, size + upper + extra, LANES), f32),
            pltpu.HBM((groups, rest, LANES), f32),
        ],
        in_specs=[SMEM, VMEM] + [HBM] * 4,
        out_specs=[HBM, HBM],
        scratch_shapes=[
            pltpu.VMEM((2 * groups, size, LANES), f32),
            *[pltpu.VMEM(t.shape, f32) for t in tails],
            pltpu.VMEM((groups, extra, LANES), f32),
            pltpu.SemaphoreType.DMA((2 * groups,)),
            pltpu.SemaphoreType.DMA((3,)),
            pltpu.SemaphoreType.DMA((2,)),
        ],
        compiler_params=params(32),
        cost_estimate=cost(0, 4 * groups * size * LANES * 4),
        name="pack",
    )(send, send, old, *[in_hbm(t) for t in tails])
    recv1 = lax.all_to_all(out1, "group", split_axis=0, concat_axis=0, tiled=True)

    recv1, out2, hidden_in, recv_slot, live_count, conv_query, conv_key, conv_value = (
        lax.optimization_barrier(
            (recv1, out2, hidden_in, recv_slot, live_count, conv_query, conv_key, conv_value)
        )
    )
    recv2 = lax.all_to_all(out2, "group", split_axis=0, concat_axis=0, tiled=True)

    recv = jnp.transpose(recv_slot[0], (1, 0))
    place = jnp.arange(slots, dtype=jnp.int32)
    order = jnp.arange(groups, dtype=jnp.int32)
    codes = jnp.concatenate([order, jnp.full((groups,), -2, jnp.int32)])
    hits = recv.reshape(-1)[None, :] == place[:, None]
    src = jnp.sum(jnp.where(hits, codes[None, :] + 1, 0), axis=1) - 1
    flat_hidden = step_major(hidden_in).reshape(steps * slots, width)

    def project(weight):
        product = jnp.dot(flat_hidden, weight, preferred_element_type=f32)
        return product.reshape(steps, slots, weight.shape[1])

    pq, pk, pv, pg = (project(w) for w in (w_query, w_key, w_value, w_gate_z))
    write = jax.nn.sigmoid(project(w_write))
    decay = jnp.exp(-decay_rate * jax.nn.softplus(project(w_decay) + dt_bias))
    rates = jnp.concatenate([decay, write], axis=2)

    small = recv1[:, size + upper :, :]
    kernels = [c.astype(f32) for c in (conv_query, conv_key, conv_value)]
    key_width, value_width = pq.shape[2], pv.shape[2]
    xt, xs, values, xt_late, xs_late, v_late, g_late, rates_late, live_late, ntq, ntk, ntv = (
        pl.pallas_call(
            prepare,
            out_shape=[
                shape((2 * steps, slots, key_width), f32),
                shape((slots, 2 * steps, key_width), f32),
                shape((steps, slots, value_width), f32),
                shape((2 * steps, groups, key_width), f32),
                shape((groups, 2 * steps, key_width), f32),
                shape((steps, groups, value_width), f32),
                shape((steps, groups, value_width), f32),
                shape((steps, groups, 2 * heads), f32),
                shape((groups, LANES), f32),
                *[shape(t.shape, f32) for t in tails],
            ],
            in_specs=[VMEM, SMEM] + [VMEM] * 12,
            out_specs=[VMEM] * 12,
            compiler_params=params(32),
            cost_estimate=cost(2_000_000, 4_000_000),
            name="prepare",
        )(recv, live_count, small, *tails, pq, pk, pv, pg, rates, *kernels)
    )
    gain = norm_gain.reshape(1, dim)

    normed, u = pl.pallas_call(
        read_early,
        out_shape=[
            shape((steps, slots, size), jnp.bfloat16),
            shape((slots, 2 * steps, size), f32),
        ],
        in_specs=[SMEM, SMEM, HBM, HBM] + [VMEM] * 6,
        out_specs=[VMEM] * 2,
        scratch_shapes=[
            pltpu.VMEM((slots, size, dim), f32),
            pltpu.VMEM((slots, 2 * steps, size), f32),
            pltpu.SemaphoreType.DMA((slots,)),
        ],
        compiler_params=params(32),
        cost_estimate=cost(128_000_000, 12_000_000),
        name="read_early",
    )(src, live_count, old, in_hbm(recv1), xs, xt, values, pg, rates, gain)
    partial = jnp.dot(
        normed.reshape(steps * slots, size), w_out, preferred_element_type=f32
    )
    early = lax.psum_scatter(partial, "head", scatter_dimension=1, tiled=True)

    new_states = pl.pallas_call(
        update_early,
        out_shape=pltpu.HBM((slots, size, dim), f32),
        in_specs=[SMEM, HBM, HBM, VMEM, VMEM],
        out_specs=HBM,
        scratch_shapes=[
            pltpu.VMEM((slots, size, dim), f32),
            pltpu.SemaphoreType.DMA((slots,)),
            pltpu.SemaphoreType.DMA((slots,)),
        ],
        compiler_params=params(32),
        cost_estimate=cost(64_000_000, 2 * slots * size * dim * 4),
        name="update_early",
    )(src, old, in_hbm(recv1), xs, u)

    def read(index, offset, arrived):
        return pl.pallas_call(
            functools.partial(read_late, index, offset),
            out_shape=[
                shape((steps, groups, half), jnp.bfloat16),
                shape((groups, 2 * steps, half), f32),
            ],
            in_specs=[HBM] + [VMEM] * 7,
            out_specs=[VMEM] * 2,
            scratch_shapes=[
                pltpu.VMEM((groups, half, dim), f32),
                pltpu.VMEM((groups, 2 * steps, half), f32),
                pltpu.SemaphoreType.DMA((groups,)),
            ],
            compiler_params=params(32),
            cost_estimate=cost(32_000_000, 3_000_000),
            name="read_late",
        )(in_hbm(arrived), xs_late, xt_late, v_late, g_late, rates_late, live_late, gain)

    normed1, u1 = read(0, size, recv1)
    normed2, u2 = read(1, 0, recv2)
    parts = lax.axis_size("head")

    def out_part(rows, weight):
        return jnp.dot(
            rows.reshape(steps * groups, half), weight, preferred_element_type=f32
        )

    late = out_part(normed1, w_out[:half]) + out_part(normed2, w_out[half:])
    pieces = jnp.transpose(
        late.reshape(steps * groups, parts, width // parts), (1, 0, 2)
    )
    shared = lax.all_to_all(pieces, "head", split_axis=0, concat_axis=0, tiled=True)

    new_states = pl.pallas_call(
        update_late,
        out_shape=pltpu.HBM((slots, size, dim), f32),
        in_specs=[SMEM, HBM, HBM] + [VMEM] * 3 + [HBM],
        out_specs=HBM,
        scratch_shapes=[
            pltpu.VMEM((groups, size, dim), f32),
            pltpu.SemaphoreType.DMA((2, groups)),
            pltpu.SemaphoreType.DMA((groups,)),
        ],
        input_output_aliases={6: 0},
        compiler_params=params(32),
        cost_estimate=cost(64_000_000, 2 * groups * size * dim * 4),
        name="update_late",
    )(recv, in_hbm(recv1), in_hbm(recv2), xs_late, u1, u2, new_states)

    layer_out = pl.pallas_call(
        finish_rows,
        out_shape=shape((steps, slots, width // parts), jnp.bfloat16),
        in_specs=[VMEM, SMEM, VMEM, VMEM],
        out_specs=VMEM,
        compiler_params=params(16),
        cost_estimate=cost(1_000_000, 1_000_000),
        name="finish_rows",
    )(
        recv, live_count, early.reshape(steps, slots, width // parts),
        shared.reshape(parts, steps, groups, width // parts),
    )
    return (
        step_major(layer_out),
        new_states.reshape(states.shape),
        step_major(ntq),
        step_major(ntk),
        step_major(ntv),
    )


def solution(mesh):
    by_head = P(None, "head")
    by_both = P("group", None, "head")
    return jax.shard_map(
        shards,
        mesh=mesh,
        in_specs=(
            P("group", None, None),
            *([by_head] * 9),
            P("head"),
            P("head"),
            P(),
            P("head", None),
            P("group", "head", None, None),
            by_both,
            by_both,
            by_both,
            P("group", None, None),
            P("group", None, None),
            P("group"),
        ),
        out_specs=(
            by_both,
            P("group", "head", None, None),
            by_both,
            by_both,
            by_both,
        ),
        check_vma=False,
    )
```

```python
import functools

import jax
import jax.numpy as jnp
from jax import lax
from jax.experimental import pallas as pl
from jax.experimental.pallas import tpu as pltpu
from jax.sharding import PartitionSpec as P

SMEM = pl.BlockSpec(memory_space=pltpu.SMEM)
VMEM = pl.BlockSpec(memory_space=pltpu.VMEM)
HBM = pl.BlockSpec(memory_space=pltpu.HBM)
LANES = 128


def params(mib):
    return pltpu.CompilerParams(vmem_limit_bytes=mib * 1024 * 1024)


def cost(flops, moved):
    return pl.CostEstimate(flops=flops, bytes_accessed=moved, transcendentals=0)


def in_hbm(v):
    return pltpu.with_memory_space_constraint(v, pltpu.HBM)


def wait_all(ref, sem):
    pltpu.make_async_copy(ref, ref, sem).wait()


def exact(a, b):
    return jnp.dot(a, b, precision=lax.Precision.HIGHEST, preferred_element_type=jnp.float32)


def exact_t(a, b):
    return lax.dot_general(
        a, b, (((0,), (0,)), ((), ())),
        precision=lax.Precision.HIGHEST, preferred_element_type=jnp.float32,
    )


def one_hot(slots, ids):
    hit = lax.broadcasted_iota(jnp.int32, (slots, ids.shape[1]), 0) == ids
    return hit.astype(jnp.float32)


def split(v):
    high = v.astype(jnp.bfloat16)
    return high, (v - high.astype(jnp.float32)).astype(jnp.bfloat16)


def pack(
    send, ids, states, tq, tk, tv, out1, out2,
    buf, bq, bk, bv, rows, in_sems, tail_sems, sems,
):
    groups, slots, size = send.shape[1], states.shape[0], states.shape[1]
    rest = out2.shape[1]
    lower = size - rest
    extra = rows.shape[1]
    tails = (tq, tk, tv)
    held = (bq, bk, bv)
    for n in range(3):
        pltpu.make_async_copy(tails[n], held[n], tail_sems.at[n]).start()
    for c in range(2):

        def start(g, carry, c=c):
            slot = jnp.maximum(send[c, g], 0)
            pltpu.make_async_copy(
                states.at[slot], buf.at[c * groups + g], in_sems.at[c * groups + g]
            ).start()
            return carry

        lax.fori_loop(0, groups, start, 0, unroll=8)
    for n in range(3):
        pltpu.make_async_copy(tails[n], held[n], tail_sems.at[n]).wait()
    for c in range(2):
        pick = one_hot(slots, ids[c : c + 1, :])
        at = c * (extra // 2)
        for j in range(tq.shape[0]):
            for ref in held:
                chosen = exact_t(pick, ref[j])
                for g in range(ref.shape[2] // LANES):
                    rows[:, at, :] = chosen[:, g * LANES : (g + 1) * LANES]
                    at += 1
    pltpu.make_async_copy(rows, out1.at[:, pl.ds(size + lower, extra)], sems.at[0]).start()

    def first(g, carry):
        pltpu.make_async_copy(states.at[0], buf.at[g], in_sems.at[g]).wait()
        pltpu.make_async_copy(buf.at[g], out1.at[g, pl.ds(0, size)], sems.at[0]).start()
        return carry

    lax.fori_loop(0, groups, first, 0, unroll=4)

    def second(g, carry):
        e = g + groups
        pltpu.make_async_copy(states.at[0], buf.at[e], in_sems.at[e]).wait()
        pltpu.make_async_copy(
            buf.at[e, pl.ds(0, lower)], out1.at[g, pl.ds(size, lower)], sems.at[0]
        ).start()
        pltpu.make_async_copy(buf.at[e, pl.ds(lower, rest)], out2.at[g], sems.at[1]).start()
        return carry

    lax.fori_loop(0, groups, second, 0, unroll=4)
    wait_all(out1, sems.at[0])
    wait_all(out2, sems.at[1])


def prepare(
    ids, live, recv, tq, tk, tv, pq, pk, pv, pg, pw, pd, cq, ck, cv, pace, bias,
    xt, xs, v_ref, rates, xt_late, xs_late, v_late, g_late, rates_late, live_late,
    ntq, ntk, ntv, bq, bk, bv, rows, sems,
):
    held = (bq, bk, bv)
    copies = [
        pltpu.make_async_copy(ref, dst, sems.at[n])
        for n, (ref, dst) in enumerate(zip((tq, tk, tv), held))
    ]
    extra = rows.shape[1]
    copies.append(
        pltpu.make_async_copy(recv.at[:, pl.ds(recv.shape[1] - extra, extra)], rows, sems.at[3])
    )
    for copy in copies:
        copy.start()
    taps, slots = tq.shape[0], tq.shape[1]
    puts = [one_hot(slots, ids[c : c + 1, :]) for c in range(2)]
    put = jnp.concatenate(puts, axis=1)
    arrived = jnp.sum(put, axis=1, keepdims=True) > 0.0
    late = puts[1]
    steps = pq.shape[0]
    is_live = lax.broadcasted_iota(jnp.int32, (slots, 1), 0) < live[0]
    heads = pw.shape[2]
    for t in range(steps):
        x = pd[t] + bias[...]
        soft = jnp.maximum(x, 0.0) + jnp.log1p(jnp.exp(-jnp.abs(x)))
        rates[t, :, 0:heads] = jnp.exp(-pace[...] * soft)
        rates[t, :, heads : 2 * heads] = jax.nn.sigmoid(pw[t])
    for t in range(steps):
        g_late[t] = exact_t(late, pg[t])
        rates_late[t] = exact_t(late, rates[t])
    live_late[...] = exact_t(
        late, jnp.broadcast_to(is_live.astype(jnp.float32), (slots, LANES))
    )
    for copy in copies:
        copy.wait()
    moved = {n: [] for n in range(3)}
    at = 0
    for j in range(taps):
        for n, ref in enumerate(held):
            groups = ref.shape[2] // LANES
            sent = [
                jnp.concatenate([rows[:, at + c + g, :] for g in range(groups)], axis=1)
                for c in (0, extra // 2)
            ]
            at += groups
            sent = exact(put, jnp.concatenate(sent, axis=0))
            moved[n].append(jnp.where(arrived, sent, ref[j]))

    def conv(before, proj, kernel, new):
        kernel = kernel[...].astype(jnp.float32)
        window = before + [proj[t] for t in range(steps)]
        outs = []
        for t in range(steps):
            mixed = window[t] * kernel[0:1, :]
            for j in range(1, taps + 1):
                mixed = mixed + window[t + j] * kernel[j : j + 1, :]
            outs.append(mixed * jax.nn.sigmoid(mixed))
        for j in range(taps):
            new[j] = jnp.where(is_live, window[steps + j], window[j])
        return outs

    def unit(v, scale):
        parts = []
        for h in range(v.shape[1] // LANES):
            part = v[:, h * LANES : (h + 1) * LANES]
            total = jnp.sum(part * part, axis=1, keepdims=True)
            parts.append(part * (lax.rsqrt(total + 1e-06) * scale))
        return jnp.concatenate(parts, axis=1)

    queries = [unit(v, LANES**-0.5) for v in conv(moved[0], pq, cq, ntq)]
    keys = [unit(v, 1.0) for v in conv(moved[1], pk, ck, ntk)]
    for n, v in enumerate(keys + queries):
        xt[n] = v
        xs[:, n, :] = v
        v = exact_t(late, v)
        xt_late[n] = v
        xs_late[:, n, :] = v
    for t, v in enumerate(conv(moved[2], pv, cv, ntv)):
        v_ref[t] = v
        v_late[t] = exact_t(late, v)


def solve(halves, is_live, xt, v_ref, gate, rates, gain, normed, u_ref, pr):
    dim = LANES
    steps = v_ref.shape[0]
    slots = v_ref.shape[1]
    heads = rates.shape[2] // 2
    inner = lambda a, b: jnp.sum(a * b, axis=1, keepdims=True)
    for n, half in enumerate(halves):
        key_lanes = pl.ds(half * dim, dim)
        keys = [xt[t, :, key_lanes] for t in range(steps)]
        queries = [xt[steps + t, :, key_lanes] for t in range(steps)]
        kk = {(s, t): inner(keys[s], keys[t]) for t in range(steps) for s in range(t)}
        kq = {(s, t): inner(keys[s], queries[t]) for t in range(steps) for s in range(t + 1)}
        for h in range(2):
            head = 2 * half + h
            lanes = pl.ds((2 * n + h) * dim, dim)
            wide = pl.ds(head * dim, dim)
            fall = [rates[t, :, head : head + 1] for t in range(steps)]
            rate = [rates[t, :, heads + head : heads + head + 1] for t in range(steps)]
            ratio = {}
            for s in range(steps):
                for t in range(s + 1, steps):
                    ratio[s, t] = fall[t] if t == s + 1 else ratio[s, t - 1] * fall[t]
            total = [fall[0]]
            for t in range(1, steps):
                total.append(total[-1] * fall[t])
            us = []
            for t in range(steps):
                gap = v_ref[t, :, wide] - total[t] * pr[:, t, lanes]
                for s in range(t):
                    gap = gap - (ratio[s, t] * kk[s, t]) * us[s]
                us.append(gap * rate[t])
                out = total[t] * pr[:, steps + t, lanes]
                for s in range(t + 1):
                    weight = kq[s, t] if s == t else ratio[s, t] * kq[s, t]
                    out = out + weight * us[s]
                mean = jnp.mean(out * out, axis=1, keepdims=True)
                z = gate[t, :, wide]
                out = out * lax.rsqrt(mean + 1e-06) * gain[...] * (z * jax.nn.sigmoid(z))
                normed[t, :, lanes] = out.astype(normed.dtype)
            for s in range(steps):
                last = us[s] if s == steps - 1 else ratio[s, steps - 1] * us[s]
                u_ref[:, s, lanes] = jnp.where(is_live, last, 0.0)
            u_ref[:, steps, lanes] = jnp.broadcast_to(
                jnp.where(is_live, total[-1], 1.0), (slots, dim)
            )


def products(halves, xs, buf, pr, wait):
    dim = LANES
    batch = 8 // len(halves)

    def some(k, carry):
        for i in range(batch):
            wait(k * batch + i)
        for i in range(batch):
            r = k * batch + i
            for n, half in enumerate(halves):
                state = jnp.concatenate(
                    [buf[r, pl.ds((2 * n + h) * dim, dim), :] for h in range(2)], axis=1
                )
                high, low = split(state)
                both = jnp.concatenate(split(xs[r, :, pl.ds(half * dim, dim)]), axis=0)
                a = jnp.dot(both, high, preferred_element_type=jnp.float32)
                a = a + jnp.dot(both, low, preferred_element_type=jnp.float32)
                rows = both.shape[0] // 2
                pr[r, :, pl.ds(2 * n * dim, 2 * dim)] = a[0:rows] + a[rows:]
        return carry

    lax.fori_loop(0, buf.shape[0] // batch, some, 0)


def sources(ids, src):
    groups = ids.shape[1]

    def clear(r, carry):
        src[r] = -1
        return carry

    lax.fori_loop(0, src.shape[0], clear, 0, unroll=8)
    for c in range(2):

        def put(g, carry, c=c):
            @pl.when(ids[c, g] >= 0)
            def _():
                src[ids[c, g]] = g if c == 0 else -2

            return carry

        lax.fori_loop(0, groups, put, 0, unroll=4)


def fetch(src, states, recv, buf, sems):
    slots, size = states.shape[0], states.shape[1]

    def start(r, carry):
        @pl.when(src[r] >= 0)
        def _():
            pltpu.make_async_copy(
                recv.at[src[r], pl.ds(0, size)], buf.at[r], sems.at[r]
            ).start()

        @pl.when(src[r] < 0)
        def _():
            pltpu.make_async_copy(states.at[r], buf.at[r], sems.at[r]).start()

        return carry

    lax.fori_loop(0, slots, start, 0)


def read_early(
    ids, live, states, recv, weight_ref, xs, xt, v_ref, gate, rates, gain,
    sent, kept, u_ref, src, buf, pr, normed, weight, sems, weight_sem,
):
    slots, size = buf.shape[0], buf.shape[1]
    halves = tuple(range(size // (2 * LANES)))
    sources(ids, src)
    fetch(src, states, recv, buf, sems)
    load = pltpu.make_async_copy(weight_ref, weight, weight_sem)
    load.start()
    wait = lambda r: pltpu.make_async_copy(states.at[0], buf.at[r], sems.at[r]).wait()
    products(halves, xs, buf, pr, wait)
    is_live = lax.broadcasted_iota(jnp.int32, (slots, 1), 0) < live[0]
    solve(halves, is_live, xt, v_ref, gate, rates, gain, normed, u_ref, pr)
    rows = jnp.concatenate([normed[t] for t in range(normed.shape[0])], axis=0)
    columns = sent.shape[2]
    core = lax.rem(lax.axis_index("head"), 2)
    load.wait()
    for j in range(sent.shape[0]):
        for out, c in ((sent, 1 - core), (kept, core)):
            at = pl.multiple_of((2 * j + c) * columns, columns)
            out[j] = jnp.dot(
                rows, weight[:, pl.ds(at, columns)], preferred_element_type=jnp.float32
            )


def read_late(
    half, base, recv, weight_ref, *refs
):
    ins, (out, u_ref, buf, pr, normed, weight, sems, weight_sem) = refs[:-8], refs[-8:]
    xs, xt, v_ref, gate, rates, live, gain = ins[:7]
    count, size = buf.shape[0], buf.shape[1]
    load = pltpu.make_async_copy(
        weight_ref.at[pl.ds(half * size, size)], weight, weight_sem
    )

    def copy(i):
        return pltpu.make_async_copy(recv.at[i, pl.ds(base, size)], buf.at[i], sems.at[i])

    def start(i, carry):
        copy(i).start()
        return carry

    lax.fori_loop(0, count, start, 0, unroll=8)
    load.start()
    products((half,), xs, buf, pr, lambda i: copy(i).wait())
    is_live = live[:, 0:1] > 0.5
    solve((half,), is_live, xt, v_ref, gate, rates, gain, normed, u_ref, pr)
    steps = normed.shape[0]
    rows = jnp.concatenate([normed[t] for t in range(steps)], axis=0)
    columns = out.shape[2]
    load.wait()
    for p in range(out.shape[0]):
        share = jnp.dot(
            rows, weight[:, pl.ds(p * columns, columns)], preferred_element_type=jnp.float32
        )
        out[p] = share if len(ins) == 7 else share + ins[7][p]


def renew(half, place, xs, u, buf, new, r):
    dim = LANES
    steps = xs.shape[1] // 2
    wide = lambda v: v.astype(jnp.float32)
    k_high, k_low = split(xs[r, 0:steps, pl.ds(half * dim, dim)])
    rows = u[r, :, pl.ds(2 * place * dim, 2 * dim)]
    u_high, u_low = split(rows[0:steps])
    left = jnp.concatenate([wide(k_high), wide(k_high), wide(k_low), wide(k_low)], axis=0)
    right = jnp.concatenate([wide(u_high), wide(u_low), wide(u_high), wide(u_low)], axis=0)
    change = jnp.dot(
        left.T.astype(jnp.bfloat16),
        right.astype(jnp.bfloat16),
        preferred_element_type=jnp.float32,
    )
    for h in range(2):
        at = pl.ds((2 * place + h) * dim, dim)
        lanes = slice(h * dim, (h + 1) * dim)
        new[r, at, :] = buf[r, at, :] * rows[steps : steps + 1, lanes] + change[:, lanes]


def update_early(ids, states, recv, xs, u, out, src, buf, new, in_sems, out_sems):
    slots, size = states.shape[0], states.shape[1]
    half = 2 * LANES
    batch = 4
    sources(ids, src)
    fetch(src, states, recv, buf, in_sems)

    def some(k, carry):
        for i in range(batch):
            r = k * batch + i
            pltpu.make_async_copy(states.at[0], buf.at[r], in_sems.at[r]).wait()
        for i in range(batch):
            for n in range(size // half):
                renew(n, n, xs, u, buf, new, k * batch + i)
        for i in range(batch):
            r = k * batch + i

            @pl.when(src[r] >= -1)
            def _():
                pltpu.make_async_copy(new.at[r], out.at[r], out_sems.at[r]).start()

        return carry

    lax.fori_loop(0, slots // batch, some, 0)

    def finish(r, carry):
        @pl.when(src[r] >= -1)
        def _():
            pltpu.make_async_copy(new.at[r], out.at[r], out_sems.at[r]).wait()

        return carry

    lax.fori_loop(0, slots, finish, 0)


def update_late(half, base, ids, recv, xs, u, before, out, buf, new, in_sems, out_sems):
    count, size = buf.shape[0], buf.shape[1]
    rows = pl.ds(half * size, size)
    batch = 8

    def copy(i):
        return pltpu.make_async_copy(recv.at[i, pl.ds(base, size)], buf.at[i], in_sems.at[i])

    def start(i, carry):
        copy(i).start()
        return carry

    lax.fori_loop(0, count, start, 0, unroll=8)

    def some(k, carry):
        for j in range(batch):
            copy(k * batch + j).wait()
        for j in range(batch):
            renew(half, 0, xs, u, buf, new, k * batch + j)
        for j in range(batch):
            i = k * batch + j

            @pl.when(ids[1, i] >= 0)
            def _():
                pltpu.make_async_copy(
                    new.at[i], out.at[ids[1, i], rows], out_sems.at[i]
                ).start()

        return carry

    lax.fori_loop(0, count // batch, some, 0)

    def finish(i, carry):
        @pl.when(ids[1, i] >= 0)
        def _():
            pltpu.make_async_copy(new.at[i], out.at[0, rows], out_sems.at[i]).wait()

        return carry

    lax.fori_loop(0, count, finish, 0)


def finish_rows(ids, live, mine, first, second, third, shared, out):
    steps, slots = mine.shape[0], mine.shape[1]
    put = one_hot(slots, ids[1:2, :])
    arrived = jnp.sum(put, axis=1, keepdims=True) > 0.0
    is_live = lax.broadcasted_iota(jnp.int32, (slots, 1), 0) < live[0]
    for t in range(steps):
        total = shared[0, t]
        for p in range(1, shared.shape[0]):
            total = total + shared[p, t]
        early = (mine[t] + first[t]) + (second[t] + third[t])
        value = jnp.where(arrived, exact(put, total), early)
        out[t] = jnp.where(is_live, value, 0.0).astype(out.dtype)


def early_sum(sent, kept):
    cores = 2
    parts = lax.axis_size("head")
    chips = parts // cores
    chip = lax.axis_index("head") // cores
    swap = [(i, i ^ 1) for i in range(parts)]
    summed = kept + lax.ppermute(sent, "head", swap)
    terms = [lax.dynamic_index_in_dim(summed, chip, 0, keepdims=False)]
    for k in range(1, chips):
        to = [(i, (i + k * cores) % parts) for i in range(parts)]
        part = lax.dynamic_index_in_dim(summed, (chip + k) % chips, 0, keepdims=False)
        terms.append(lax.ppermute(part, "head", to))
    return terms


def shards(
    hidden_in, w_query, w_key, w_value, w_gate_z, w_write, w_decay,
    conv_query, conv_key, conv_value, decay_rate, dt_bias, norm_gain, w_out,
    states, tail_query, tail_key, tail_value, send_slot, recv_slot, live_count,
):
    slots, steps, width = hidden_in.shape
    heads, dim = states.shape[1], states.shape[2]
    f32 = jnp.float32
    shape = jax.ShapeDtypeStruct
    size = heads * dim
    half = size // 2
    old = in_hbm(states.reshape(slots, size, dim))
    step_major = lambda v: jnp.transpose(v, (1, 0, 2))
    tails = [step_major(t) for t in (tail_query, tail_key, tail_value)]
    taps = tails[0].shape[0]
    extra = 2 * taps * sum(t.shape[2] for t in tails) // LANES
    extra += -extra % 64
    send = jnp.transpose(send_slot[0], (1, 0))
    groups = send.shape[1]

    out1, out2 = pl.pallas_call(
        pack,
        out_shape=[
            pltpu.HBM((groups, size + half + extra, LANES), f32),
            pltpu.HBM((groups, half, LANES), f32),
        ],
        in_specs=[SMEM, VMEM] + [HBM] * 4,
        out_specs=[HBM, HBM],
        scratch_shapes=[
            pltpu.VMEM((2 * groups, size, LANES), f32),
            *[pltpu.VMEM(t.shape, f32) for t in tails],
            pltpu.VMEM((groups, extra, LANES), f32),
            pltpu.SemaphoreType.DMA((2 * groups,)),
            pltpu.SemaphoreType.DMA((3,)),
            pltpu.SemaphoreType.DMA((2,)),
        ],
        compiler_params=params(16),
        cost_estimate=cost(0, 4 * groups * size * LANES * 4),
        name="pack",
    )(send, send, old, *[in_hbm(t) for t in tails])

    def exchange(v):
        return lax.all_to_all(v, "group", split_axis=0, concat_axis=0, tiled=True)

    tie = lax.optimization_barrier
    recv1 = lax.cond(live_count[0] >= 0, exchange, jnp.zeros_like, out1)
    recv1, out2 = tie((recv1, out2))
    recv2 = exchange(out2)

    recv = jnp.transpose(recv_slot[0], (1, 0))
    flat_hidden = step_major(hidden_in).reshape(steps * slots, width)

    def project(weight):
        product = jnp.dot(flat_hidden, weight, preferred_element_type=f32)
        return product.reshape(steps, slots, weight.shape[1])

    pq, pk, pv, pg = (project(w) for w in (w_query, w_key, w_value, w_gate_z))
    pw, pd = project(w_write), project(w_decay)
    key_width, value_width = pq.shape[2], pv.shape[2]
    (
        xt, xs, values, rates, xt_late, xs_late, v_late, g_late, rates_late, live_late,
        ntq, ntk, ntv,
    ) = pl.pallas_call(
        prepare,
        out_shape=[
            shape((2 * steps, slots, key_width), f32),
            shape((slots, 2 * steps, key_width), f32),
            shape((steps, slots, value_width), f32),
            shape((steps, slots, 2 * heads), f32),
            shape((2 * steps, groups, key_width), f32),
            shape((groups, 2 * steps, key_width), f32),
            shape((steps, groups, value_width), f32),
            shape((steps, groups, value_width), f32),
            shape((steps, groups, 2 * heads), f32),
            shape((groups, LANES), f32),
            *[shape(t.shape, f32) for t in tails],
        ],
        in_specs=[VMEM, SMEM] + [HBM] * 4 + [VMEM] * 11,
        out_specs=[VMEM] * 13,
        scratch_shapes=[
            *[pltpu.VMEM(t.shape, f32) for t in tails],
            pltpu.VMEM((groups, extra, LANES), f32),
            pltpu.SemaphoreType.DMA((4,)),
        ],
        compiler_params=params(16),
        cost_estimate=cost(2_000_000, 4_000_000),
        name="prepare",
    )(
        recv, live_count, in_hbm(recv1), *[in_hbm(t) for t in tails], pq, pk, pv, pg, pw, pd,
        conv_query, conv_key, conv_value,
        decay_rate.reshape(1, heads), dt_bias.reshape(1, heads),
    )
    gain = norm_gain.reshape(1, dim)

    parts = lax.axis_size("head")
    columns = width // parts
    weight = in_hbm(w_out)
    sent, kept, u = pl.pallas_call(
        read_early,
        out_shape=[
            shape((parts // 2, steps * slots, columns), f32),
            shape((parts // 2, steps * slots, columns), f32),
            shape((slots, 2 * steps, size), f32),
        ],
        in_specs=[SMEM, SMEM, HBM, HBM, HBM] + [VMEM] * 6,
        out_specs=[VMEM] * 3,
        scratch_shapes=[
            pltpu.SMEM((slots,), jnp.int32),
            pltpu.VMEM((slots, size, dim), f32),
            pltpu.VMEM((slots, 2 * steps, size), f32),
            pltpu.VMEM((steps, slots, size), jnp.bfloat16),
            pltpu.VMEM((size, width), jnp.bfloat16),
            pltpu.SemaphoreType.DMA((slots,)),
            pltpu.SemaphoreType.DMA,
        ],
        compiler_params=params(20),
        cost_estimate=cost(400_000_000, 14_000_000),
        name="read_early",
    )(recv, live_count, old, in_hbm(recv1), weight, xs, xt, values, pg, rates, gain)
    terms = early_sum(sent, kept)
    new_states = pl.pallas_call(
        update_early,
        out_shape=pltpu.HBM((slots, size, dim), f32),
        in_specs=[SMEM, HBM, HBM, VMEM, VMEM],
        out_specs=HBM,
        scratch_shapes=[
            pltpu.SMEM((slots,), jnp.int32),
            pltpu.VMEM((slots, size, dim), f32),
            pltpu.VMEM((slots, size, dim), f32),
            pltpu.SemaphoreType.DMA((slots,)),
            pltpu.SemaphoreType.DMA((slots,)),
        ],
        compiler_params=params(20),
        cost_estimate=cost(64_000_000, 2 * slots * size * dim * 4),
        name="update_early",
    )(recv, old, in_hbm(recv1), xs, u)

    late_args = (xs_late, xt_late, v_late, g_late, rates_late, live_late, gain)

    def read_second(index, base, arrived, *more):
        return pl.pallas_call(
            functools.partial(read_late, index, base),
            out_shape=[
                shape((parts, steps * groups, columns), f32),
                shape((groups, 2 * steps, half), f32),
            ],
            in_specs=[HBM, HBM] + [VMEM] * (len(late_args) + len(more)),
            out_specs=[VMEM] * 2,
            scratch_shapes=[
                pltpu.VMEM((groups, half, dim), f32),
                pltpu.VMEM((groups, 2 * steps, half), f32),
                pltpu.VMEM((steps, groups, half), jnp.bfloat16),
                pltpu.VMEM((half, width), jnp.bfloat16),
                pltpu.SemaphoreType.DMA((groups,)),
                pltpu.SemaphoreType.DMA,
            ],
            compiler_params=params(16),
            cost_estimate=cost(150_000_000, 5_000_000),
            name="read_late",
        )(in_hbm(arrived), weight, *late_args, *more)

    def update_second(index, base, arrived, u, before):
        return pl.pallas_call(
            functools.partial(update_late, index, base),
            out_shape=pltpu.HBM((slots, size, dim), f32),
            in_specs=[SMEM, HBM, VMEM, VMEM, HBM],
            out_specs=HBM,
            scratch_shapes=[
                pltpu.VMEM((groups, half, dim), f32),
                pltpu.VMEM((groups, half, dim), f32),
                pltpu.SemaphoreType.DMA((groups,)),
                pltpu.SemaphoreType.DMA((groups,)),
            ],
            input_output_aliases={4: 0},
            compiler_params=params(16),
            cost_estimate=cost(32_000_000, 2 * groups * half * dim * 4),
            name="update_late",
        )(recv, in_hbm(arrived), xs_late, u, before)

    pieces, u1 = read_second(0, size, recv1)
    recv2, pieces, terms[0] = tie((recv2, pieces, terms[0]))
    pieces, u2 = read_second(1, 0, recv2, pieces)
    shared = lax.all_to_all(pieces, "head", split_axis=0, concat_axis=0, tiled=True)
    new_states = update_second(0, size, recv1, u1, new_states)
    new_states = update_second(1, 0, recv2, u2, new_states)

    layer_out = pl.pallas_call(
        finish_rows,
        out_shape=shape((steps, slots, columns), jnp.bfloat16),
        in_specs=[VMEM, SMEM] + [VMEM] * 5,
        out_specs=VMEM,
        compiler_params=params(16),
        cost_estimate=cost(1_000_000, 2_000_000),
        name="finish_rows",
    )(
        recv, live_count, *[v.reshape(steps, slots, columns) for v in terms],
        shared.reshape(parts, steps, groups, columns),
    )
    return (
        step_major(layer_out),
        new_states.reshape(states.shape),
        step_major(ntq),
        step_major(ntk),
        step_major(ntv),
    )


def solution(mesh):
    by_head = P(None, "head")
    by_both = P("group", None, "head")
    return jax.shard_map(
        shards,
        mesh=mesh,
        in_specs=(
            P("group", None, None),
            *([by_head] * 9),
            P("head"),
            P("head"),
            P(),
            P("head", None),
            P("group", "head", None, None),
            by_both,
            by_both,
            by_both,
            P("group", None, None),
            P("group", None, None),
            P("group"),
        ),
        out_specs=(
            by_both,
            P("group", "head", None, None),
            by_both,
            by_both,
            by_both,
        ),
        check_vma=False,
    )
```

```python
import functools

import jax
import jax.numpy as jnp
from jax import lax
from jax.experimental import pallas as pl
from jax.experimental.pallas import tpu as pltpu
from jax.sharding import PartitionSpec as P

SMEM = pl.BlockSpec(memory_space=pltpu.SMEM)
VMEM = pl.BlockSpec(memory_space=pltpu.VMEM)
HBM = pl.BlockSpec(memory_space=pltpu.HBM)
ANY = pl.BlockSpec(memory_space=pl.ANY)
LANES = 128


def params(mib):
    return pltpu.CompilerParams(vmem_limit_bytes=mib * 1024 * 1024)


def cost(flops, moved):
    return pl.CostEstimate(flops=flops, bytes_accessed=moved, transcendentals=0)


def in_hbm(v):
    return pltpu.with_memory_space_constraint(v, pltpu.HBM)


def wait_all(ref, sem):
    pltpu.make_async_copy(ref, ref, sem).wait()


def load(refs, bufs, sems):
    copies = [
        pltpu.make_async_copy(ref, buf, sems.at[n]) for n, (ref, buf) in enumerate(zip(refs, bufs))
    ]
    for copy in copies:
        copy.start()
    return copies


def exact(a, b):
    return jnp.dot(a, b, precision=lax.Precision.HIGHEST, preferred_element_type=jnp.float32)


def exact_t(a, b):
    return lax.dot_general(
        a, b, (((0,), (0,)), ((), ())),
        precision=lax.Precision.HIGHEST, preferred_element_type=jnp.float32,
    )


def one_hot(slots, ids):
    hit = lax.broadcasted_iota(jnp.int32, (slots, ids.shape[1]), 0) == ids
    return hit.astype(jnp.float32)


def split(v):
    high = v.astype(jnp.bfloat16)
    return high, (v - high.astype(jnp.float32)).astype(jnp.bfloat16)


def pack(
    send, ids_ref, states, tq, tk, tv, out1, out2,
    buf, bq, bk, bv, ids, rows, in_sems, tail_sems, sems,
):
    groups, slots, size = send.shape[1], states.shape[0], states.shape[1]
    rest = out2.shape[1]
    lower = size - rest
    extra = rows.shape[1]
    held = (bq, bk, bv)
    tails = load((tq, tk, tv, ids_ref), (bq, bk, bv, ids), tail_sems)
    for c in range(2):

        def start(g, carry, c=c):
            slot = jnp.maximum(send[c, g], 0)
            pltpu.make_async_copy(
                states.at[slot], buf.at[c * groups + g], in_sems.at[c * groups + g]
            ).start()
            return carry

        lax.fori_loop(0, groups, start, 0, unroll=8)
    for copy in tails:
        copy.wait()
    for c in range(2):
        pick = one_hot(slots, ids[c : c + 1, :])
        at = c * (extra // 2)
        for j in range(tq.shape[0]):
            for ref in held:
                chosen = exact_t(pick, ref[j])
                for g in range(ref.shape[2] // LANES):
                    rows[:, at, :] = chosen[:, g * LANES : (g + 1) * LANES]
                    at += 1
    pltpu.make_async_copy(rows, out1.at[:, pl.ds(size + lower, extra)], sems.at[0]).start()

    def first(g, carry):
        pltpu.make_async_copy(states.at[0], buf.at[g], in_sems.at[g]).wait()
        pltpu.make_async_copy(buf.at[g], out1.at[g, pl.ds(0, size)], sems.at[0]).start()
        return carry

    lax.fori_loop(0, groups, first, 0, unroll=4)

    def second(g, carry):
        e = g + groups
        pltpu.make_async_copy(states.at[0], buf.at[e], in_sems.at[e]).wait()
        pltpu.make_async_copy(
            buf.at[e, pl.ds(0, lower)], out1.at[g, pl.ds(size, lower)], sems.at[0]
        ).start()
        pltpu.make_async_copy(buf.at[e, pl.ds(lower, rest)], out2.at[g], sems.at[1]).start()
        return carry

    lax.fori_loop(0, groups, second, 0, unroll=4)
    wait_all(out1, sems.at[0])
    wait_all(out2, sems.at[1])


def prepare(
    ids, live, recv, tq, tk, tv, pq, pk, pv, pg, pw, pd, cq, ck, cv, pace, bias,
    xt, xs, v_ref, rates, xt_late, xs_late, v_late, g_late, rates_late, live_late,
    ntq, ntk, ntv, bq, bk, bv, rows, gate, sems,
):
    held = (bq, bk, bv)
    copies = [
        pltpu.make_async_copy(ref, dst, sems.at[n])
        for n, (ref, dst) in enumerate(zip((tq, tk, tv), held))
    ]
    extra = rows.shape[1]
    copies.append(
        pltpu.make_async_copy(recv.at[:, pl.ds(recv.shape[1] - extra, extra)], rows, sems.at[3])
    )
    copies.append(pltpu.make_async_copy(pg, gate, sems.at[4]))
    for copy in copies:
        copy.start()
    taps, slots = tq.shape[0], tq.shape[1]
    puts = [one_hot(slots, ids[c : c + 1, :]) for c in range(2)]
    put = jnp.concatenate(puts, axis=1)
    arrived = jnp.sum(put, axis=1, keepdims=True) > 0.0
    late = puts[1]
    steps = pq.shape[0]
    is_live = lax.broadcasted_iota(jnp.int32, (slots, 1), 0) < live[0]
    heads = pw.shape[2]
    for t in range(steps):
        x = pd[t] + bias[...]
        soft = jnp.maximum(x, 0.0) + jnp.log1p(jnp.exp(-jnp.abs(x)))
        rates[t, :, 0:heads] = jnp.exp(-pace[...] * soft)
        rates[t, :, heads : 2 * heads] = jax.nn.sigmoid(pw[t])
        rates_late[t] = exact_t(late, rates[t])
    live_late[...] = exact_t(
        late, jnp.broadcast_to(is_live.astype(jnp.float32), (slots, LANES))
    )
    for copy in copies:
        copy.wait()
    for t in range(steps):
        g_late[t] = exact_t(late, gate[t])
    moved = {n: [] for n in range(3)}
    at = 0
    for j in range(taps):
        for n, ref in enumerate(held):
            groups = ref.shape[2] // LANES
            sent = [
                jnp.concatenate([rows[:, at + c + g, :] for g in range(groups)], axis=1)
                for c in (0, extra // 2)
            ]
            at += groups
            sent = exact(put, jnp.concatenate(sent, axis=0))
            moved[n].append(jnp.where(arrived, sent, ref[j]))

    def conv(before, proj, kernel, new):
        kernel = kernel[...].astype(jnp.float32)
        window = before + [proj[t] for t in range(steps)]
        outs = []
        for t in range(steps):
            mixed = window[t] * kernel[0:1, :]
            for j in range(1, taps + 1):
                mixed = mixed + window[t + j] * kernel[j : j + 1, :]
            outs.append(mixed * jax.nn.sigmoid(mixed))
        for j in range(taps):
            new[j] = jnp.where(is_live, window[steps + j], window[j])
        return outs

    def unit(v, scale):
        parts = []
        for h in range(v.shape[1] // LANES):
            part = v[:, h * LANES : (h + 1) * LANES]
            total = jnp.sum(part * part, axis=1, keepdims=True)
            parts.append(part * (lax.rsqrt(total + 1e-06) * scale))
        return jnp.concatenate(parts, axis=1)

    queries = [unit(v, LANES**-0.5) for v in conv(moved[0], pq, cq, ntq)]
    keys = [unit(v, 1.0) for v in conv(moved[1], pk, ck, ntk)]
    for n, v in enumerate(keys + queries):
        xt[n] = v
        xs[:, n, :] = v
        v = exact_t(late, v)
        xt_late[n] = v
        xs_late[:, n, :] = v
    for t, v in enumerate(conv(moved[2], pv, cv, ntv)):
        v_ref[t] = v
        v_late[t] = exact_t(late, v)


def solve(halves, is_live, xt, v_ref, gate, rates, gain, normed, u_ref, pr):
    dim = LANES
    steps = v_ref.shape[0]
    slots = v_ref.shape[1]
    heads = rates.shape[2] // 2
    inner = lambda a, b: jnp.sum(a * b, axis=1, keepdims=True)
    for n, half in enumerate(halves):
        key_lanes = pl.ds(half * dim, dim)
        keys = [xt[t, :, key_lanes] for t in range(steps)]
        queries = [xt[steps + t, :, key_lanes] for t in range(steps)]
        kk = {(s, t): inner(keys[s], keys[t]) for t in range(steps) for s in range(t)}
        kq = {(s, t): inner(keys[s], queries[t]) for t in range(steps) for s in range(t + 1)}
        for h in range(2):
            head = 2 * half + h
            lanes = pl.ds((2 * n + h) * dim, dim)
            wide = pl.ds(head * dim, dim)
            fall = [rates[t, :, head : head + 1] for t in range(steps)]
            rate = [rates[t, :, heads + head : heads + head + 1] for t in range(steps)]
            ratio = {}
            for s in range(steps):
                for t in range(s + 1, steps):
                    ratio[s, t] = fall[t] if t == s + 1 else ratio[s, t - 1] * fall[t]
            total = [fall[0]]
            for t in range(1, steps):
                total.append(total[-1] * fall[t])
            us = []
            for t in range(steps):
                gap = v_ref[t, :, wide] - total[t] * pr[:, t, lanes]
                for s in range(t):
                    gap = gap - (ratio[s, t] * kk[s, t]) * us[s]
                us.append(gap * rate[t])
                out = total[t] * pr[:, steps + t, lanes]
                for s in range(t + 1):
                    weight = kq[s, t] if s == t else ratio[s, t] * kq[s, t]
                    out = out + weight * us[s]
                mean = jnp.mean(out * out, axis=1, keepdims=True)
                z = gate[t, :, wide]
                out = out * lax.rsqrt(mean + 1e-06) * gain[...] * (z * jax.nn.sigmoid(z))
                normed[t, :, lanes] = out.astype(normed.dtype)
            for s in range(steps):
                last = us[s] if s == steps - 1 else ratio[s, steps - 1] * us[s]
                u_ref[:, s, lanes] = jnp.where(is_live, last, 0.0)
            u_ref[:, steps, lanes] = jnp.broadcast_to(
                jnp.where(is_live, total[-1], 1.0), (slots, dim)
            )


def products(halves, xs, buf, pr, wait):
    dim = LANES
    batch = 8 // len(halves)

    def some(k, carry):
        for i in range(batch):
            wait(k * batch + i)
        for i in range(batch):
            r = k * batch + i
            for n, half in enumerate(halves):
                state = jnp.concatenate(
                    [buf[r, pl.ds((2 * n + h) * dim, dim), :] for h in range(2)], axis=1
                )
                high, low = split(state)
                both = jnp.concatenate(split(xs[r, :, pl.ds(half * dim, dim)]), axis=0)
                a = jnp.dot(both, high, preferred_element_type=jnp.float32)
                a = a + jnp.dot(both, low, preferred_element_type=jnp.float32)
                rows = both.shape[0] // 2
                pr[r, :, pl.ds(2 * n * dim, 2 * dim)] = a[0:rows] + a[rows:]
        return carry

    lax.fori_loop(0, buf.shape[0] // batch, some, 0)


def sources(ids, src):
    groups = ids.shape[1]

    def clear(r, carry):
        src[r] = -1
        return carry

    lax.fori_loop(0, src.shape[0], clear, 0, unroll=8)
    for c in range(2):

        def put(g, carry, c=c):
            @pl.when(ids[c, g] >= 0)
            def _():
                src[ids[c, g]] = g if c == 0 else -2

            return carry

        lax.fori_loop(0, groups, put, 0, unroll=4)


def fetch(src, states, recv, buf, sems):
    slots, size = states.shape[0], states.shape[1]

    def start(r, carry):
        @pl.when(src[r] >= 0)
        def _():
            pltpu.make_async_copy(
                recv.at[src[r], pl.ds(0, size)], buf.at[r], sems.at[r]
            ).start()

        @pl.when(src[r] < 0)
        def _():
            pltpu.make_async_copy(states.at[r], buf.at[r], sems.at[r]).start()

        return carry

    lax.fori_loop(0, slots, start, 0)


def early_rows(
    ids, live, states, recv, weight_ref, s0, s1, s2, s3, s4, s5,
    sent, kept, new_states, h0, h1, h2, h3, h4, h5,
    src, buf, new, pr, u_ref, normed, weight, share,
    small_sems, sems, out_sems, weight_sem, share_sems,
):
    slots, size = buf.shape[0], buf.shape[1]
    halves = tuple(range(size // (2 * LANES)))
    held = (h0, h1, h2, h3, h4, h5)
    xs, xt, v_ref, gate, rates, gain = held
    copies = load((s0, s1, s2, s3, s4, s5), held, small_sems)
    sources(ids, src)
    fetch(src, states, recv, buf, sems)
    for copy in copies:
        copy.wait()
    weight_copy = pltpu.make_async_copy(weight_ref, weight, weight_sem)
    weight_copy.start()
    wait = lambda r: pltpu.make_async_copy(states.at[0], buf.at[r], sems.at[r]).wait()
    products(halves, xs, buf, pr, wait)
    is_live = lax.broadcasted_iota(jnp.int32, (slots, 1), 0) < live[0]
    solve(halves, is_live, xt, v_ref, gate, rates, gain, normed, u_ref, pr)
    batch = 4

    def some(k, carry):
        for i in range(batch):
            for n in halves:
                renew(n, n, xs, u_ref, buf, new, k * batch + i)
        for i in range(batch):
            r = k * batch + i

            @pl.when(src[r] >= -1)
            def _():
                pltpu.make_async_copy(new.at[r], new_states.at[r], out_sems.at[r]).start()

        return carry

    lax.fori_loop(0, slots // batch, some, 0)
    rows = jnp.concatenate([normed[t] for t in range(normed.shape[0])], axis=0)
    columns = sent.shape[2]
    core = lax.rem(lax.axis_index("head"), 2)
    weight_copy.wait()
    for n, (out, c) in enumerate(((sent, 1 - core), (kept, core))):
        for j in range(sent.shape[0]):
            at = pl.multiple_of((2 * j + c) * columns, columns)
            share[n, j] = jnp.dot(
                rows, weight[:, pl.ds(at, columns)], preferred_element_type=jnp.float32
            )
        pltpu.make_async_copy(share.at[n], out, share_sems.at[n]).start()

    def finish(r, carry):
        @pl.when(src[r] >= -1)
        def _():
            pltpu.make_async_copy(new.at[r], new_states.at[r], out_sems.at[r]).wait()

        return carry

    lax.fori_loop(0, slots, finish, 0)
    for n, out in enumerate((sent, kept)):
        wait_all(out, share_sems.at[n])


def late_share(half, base, recv, weight_ref, smalls, held, small_sems, work):
    buf, pr, u_ref, normed, weight, sems, weight_sem = work
    count, size = buf.shape[0], buf.shape[1]

    def copy(i):
        return pltpu.make_async_copy(recv.at[i, pl.ds(base, size)], buf.at[i], sems.at[i])

    def start(i, carry):
        copy(i).start()
        return carry

    copies = load(smalls, held, small_sems)
    lax.fori_loop(0, count, start, 0, unroll=8)
    weight_copy = pltpu.make_async_copy(
        weight_ref.at[pl.ds(half * size, size)], weight, weight_sem
    )
    weight_copy.start()
    for small in copies:
        small.wait()
    xs, xt, v_ref, gate, rates, live, gain = held[:7]
    products((half,), xs, buf, pr, lambda i: copy(i).wait())
    is_live = live[:, 0:1] > 0.5
    solve((half,), is_live, xt, v_ref, gate, rates, gain, normed, u_ref, pr)
    rows = jnp.concatenate([normed[t] for t in range(normed.shape[0])], axis=0)
    weight_copy.wait()
    return rows


def late_update(half, ids, xs, u, buf, new, out, sems, wait):
    count, size = buf.shape[0], buf.shape[1]
    rows = pl.ds(half * size, size)
    batch = 8

    def some(k, carry):
        for j in range(batch):
            wait(k * batch + j)
        for j in range(batch):
            renew(half, 0, xs, u, buf, new, k * batch + j)
        for j in range(batch):
            i = k * batch + j

            @pl.when(ids[1, i] >= 0)
            def _():
                pltpu.make_async_copy(
                    new.at[i], out.at[ids[1, i], rows], sems.at[i]
                ).start()

        return carry

    lax.fori_loop(0, count // batch, some, 0)

    def finish(i, carry):
        @pl.when(ids[1, i] >= 0)
        def _():
            pltpu.make_async_copy(new.at[i], out.at[0, rows], sems.at[i]).wait()

        return carry

    lax.fori_loop(0, count, finish, 0)


def late_first(
    base, ids, recv, weight_ref, s0, s1, s2, s3, s4, s5, s6, before, out, new_states,
    h0, h1, h2, h3, h4, h5, h6, buf, pr, u_ref, normed, weight, new, share,
    small_sems, sems, weight_sem, out_sems, share_sem,
):
    held = (h0, h1, h2, h3, h4, h5, h6)
    work = (buf, pr, u_ref, normed, weight, sems, weight_sem)
    smalls = (s0, s1, s2, s3, s4, s5, s6)
    rows = late_share(0, base, recv, weight_ref, smalls, held, small_sems, work)
    columns = out.shape[2]
    for p in range(out.shape[0]):
        share[p] = jnp.dot(
            rows, weight[:, pl.ds(p * columns, columns)], preferred_element_type=jnp.float32
        )
        pltpu.make_async_copy(share.at[p], out.at[p], share_sem).start()
    late_update(0, ids, h0, u_ref, buf, new, new_states, out_sems, lambda i: None)
    wait_all(out, share_sem)


def late_second(
    base, recv, weight_ref, s0, s1, s2, s3, s4, s5, s6, s7, sent, kept, u_out,
    h0, h1, h2, h3, h4, h5, h6, h7, buf, pr, u_ref, normed, weight, share,
    small_sems, sems, weight_sem, out_sems,
):
    held = (h0, h1, h2, h3, h4, h5, h6, h7)
    work = (buf, pr, u_ref, normed, weight, sems, weight_sem)
    smalls = (s0, s1, s2, s3, s4, s5, s6, s7)
    rows = late_share(1, base, recv, weight_ref, smalls, held, small_sems, work)
    u_copy = pltpu.make_async_copy(u_ref, u_out, out_sems.at[0])
    u_copy.start()
    columns = sent.shape[2]
    core = lax.rem(lax.axis_index("head"), 2)
    for n, (out, c) in enumerate(((sent, 1 - core), (kept, core))):
        for j in range(sent.shape[0]):
            p = 2 * j + c
            at = pl.multiple_of(p * columns, columns)
            share[n, j] = h7[p] + jnp.dot(
                rows, weight[:, pl.ds(at, columns)], preferred_element_type=jnp.float32
            )
        pltpu.make_async_copy(share.at[n], out, out_sems.at[1 + n]).start()
    u_copy.wait()
    for n, out in enumerate((sent, kept)):
        wait_all(out, out_sems.at[1 + n])


def renew(half, place, xs, u, buf, new, r):
    dim = LANES
    steps = xs.shape[1] // 2
    wide = lambda v: v.astype(jnp.float32)
    k_high, k_low = split(xs[r, 0:steps, pl.ds(half * dim, dim)])
    rows = u[r, :, pl.ds(2 * place * dim, 2 * dim)]
    u_high, u_low = split(rows[0:steps])
    left = jnp.concatenate([wide(k_high), wide(k_high), wide(k_low), wide(k_low)], axis=0)
    right = jnp.concatenate([wide(u_high), wide(u_low), wide(u_high), wide(u_low)], axis=0)
    change = jnp.dot(
        left.T.astype(jnp.bfloat16),
        right.astype(jnp.bfloat16),
        preferred_element_type=jnp.float32,
    )
    for h in range(2):
        at = pl.ds((2 * place + h) * dim, dim)
        lanes = slice(h * dim, (h + 1) * dim)
        new[r, at, :] = buf[r, at, :] * rows[steps : steps + 1, lanes] + change[:, lanes]


def update_last(
    base, ids, recv, xs_ref, u_ref, before, out, buf, new, xs, u, small_sems, in_sems, out_sems
):
    count, size = buf.shape[0], buf.shape[1]
    copies = load((xs_ref, u_ref), (xs, u), small_sems)

    def copy(i):
        return pltpu.make_async_copy(recv.at[i, pl.ds(base, size)], buf.at[i], in_sems.at[i])

    def start(i, carry):
        copy(i).start()
        return carry

    lax.fori_loop(0, count, start, 0, unroll=8)
    for small in copies:
        small.wait()
    late_update(1, ids, xs, u, buf, new, out, out_sems, lambda i: copy(i).wait())


def merge_rows(
    ids_ref, early_kept, early_got, late_kept, late_got, o0, o1, o2, o3,
    ids, h0, h1, h2, h3, result, sems, out_sem,
):
    copies = load(
        (ids_ref, early_kept, early_got, late_kept, late_got), (ids, h0, h1, h2, h3), sems
    )
    for copy in copies:
        copy.wait()
    outs = (o0, o1, o2, o3)
    chips = len(outs)
    chip = lax.axis_index("head") // 2
    count = ids.shape[1]
    steps = h2.shape[1] // count
    slots = h0.shape[1] // steps
    put = one_hot(slots, ids[1:2, :])
    arrived = jnp.sum(put, axis=1, keepdims=True) > 0.0
    order = list(range(1, chips)) + [0]
    for k in order:
        j = lax.rem(chip + k, chips)
        for t in range(steps):
            rows = pl.ds(t * slots, slots)
            few = pl.ds(t * count, count)
            late = exact(put, h2[j, few, :] + h3[j, few, :])
            result[k, rows, :] = jnp.where(arrived, late, h0[j, rows, :] + h1[j, rows, :])
        pltpu.make_async_copy(result.at[k], outs[k], out_sem.at[k]).start()
    for k in order:
        pltpu.make_async_copy(result.at[k], outs[k], out_sem.at[k]).wait()


def finish_rows(live, t0, t1, t2, t3, out, h0, h1, h2, h3, sems):
    for copy in load((t0, t1, t2, t3), (h0, h1, h2, h3), sems):
        copy.wait()
    steps, slots = out.shape[0], out.shape[1]
    is_live = lax.broadcasted_iota(jnp.int32, (slots, 1), 0) < live[0]
    for t in range(steps):
        rows = pl.ds(t * slots, slots)
        total = (h0[rows, :] + h1[rows, :]) + (h2[rows, :] + h3[rows, :])
        out[t] = jnp.where(is_live, total, 0.0).astype(out.dtype)


def swap(v):
    parts = lax.axis_size("head")
    return lax.ppermute(v, "head", [(i, i ^ 1) for i in range(parts)])


def onward(v, k):
    parts = lax.axis_size("head")
    return lax.ppermute(v, "head", [(i, (i + 2 * k) % parts) for i in range(parts)])


def shards(
    hidden_in, w_query, w_key, w_value, w_gate_z, w_write, w_decay,
    conv_query, conv_key, conv_value, decay_rate, dt_bias, norm_gain, w_out,
    states, tail_query, tail_key, tail_value, send_slot, recv_slot, live_count,
):
    slots, steps, width = hidden_in.shape
    heads, dim = states.shape[1], states.shape[2]
    f32 = jnp.float32
    shape = jax.ShapeDtypeStruct
    size = heads * dim
    half = size // 2
    old = in_hbm(states.reshape(slots, size, dim))
    step_major = lambda v: jnp.transpose(v, (1, 0, 2))
    tails = [step_major(t) for t in (tail_query, tail_key, tail_value)]
    taps = tails[0].shape[0]
    extra = 2 * taps * sum(t.shape[2] for t in tails) // LANES
    extra += -extra % 64
    send = jnp.transpose(send_slot[0], (1, 0))
    groups = send.shape[1]

    out1, out2 = pl.pallas_call(
        pack,
        out_shape=[
            pltpu.HBM((groups, size + half + extra, LANES), f32),
            pltpu.HBM((groups, half, LANES), f32),
        ],
        in_specs=[SMEM] + [HBM] * 5,
        out_specs=[HBM, HBM],
        scratch_shapes=[
            pltpu.VMEM((2 * groups, size, LANES), f32),
            *[pltpu.VMEM(t.shape, f32) for t in tails],
            pltpu.VMEM(send.shape, jnp.int32),
            pltpu.VMEM((groups, extra, LANES), f32),
            pltpu.SemaphoreType.DMA((2 * groups,)),
            pltpu.SemaphoreType.DMA((4,)),
            pltpu.SemaphoreType.DMA((2,)),
        ],
        compiler_params=params(16),
        cost_estimate=cost(0, 4 * groups * size * LANES * 4),
        name="pack",
    )(send, in_hbm(send), old, *[in_hbm(t) for t in tails])

    def exchange(v):
        return lax.all_to_all(v, "group", split_axis=0, concat_axis=0, tiled=True)

    tie = lax.optimization_barrier
    recv1 = lax.cond(live_count[0] >= 0, exchange, jnp.zeros_like, out1)
    recv1, out2 = tie((recv1, out2))
    recv2 = exchange(out2)

    recv = jnp.transpose(recv_slot[0], (1, 0))
    flat_hidden = step_major(hidden_in).reshape(steps * slots, width)

    def project(weight):
        product = jnp.dot(flat_hidden, weight, preferred_element_type=f32)
        return product.reshape(steps, slots, weight.shape[1])

    pq, pk, pv, pg = (project(w) for w in (w_query, w_key, w_value, w_gate_z))
    pw, pd = project(w_write), project(w_decay)
    key_width, value_width = pq.shape[2], pv.shape[2]
    (
        xt, xs, values, rates, xt_late, xs_late, v_late, g_late, rates_late, live_late,
        ntq, ntk, ntv,
    ) = pl.pallas_call(
        prepare,
        out_shape=[
            pltpu.HBM((2 * steps, slots, key_width), f32),
            pltpu.HBM((slots, 2 * steps, key_width), f32),
            pltpu.HBM((steps, slots, value_width), f32),
            pltpu.HBM((steps, slots, 2 * heads), f32),
            pltpu.HBM((2 * steps, groups, key_width), f32),
            pltpu.HBM((groups, 2 * steps, key_width), f32),
            pltpu.HBM((steps, groups, value_width), f32),
            pltpu.HBM((steps, groups, value_width), f32),
            pltpu.HBM((steps, groups, 2 * heads), f32),
            pltpu.HBM((groups, LANES), f32),
            *[pltpu.HBM(t.shape, f32) for t in tails],
        ],
        in_specs=[VMEM, SMEM] + [HBM] * 4 + [VMEM] * 3 + [HBM] + [VMEM] * 7,
        out_specs=[VMEM] * 13,
        scratch_shapes=[
            *[pltpu.VMEM(t.shape, f32) for t in tails],
            pltpu.VMEM((groups, extra, LANES), f32),
            pltpu.VMEM(pg.shape, f32),
            pltpu.SemaphoreType.DMA((5,)),
        ],
        compiler_params=params(16),
        cost_estimate=cost(2_000_000, 4_000_000),
        name="prepare",
    )(
        recv, live_count, in_hbm(recv1), *[in_hbm(t) for t in tails], pq, pk, pv, in_hbm(pg), pw, pd,
        conv_query, conv_key, conv_value,
        decay_rate.reshape(1, heads), dt_bias.reshape(1, heads),
    )
    gain = norm_gain.reshape(1, dim)

    parts = lax.axis_size("head")
    columns = width // parts
    weight = in_hbm(w_out)
    early_args = [in_hbm(v) for v in (xs, xt, values, pg, rates, gain)]
    early_shape = (parts // 2, steps * slots, columns)
    sent, kept, new_states = pl.pallas_call(
        early_rows,
        out_shape=[
            pltpu.HBM(early_shape, f32),
            pltpu.HBM(early_shape, f32),
            pltpu.HBM((slots, size, dim), f32),
        ],
        in_specs=[SMEM, SMEM] + [HBM] * 9,
        out_specs=[HBM] * 3,
        scratch_shapes=[
            *[pltpu.VMEM(v.shape, f32) for v in early_args],
            pltpu.SMEM((slots,), jnp.int32),
            pltpu.VMEM((slots, size, dim), f32),
            pltpu.VMEM((slots, size, dim), f32),
            pltpu.VMEM((slots, 2 * steps, size), f32),
            pltpu.VMEM((slots, 2 * steps, size), f32),
            pltpu.VMEM((steps, slots, size), jnp.bfloat16),
            pltpu.VMEM((size, width), jnp.bfloat16),
            pltpu.VMEM((2, *early_shape), f32),
            pltpu.SemaphoreType.DMA((6,)),
            pltpu.SemaphoreType.DMA((slots,)),
            pltpu.SemaphoreType.DMA((slots,)),
            pltpu.SemaphoreType.DMA,
            pltpu.SemaphoreType.DMA((2,)),
        ],
        compiler_params=params(32),
        cost_estimate=cost(500_000_000, 22_000_000),
        name="early_rows",
    )(recv, live_count, old, in_hbm(recv1), weight, *early_args)
    swapped = swap(sent)

    late_args = (xs_late, xt_late, v_late, g_late, rates_late, live_late, gain)
    late_args = [in_hbm(v) for v in late_args]
    pieces_shape = (parts, steps * groups, columns)
    work = [
        pltpu.VMEM((groups, half, dim), f32),
        pltpu.VMEM((groups, 2 * steps, half), f32),
        pltpu.VMEM((groups, 2 * steps, half), f32),
        pltpu.VMEM((steps, groups, half), jnp.bfloat16),
        pltpu.VMEM((half, width), jnp.bfloat16),
    ]
    held = [pltpu.VMEM(v.shape, f32) for v in late_args]
    pieces, new_states = pl.pallas_call(
        functools.partial(late_first, size),
        out_shape=[pltpu.HBM(pieces_shape, f32), pltpu.HBM((slots, size, dim), f32)],
        in_specs=[SMEM] + [HBM] * 10,
        out_specs=[HBM, HBM],
        scratch_shapes=[
            *held,
            *work,
            pltpu.VMEM((groups, half, dim), f32),
            pltpu.VMEM(pieces_shape, f32),
            pltpu.SemaphoreType.DMA((len(held),)),
            pltpu.SemaphoreType.DMA((groups,)),
            pltpu.SemaphoreType.DMA,
            pltpu.SemaphoreType.DMA((groups,)),
            pltpu.SemaphoreType.DMA,
        ],
        input_output_aliases={10: 1},
        compiler_params=params(16),
        cost_estimate=cost(200_000_000, 8_000_000),
        name="late_first",
    )(recv, in_hbm(recv1), weight, *late_args, new_states)
    recv2, pieces, new_states = tie((recv2, pieces, new_states))
    late_shape = (parts // 2, steps * groups, columns)
    late_sent, late_kept, u_last = pl.pallas_call(
        functools.partial(late_second, 0),
        out_shape=[
            pltpu.HBM(late_shape, f32),
            pltpu.HBM(late_shape, f32),
            pltpu.HBM((groups, 2 * steps, half), f32),
        ],
        in_specs=[HBM] * 10,
        out_specs=[HBM] * 3,
        scratch_shapes=[
            *held,
            pltpu.VMEM(pieces_shape, f32),
            *work,
            pltpu.VMEM((2, *late_shape), f32),
            pltpu.SemaphoreType.DMA((len(held) + 1,)),
            pltpu.SemaphoreType.DMA((groups,)),
            pltpu.SemaphoreType.DMA,
            pltpu.SemaphoreType.DMA((3,)),
        ],
        compiler_params=params(16),
        cost_estimate=cost(150_000_000, 5_000_000),
        name="late_second",
    )(in_hbm(recv2), weight, *late_args, in_hbm(pieces))
    chips = parts // 2
    rows_shape = (steps * slots, columns)
    merge_args = (kept, swapped, late_kept, swap(late_sent))
    terms = pl.pallas_call(
        merge_rows,
        out_shape=[pltpu.HBM(rows_shape, f32)] * chips,
        in_specs=[HBM, HBM, ANY, HBM, ANY],
        out_specs=[HBM] * chips,
        scratch_shapes=[
            pltpu.VMEM(recv.shape, jnp.int32),
            *[pltpu.VMEM(v.shape, f32) for v in merge_args],
            pltpu.VMEM((chips, *rows_shape), f32),
            pltpu.SemaphoreType.DMA((5,)),
            pltpu.SemaphoreType.DMA((chips,)),
        ],
        compiler_params=params(16),
        cost_estimate=cost(2_000_000, 3_000_000),
        name="merge_rows",
    )(in_hbm(recv), in_hbm(kept), swapped, in_hbm(late_kept), merge_args[3])
    terms = [terms[0]] + [onward(terms[k], k) for k in range(1, chips)]
    new_states = pl.pallas_call(
        functools.partial(update_last, 0),
        out_shape=pltpu.HBM((slots, size, dim), f32),
        in_specs=[SMEM] + [HBM] * 4,
        out_specs=HBM,
        scratch_shapes=[
            pltpu.VMEM((groups, half, dim), f32),
            pltpu.VMEM((groups, half, dim), f32),
            pltpu.VMEM(xs_late.shape, f32),
            pltpu.VMEM((groups, 2 * steps, half), f32),
            pltpu.SemaphoreType.DMA((2,)),
            pltpu.SemaphoreType.DMA((groups,)),
            pltpu.SemaphoreType.DMA((groups,)),
        ],
        input_output_aliases={4: 0},
        compiler_params=params(16),
        cost_estimate=cost(32_000_000, 2 * groups * half * dim * 4),
        name="update_last",
    )(recv, in_hbm(recv2), late_args[0], in_hbm(u_last), new_states)

    layer_out = pl.pallas_call(
        finish_rows,
        out_shape=shape((steps, slots, columns), jnp.bfloat16),
        in_specs=[SMEM, HBM] + [ANY] * (chips - 1),
        out_specs=VMEM,
        scratch_shapes=[
            *[pltpu.VMEM(rows_shape, f32)] * chips,
            pltpu.SemaphoreType.DMA((chips,)),
        ],
        compiler_params=params(16),
        cost_estimate=cost(1_000_000, 1_000_000),
        name="finish_rows",
    )(live_count, in_hbm(terms[0]), *terms[1:])
    return (
        step_major(layer_out),
        new_states.reshape(states.shape),
        step_major(ntq),
        step_major(ntk),
        step_major(ntv),
    )


def solution(mesh):
    by_head = P(None, "head")
    by_both = P("group", None, "head")
    return jax.shard_map(
        shards,
        mesh=mesh,
        in_specs=(
            P("group", None, None),
            *([by_head] * 9),
            P("head"),
            P("head"),
            P(),
            P("head", None),
            P("group", "head", None, None),
            by_both,
            by_both,
            by_both,
            P("group", None, None),
            P("group", None, None),
            P("group"),
        ),
        out_specs=(
            by_both,
            P("group", "head", None, None),
            by_both,
            by_both,
            by_both,
        ),
        check_vma=False,
    )
```

```python
import functools

import jax
import jax.numpy as jnp
from jax import lax
from jax.experimental import pallas as pl
from jax.experimental.pallas import tpu as pltpu
from jax.sharding import PartitionSpec as P

SMEM = pl.BlockSpec(memory_space=pltpu.SMEM)
VMEM = pl.BlockSpec(memory_space=pltpu.VMEM)
HBM = pl.BlockSpec(memory_space=pltpu.HBM)
ANY = pl.BlockSpec(memory_space=pl.ANY)
LANES = 128


def params(mib):
    return pltpu.CompilerParams(vmem_limit_bytes=mib * 1024 * 1024)


def cost(flops, moved):
    return pl.CostEstimate(flops=flops, bytes_accessed=moved, transcendentals=0)


def in_hbm(v):
    return pltpu.with_memory_space_constraint(v, pltpu.HBM)


def wait_all(ref, sem):
    pltpu.make_async_copy(ref, ref, sem).wait()


def load(refs, bufs, sems):
    copies = [
        pltpu.make_async_copy(ref, buf, sems.at[n]) for n, (ref, buf) in enumerate(zip(refs, bufs))
    ]
    for copy in copies:
        copy.start()
    return copies


def exact(a, b):
    return jnp.dot(a, b, precision=lax.Precision.HIGHEST, preferred_element_type=jnp.float32)


def exact_t(a, b):
    return lax.dot_general(
        a, b, (((0,), (0,)), ((), ())),
        precision=lax.Precision.HIGHEST, preferred_element_type=jnp.float32,
    )


def one_hot(slots, ids):
    hit = lax.broadcasted_iota(jnp.int32, (slots, ids.shape[1]), 0) == ids
    return hit.astype(jnp.float32)


def split(v):
    high = v.astype(jnp.bfloat16)
    return high, (v - high.astype(jnp.float32)).astype(jnp.bfloat16)


def pack(
    send, ids_ref, states, tq, tk, tv, out1, out2,
    buf, bq, bk, bv, ids, rows, tail_sems, in_sems, sems,
):
    groups, slots, size = send.shape[1], states.shape[0], states.shape[1]
    rest = out2.shape[1]
    lower = size - rest
    extra = rows.shape[1]
    held = (bq, bk, bv)
    tails = load((tq, tk, tv, ids_ref), (bq, bk, bv, ids), tail_sems)

    def second(g, carry):
        slot = jnp.maximum(send[1, g], 0)
        pltpu.make_async_copy(
            states.at[slot, pl.ds(lower, rest)], buf.at[g], in_sems.at[g]
        ).start()
        pltpu.make_async_copy(
            states.at[slot, pl.ds(0, lower)], out1.at[g, pl.ds(size, lower)], sems.at[0]
        ).start()
        return carry

    def first(g, carry):
        slot = jnp.maximum(send[0, g], 0)
        pltpu.make_async_copy(
            states.at[slot], out1.at[g, pl.ds(0, size)], sems.at[0]
        ).start()
        return carry

    lax.fori_loop(0, groups, second, 0, unroll=8)
    lax.fori_loop(0, groups, first, 0, unroll=8)

    def move(g, carry):
        pltpu.make_async_copy(
            states.at[0, pl.ds(lower, rest)], buf.at[g], in_sems.at[g]
        ).wait()
        pltpu.make_async_copy(buf.at[g], out2.at[g], sems.at[1]).start()
        return carry

    lax.fori_loop(0, groups, move, 0, unroll=4)
    for copy in tails:
        copy.wait()
    for c in range(2):
        pick = one_hot(slots, ids[c : c + 1, :])
        at = c * (extra // 2)
        for j in range(tq.shape[0]):
            for ref in held:
                chosen = exact_t(pick, ref[j])
                for g in range(ref.shape[2] // LANES):
                    rows[:, at, :] = chosen[:, g * LANES : (g + 1) * LANES]
                    at += 1
    pltpu.make_async_copy(rows, out1.at[:, pl.ds(size + lower, extra)], sems.at[0]).start()
    wait_all(out1, sems.at[0])
    wait_all(out2, sems.at[1])


def prepare(
    ids, live, recv, tq, tk, tv, pq, pk, pv, pg, pw, pd, cq, ck, cv, pace, bias,
    xt, xs, v_ref, rates, xt_late, xs_late, v_late, g_late, rates_late, live_late,
    ntq, ntk, ntv, bq, bk, bv, rows, gate, sems,
):
    held = (bq, bk, bv)
    copies = [
        pltpu.make_async_copy(ref, dst, sems.at[n])
        for n, (ref, dst) in enumerate(zip((tq, tk, tv), held))
    ]
    extra = rows.shape[1]
    copies.append(
        pltpu.make_async_copy(recv.at[:, pl.ds(recv.shape[1] - extra, extra)], rows, sems.at[3])
    )
    copies.append(pltpu.make_async_copy(pg, gate, sems.at[4]))
    for copy in copies:
        copy.start()
    taps, slots = tq.shape[0], tq.shape[1]
    puts = [one_hot(slots, ids[c : c + 1, :]) for c in range(2)]
    put = jnp.concatenate(puts, axis=1)
    arrived = jnp.sum(put, axis=1, keepdims=True) > 0.0
    late = puts[1]
    steps = pq.shape[0]
    is_live = lax.broadcasted_iota(jnp.int32, (slots, 1), 0) < live[0]
    heads = pw.shape[2]
    for t in range(steps):
        x = pd[t] + bias[...]
        soft = jnp.maximum(x, 0.0) + jnp.log1p(jnp.exp(-jnp.abs(x)))
        rates[t, :, 0:heads] = jnp.exp(-pace[...] * soft)
        rates[t, :, heads : 2 * heads] = jax.nn.sigmoid(pw[t])
        rates_late[t] = exact_t(late, rates[t])
    live_late[...] = exact_t(
        late, jnp.broadcast_to(is_live.astype(jnp.float32), (slots, LANES))
    )
    for copy in copies:
        copy.wait()
    for t in range(steps):
        g_late[t] = exact_t(late, gate[t])
    moved = {n: [] for n in range(3)}
    at = 0
    for j in range(taps):
        for n, ref in enumerate(held):
            groups = ref.shape[2] // LANES
            sent = [
                jnp.concatenate([rows[:, at + c + g, :] for g in range(groups)], axis=1)
                for c in (0, extra // 2)
            ]
            at += groups
            sent = exact(put, jnp.concatenate(sent, axis=0))
            moved[n].append(jnp.where(arrived, sent, ref[j]))

    def conv(before, proj, kernel, new):
        kernel = kernel[...].astype(jnp.float32)
        window = before + [proj[t] for t in range(steps)]
        outs = []
        for t in range(steps):
            mixed = window[t] * kernel[0:1, :]
            for j in range(1, taps + 1):
                mixed = mixed + window[t + j] * kernel[j : j + 1, :]
            outs.append(mixed * jax.nn.sigmoid(mixed))
        for j in range(taps):
            new[j] = jnp.where(is_live, window[steps + j], window[j])
        return outs

    def unit(v, scale):
        parts = []
        for h in range(v.shape[1] // LANES):
            part = v[:, h * LANES : (h + 1) * LANES]
            total = jnp.sum(part * part, axis=1, keepdims=True)
            parts.append(part * (lax.rsqrt(total + 1e-06) * scale))
        return jnp.concatenate(parts, axis=1)

    queries = [unit(v, LANES**-0.5) for v in conv(moved[0], pq, cq, ntq)]
    keys = [unit(v, 1.0) for v in conv(moved[1], pk, ck, ntk)]
    for n, v in enumerate(keys + queries):
        xt[n] = v
        xs[:, n, :] = v
        v = exact_t(late, v)
        xt_late[n] = v
        xs_late[:, n, :] = v
    for t, v in enumerate(conv(moved[2], pv, cv, ntv)):
        v_ref[t] = v
        v_late[t] = exact_t(late, v)


def solve(halves, is_live, xt, v_ref, gate, rates, gain, normed, u_ref, pr):
    dim = LANES
    steps = v_ref.shape[0]
    slots = v_ref.shape[1]
    heads = rates.shape[2] // 2
    inner = lambda a, b: jnp.sum(a * b, axis=1, keepdims=True)
    for n, half in enumerate(halves):
        key_lanes = pl.ds(half * dim, dim)
        keys = [xt[t, :, key_lanes] for t in range(steps)]
        queries = [xt[steps + t, :, key_lanes] for t in range(steps)]
        kk = {(s, t): inner(keys[s], keys[t]) for t in range(steps) for s in range(t)}
        kq = {(s, t): inner(keys[s], queries[t]) for t in range(steps) for s in range(t + 1)}
        for h in range(2):
            head = 2 * half + h
            lanes = pl.ds((2 * n + h) * dim, dim)
            wide = pl.ds(head * dim, dim)
            fall = [rates[t, :, head : head + 1] for t in range(steps)]
            rate = [rates[t, :, heads + head : heads + head + 1] for t in range(steps)]
            ratio = {}
            for s in range(steps):
                for t in range(s + 1, steps):
                    ratio[s, t] = fall[t] if t == s + 1 else ratio[s, t - 1] * fall[t]
            total = [fall[0]]
            for t in range(1, steps):
                total.append(total[-1] * fall[t])
            us = []
            for t in range(steps):
                gap = v_ref[t, :, wide] - total[t] * pr[:, t, lanes]
                for s in range(t):
                    gap = gap - (ratio[s, t] * kk[s, t]) * us[s]
                us.append(gap * rate[t])
                out = total[t] * pr[:, steps + t, lanes]
                for s in range(t + 1):
                    weight = kq[s, t] if s == t else ratio[s, t] * kq[s, t]
                    out = out + weight * us[s]
                mean = jnp.mean(out * out, axis=1, keepdims=True)
                z = gate[t, :, wide]
                out = out * lax.rsqrt(mean + 1e-06) * gain[...] * (z * jax.nn.sigmoid(z))
                normed[t, :, lanes] = out.astype(normed.dtype)
            for s in range(steps):
                last = us[s] if s == steps - 1 else ratio[s, steps - 1] * us[s]
                u_ref[:, s, lanes] = jnp.where(is_live, last, 0.0)
            u_ref[:, steps, lanes] = jnp.broadcast_to(
                jnp.where(is_live, total[-1], 1.0), (slots, dim)
            )


def products(halves, xs, buf, pr, wait):
    dim = LANES
    batch = 8 // len(halves)

    def some(k, carry):
        for i in range(batch):
            wait(k * batch + i)
        for i in range(batch):
            r = k * batch + i
            for n, half in enumerate(halves):
                state = jnp.concatenate(
                    [buf[r, pl.ds((2 * n + h) * dim, dim), :] for h in range(2)], axis=1
                )
                high, low = split(state)
                both = jnp.concatenate(split(xs[r, :, pl.ds(half * dim, dim)]), axis=0)
                a = jnp.dot(both, high, preferred_element_type=jnp.float32)
                a = a + jnp.dot(both, low, preferred_element_type=jnp.float32)
                rows = both.shape[0] // 2
                pr[r, :, pl.ds(2 * n * dim, 2 * dim)] = a[0:rows] + a[rows:]
        return carry

    lax.fori_loop(0, buf.shape[0] // batch, some, 0)


def sources(ids, src):
    groups = ids.shape[1]

    def clear(r, carry):
        src[r] = -1
        return carry

    lax.fori_loop(0, src.shape[0], clear, 0, unroll=8)
    for c in range(2):

        def put(g, carry, c=c):
            @pl.when(ids[c, g] >= 0)
            def _():
                src[ids[c, g]] = g if c == 0 else -2

            return carry

        lax.fori_loop(0, groups, put, 0, unroll=4)


def fetch(src, states, recv, buf, sems):
    slots, size = states.shape[0], states.shape[1]

    def start(r, carry):
        @pl.when(src[r] >= 0)
        def _():
            pltpu.make_async_copy(
                recv.at[src[r], pl.ds(0, size)], buf.at[r], sems.at[r]
            ).start()

        @pl.when(src[r] < 0)
        def _():
            pltpu.make_async_copy(states.at[r], buf.at[r], sems.at[r]).start()

        return carry

    lax.fori_loop(0, slots, start, 0)


def early_rows(
    ids, live, states, recv, weight_ref, s0, s1, s2, s3, s4, s5,
    sent, kept, new_states, h0, h1, h2, h3, h4, h5,
    src, buf, new, pr, u_ref, normed, weight, share,
    small_sems, sems, out_sems, weight_sem, share_sems,
):
    slots, size = buf.shape[0], buf.shape[1]
    halves = tuple(range(size // (2 * LANES)))
    held = (h0, h1, h2, h3, h4, h5)
    xs, xt, v_ref, gate, rates, gain = held
    copies = load((s0, s1, s2, s3, s4, s5), held, small_sems)
    sources(ids, src)
    fetch(src, states, recv, buf, sems)
    for copy in copies:
        copy.wait()
    weight_copy = pltpu.make_async_copy(weight_ref, weight, weight_sem)
    weight_copy.start()
    wait = lambda r: pltpu.make_async_copy(states.at[0], buf.at[r], sems.at[r]).wait()
    products(halves, xs, buf, pr, wait)
    is_live = lax.broadcasted_iota(jnp.int32, (slots, 1), 0) < live[0]
    solve(halves, is_live, xt, v_ref, gate, rates, gain, normed, u_ref, pr)
    batch = 4

    def some(k, carry):
        for i in range(batch):
            for n in halves:
                renew(n, n, xs, u_ref, buf, new, k * batch + i)
        for i in range(batch):
            r = k * batch + i

            @pl.when(src[r] >= -1)
            def _():
                pltpu.make_async_copy(new.at[r], new_states.at[r], out_sems.at[r]).start()

        return carry

    lax.fori_loop(0, slots // batch, some, 0)
    rows = jnp.concatenate([normed[t] for t in range(normed.shape[0])], axis=0)
    columns = sent.shape[2]
    core = lax.rem(lax.axis_index("head"), 2)
    weight_copy.wait()
    for n, (out, c) in enumerate(((sent, 1 - core), (kept, core))):
        for j in range(sent.shape[0]):
            at = pl.multiple_of((2 * j + c) * columns, columns)
            share[n, j] = jnp.dot(
                rows, weight[:, pl.ds(at, columns)], preferred_element_type=jnp.float32
            )
        pltpu.make_async_copy(share.at[n], out, share_sems.at[n]).start()

    def finish(r, carry):
        @pl.when(src[r] >= -1)
        def _():
            pltpu.make_async_copy(new.at[r], new_states.at[r], out_sems.at[r]).wait()

        return carry

    lax.fori_loop(0, slots, finish, 0)
    for n, out in enumerate((sent, kept)):
        wait_all(out, share_sems.at[n])


def late_share(half, base, recv, weight_ref, smalls, held, small_sems, work):
    buf, pr, u_ref, normed, weight, sems, weight_sem = work
    count, size = buf.shape[0], buf.shape[1]

    def copy(i):
        return pltpu.make_async_copy(recv.at[i, pl.ds(base, size)], buf.at[i], sems.at[i])

    def start(i, carry):
        copy(i).start()
        return carry

    copies = load(smalls, held, small_sems)
    lax.fori_loop(0, count, start, 0, unroll=8)
    weight_copy = pltpu.make_async_copy(
        weight_ref.at[pl.ds(half * size, size)], weight, weight_sem
    )
    weight_copy.start()
    for small in copies:
        small.wait()
    xs, xt, v_ref, gate, rates, live, gain = held[:7]
    products((half,), xs, buf, pr, lambda i: copy(i).wait())
    is_live = live[:, 0:1] > 0.5
    solve((half,), is_live, xt, v_ref, gate, rates, gain, normed, u_ref, pr)
    rows = jnp.concatenate([normed[t] for t in range(normed.shape[0])], axis=0)
    weight_copy.wait()
    return rows


def late_update(half, ids, xs, u, buf, new, out, sems, wait):
    count, size = buf.shape[0], buf.shape[1]
    rows = pl.ds(half * size, size)
    batch = 8

    def some(k, carry):
        for j in range(batch):
            wait(k * batch + j)
        for j in range(batch):
            renew(half, 0, xs, u, buf, new, k * batch + j)
        for j in range(batch):
            i = k * batch + j

            @pl.when(ids[1, i] >= 0)
            def _():
                pltpu.make_async_copy(
                    new.at[i], out.at[ids[1, i], rows], sems.at[i]
                ).start()

        return carry

    lax.fori_loop(0, count // batch, some, 0)

    def finish(i, carry):
        @pl.when(ids[1, i] >= 0)
        def _():
            pltpu.make_async_copy(new.at[i], out.at[0, rows], sems.at[i]).wait()

        return carry

    lax.fori_loop(0, count, finish, 0)


def late_first(
    base, ids, recv, weight_ref, s0, s1, s2, s3, s4, s5, s6, before, out, new_states,
    h0, h1, h2, h3, h4, h5, h6, buf, pr, u_ref, normed, weight, new, share,
    small_sems, sems, weight_sem, out_sems, share_sem,
):
    held = (h0, h1, h2, h3, h4, h5, h6)
    work = (buf, pr, u_ref, normed, weight, sems, weight_sem)
    smalls = (s0, s1, s2, s3, s4, s5, s6)
    rows = late_share(0, base, recv, weight_ref, smalls, held, small_sems, work)
    columns = out.shape[2]
    for p in range(out.shape[0]):
        share[p] = jnp.dot(
            rows, weight[:, pl.ds(p * columns, columns)], preferred_element_type=jnp.float32
        )
        pltpu.make_async_copy(share.at[p], out.at[p], share_sem).start()
    late_update(0, ids, h0, u_ref, buf, new, new_states, out_sems, lambda i: None)
    wait_all(out, share_sem)


def late_second(
    base, recv, weight_ref, s0, s1, s2, s3, s4, s5, s6, s7, sent, kept, u_out,
    h0, h1, h2, h3, h4, h5, h6, h7, buf, pr, u_ref, normed, weight, share,
    small_sems, sems, weight_sem, out_sems,
):
    held = (h0, h1, h2, h3, h4, h5, h6, h7)
    work = (buf, pr, u_ref, normed, weight, sems, weight_sem)
    smalls = (s0, s1, s2, s3, s4, s5, s6, s7)
    rows = late_share(1, base, recv, weight_ref, smalls, held, small_sems, work)
    u_copy = pltpu.make_async_copy(u_ref, u_out, out_sems.at[0])
    u_copy.start()
    columns = sent.shape[2]
    core = lax.rem(lax.axis_index("head"), 2)
    for n, (out, c) in enumerate(((sent, 1 - core), (kept, core))):
        for j in range(sent.shape[0]):
            p = 2 * j + c
            at = pl.multiple_of(p * columns, columns)
            share[n, j] = h7[p] + jnp.dot(
                rows, weight[:, pl.ds(at, columns)], preferred_element_type=jnp.float32
            )
        pltpu.make_async_copy(share.at[n], out, out_sems.at[1 + n]).start()
    u_copy.wait()
    for n, out in enumerate((sent, kept)):
        wait_all(out, out_sems.at[1 + n])


def renew(half, place, xs, u, buf, new, r):
    dim = LANES
    steps = xs.shape[1] // 2
    wide = lambda v: v.astype(jnp.float32)
    k_high, k_low = split(xs[r, 0:steps, pl.ds(half * dim, dim)])
    rows = u[r, :, pl.ds(2 * place * dim, 2 * dim)]
    u_high, u_low = split(rows[0:steps])
    left = jnp.concatenate([wide(k_high), wide(k_high), wide(k_low), wide(k_low)], axis=0)
    right = jnp.concatenate([wide(u_high), wide(u_low), wide(u_high), wide(u_low)], axis=0)
    change = jnp.dot(
        left.T.astype(jnp.bfloat16),
        right.astype(jnp.bfloat16),
        preferred_element_type=jnp.float32,
    )
    for h in range(2):
        at = pl.ds((2 * place + h) * dim, dim)
        lanes = slice(h * dim, (h + 1) * dim)
        new[r, at, :] = buf[r, at, :] * rows[steps : steps + 1, lanes] + change[:, lanes]


def update_last(
    base, ids, recv, xs_ref, u_ref, before, out, buf, new, xs, u, small_sems, in_sems, out_sems
):
    count, size = buf.shape[0], buf.shape[1]
    copies = load((xs_ref, u_ref), (xs, u), small_sems)

    def copy(i):
        return pltpu.make_async_copy(recv.at[i, pl.ds(base, size)], buf.at[i], in_sems.at[i])

    def start(i, carry):
        copy(i).start()
        return carry

    lax.fori_loop(0, count, start, 0, unroll=8)
    for small in copies:
        small.wait()
    late_update(1, ids, xs, u, buf, new, out, out_sems, lambda i: copy(i).wait())


def merge_rows(
    ids_ref, early_kept, early_got, late_kept, late_got, o0, o1, o2, o3,
    ids, h0, h1, h2, h3, result, sems, out_sem,
):
    copies = load(
        (ids_ref, early_kept, early_got, late_kept, late_got), (ids, h0, h1, h2, h3), sems
    )
    for copy in copies:
        copy.wait()
    outs = (o0, o1, o2, o3)
    chips = len(outs)
    chip = lax.axis_index("head") // 2
    count = ids.shape[1]
    steps = h2.shape[1] // count
    slots = h0.shape[1] // steps
    put = one_hot(slots, ids[1:2, :])
    arrived = jnp.sum(put, axis=1, keepdims=True) > 0.0
    order = list(range(1, chips)) + [0]
    for k in order:
        j = lax.rem(chip + k, chips)
        for t in range(steps):
            rows = pl.ds(t * slots, slots)
            few = pl.ds(t * count, count)
            late = exact(put, h2[j, few, :] + h3[j, few, :])
            result[k, rows, :] = jnp.where(arrived, late, h0[j, rows, :] + h1[j, rows, :])
        pltpu.make_async_copy(result.at[k], outs[k], out_sem.at[k]).start()
    for k in order:
        pltpu.make_async_copy(result.at[k], outs[k], out_sem.at[k]).wait()


def finish_rows(live, t0, t1, t2, t3, out, h0, h1, h2, h3, sems):
    for copy in load((t0, t1, t2, t3), (h0, h1, h2, h3), sems):
        copy.wait()
    steps, slots = out.shape[0], out.shape[1]
    is_live = lax.broadcasted_iota(jnp.int32, (slots, 1), 0) < live[0]
    for t in range(steps):
        rows = pl.ds(t * slots, slots)
        total = (h0[rows, :] + h1[rows, :]) + (h2[rows, :] + h3[rows, :])
        out[t] = jnp.where(is_live, total, 0.0).astype(out.dtype)


def swap(v):
    parts = lax.axis_size("head")
    return lax.ppermute(v, "head", [(i, i ^ 1) for i in range(parts)])


def onward(v, k):
    parts = lax.axis_size("head")
    return lax.ppermute(v, "head", [(i, (i + 2 * k) % parts) for i in range(parts)])


def shards(
    hidden_in, w_query, w_key, w_value, w_gate_z, w_write, w_decay,
    conv_query, conv_key, conv_value, decay_rate, dt_bias, norm_gain, w_out,
    states, tail_query, tail_key, tail_value, send_slot, recv_slot, live_count,
):
    slots, steps, width = hidden_in.shape
    heads, dim = states.shape[1], states.shape[2]
    f32 = jnp.float32
    shape = jax.ShapeDtypeStruct
    size = heads * dim
    half = size // 2
    old = states.reshape(slots, size, dim)
    step_major = lambda v: jnp.transpose(v, (1, 0, 2))
    tails = [step_major(t) for t in (tail_query, tail_key, tail_value)]
    taps = tails[0].shape[0]
    extra = 2 * taps * sum(t.shape[2] for t in tails) // LANES
    send = jnp.transpose(send_slot[0], (1, 0))
    groups = send.shape[1]

    first_shape = (groups, size + half + extra, LANES)
    second_shape = (groups, half, LANES)

    def exchange(v):
        return lax.all_to_all(v, "group", split_axis=0, concat_axis=0, tiled=True)

    def first_exchange(send, send_ref, old, *tails):
        out1, out2 = pl.pallas_call(
            pack,
            out_shape=[pltpu.VMEM(first_shape, f32), pltpu.HBM(second_shape, f32)],
            in_specs=[SMEM] + [HBM] * 5,
            out_specs=[VMEM, HBM],
            scratch_shapes=[
                pltpu.VMEM((groups, half, LANES), f32),
                *[pltpu.VMEM(t.shape, f32) for t in tails],
                pltpu.VMEM(send.shape, jnp.int32),
                pltpu.VMEM((groups, extra, LANES), f32),
                pltpu.SemaphoreType.DMA((4,)),
                pltpu.SemaphoreType.DMA((groups,)),
                pltpu.SemaphoreType.DMA((2,)),
            ],
            compiler_params=params(24),
            cost_estimate=cost(0, 4 * groups * size * LANES * 4),
            name="pack",
        )(send, in_hbm(send_ref), in_hbm(old), *[in_hbm(t) for t in tails])
        return exchange(out1), out2

    def no_exchange(*_):
        return jnp.zeros(first_shape, f32), jnp.zeros(second_shape, f32)

    tie = lax.optimization_barrier
    recv1, out2 = lax.cond(
        live_count[0] >= 0, first_exchange, no_exchange, send, send, old, *tails
    )
    recv1, out2 = tie((recv1, out2))
    recv2 = exchange(out2)

    recv = jnp.transpose(recv_slot[0], (1, 0))
    flat_hidden = step_major(hidden_in).reshape(steps * slots, width)

    def project(weight):
        product = jnp.dot(flat_hidden, weight, preferred_element_type=f32)
        return product.reshape(steps, slots, weight.shape[1])

    pq, pk, pv, pg = (project(w) for w in (w_query, w_key, w_value, w_gate_z))
    pw, pd = project(w_write), project(w_decay)
    key_width, value_width = pq.shape[2], pv.shape[2]
    (
        xt, xs, values, rates, xt_late, xs_late, v_late, g_late, rates_late, live_late,
        ntq, ntk, ntv,
    ) = pl.pallas_call(
        prepare,
        out_shape=[
            pltpu.HBM((2 * steps, slots, key_width), f32),
            pltpu.HBM((slots, 2 * steps, key_width), f32),
            pltpu.HBM((steps, slots, value_width), f32),
            pltpu.HBM((steps, slots, 2 * heads), f32),
            pltpu.HBM((2 * steps, groups, key_width), f32),
            pltpu.HBM((groups, 2 * steps, key_width), f32),
            pltpu.HBM((steps, groups, value_width), f32),
            pltpu.HBM((steps, groups, value_width), f32),
            pltpu.HBM((steps, groups, 2 * heads), f32),
            pltpu.HBM((groups, LANES), f32),
            *[pltpu.HBM(t.shape, f32) for t in tails],
        ],
        in_specs=[VMEM, SMEM] + [HBM] * 4 + [VMEM] * 3 + [HBM] + [VMEM] * 7,
        out_specs=[VMEM] * 13,
        scratch_shapes=[
            *[pltpu.VMEM(t.shape, f32) for t in tails],
            pltpu.VMEM((groups, extra, LANES), f32),
            pltpu.VMEM(pg.shape, f32),
            pltpu.SemaphoreType.DMA((5,)),
        ],
        compiler_params=params(16),
        cost_estimate=cost(2_000_000, 4_000_000),
        name="prepare",
    )(
        recv, live_count, in_hbm(recv1), *[in_hbm(t) for t in tails], pq, pk, pv, in_hbm(pg), pw, pd,
        conv_query, conv_key, conv_value,
        decay_rate.reshape(1, heads), dt_bias.reshape(1, heads),
    )
    gain = norm_gain.reshape(1, dim)

    parts = lax.axis_size("head")
    columns = width // parts
    weight = in_hbm(w_out)
    early_args = [in_hbm(v) for v in (xs, xt, values, pg, rates, gain)]
    early_shape = (parts // 2, steps * slots, columns)
    sent, kept, new_states = pl.pallas_call(
        early_rows,
        out_shape=[
            pltpu.HBM(early_shape, f32),
            pltpu.HBM(early_shape, f32),
            pltpu.HBM((slots, size, dim), f32),
        ],
        in_specs=[SMEM, SMEM] + [HBM] * 9,
        out_specs=[HBM] * 3,
        scratch_shapes=[
            *[pltpu.VMEM(v.shape, f32) for v in early_args],
            pltpu.SMEM((slots,), jnp.int32),
            pltpu.VMEM((slots, size, dim), f32),
            pltpu.VMEM((slots, size, dim), f32),
            pltpu.VMEM((slots, 2 * steps, size), f32),
            pltpu.VMEM((slots, 2 * steps, size), f32),
            pltpu.VMEM((steps, slots, size), jnp.bfloat16),
            pltpu.VMEM((size, width), jnp.bfloat16),
            pltpu.VMEM((2, *early_shape), f32),
            pltpu.SemaphoreType.DMA((6,)),
            pltpu.SemaphoreType.DMA((slots,)),
            pltpu.SemaphoreType.DMA((slots,)),
            pltpu.SemaphoreType.DMA,
            pltpu.SemaphoreType.DMA((2,)),
        ],
        compiler_params=params(32),
        cost_estimate=cost(500_000_000, 22_000_000),
        name="early_rows",
    )(recv, live_count, in_hbm(old), in_hbm(recv1), weight, *early_args)
    swapped = swap(sent)

    late_args = (xs_late, xt_late, v_late, g_late, rates_late, live_late, gain)
    late_args = [in_hbm(v) for v in late_args]
    pieces_shape = (parts, steps * groups, columns)
    work = [
        pltpu.VMEM((groups, half, dim), f32),
        pltpu.VMEM((groups, 2 * steps, half), f32),
        pltpu.VMEM((groups, 2 * steps, half), f32),
        pltpu.VMEM((steps, groups, half), jnp.bfloat16),
        pltpu.VMEM((half, width), jnp.bfloat16),
    ]
    held = [pltpu.VMEM(v.shape, f32) for v in late_args]
    pieces, new_states = pl.pallas_call(
        functools.partial(late_first, size),
        out_shape=[pltpu.HBM(pieces_shape, f32), pltpu.HBM((slots, size, dim), f32)],
        in_specs=[SMEM] + [HBM] * 10,
        out_specs=[HBM, HBM],
        scratch_shapes=[
            *held,
            *work,
            pltpu.VMEM((groups, half, dim), f32),
            pltpu.VMEM(pieces_shape, f32),
            pltpu.SemaphoreType.DMA((len(held),)),
            pltpu.SemaphoreType.DMA((groups,)),
            pltpu.SemaphoreType.DMA,
            pltpu.SemaphoreType.DMA((groups,)),
            pltpu.SemaphoreType.DMA,
        ],
        input_output_aliases={10: 1},
        compiler_params=params(16),
        cost_estimate=cost(200_000_000, 8_000_000),
        name="late_first",
    )(recv, in_hbm(recv1), weight, *late_args, new_states)
    recv2, pieces, new_states = tie((recv2, pieces, new_states))
    late_shape = (parts // 2, steps * groups, columns)
    late_sent, late_kept, u_last = pl.pallas_call(
        functools.partial(late_second, 0),
        out_shape=[
            pltpu.HBM(late_shape, f32),
            pltpu.HBM(late_shape, f32),
            pltpu.HBM((groups, 2 * steps, half), f32),
        ],
        in_specs=[HBM] * 10,
        out_specs=[HBM] * 3,
        scratch_shapes=[
            *held,
            pltpu.VMEM(pieces_shape, f32),
            *work,
            pltpu.VMEM((2, *late_shape), f32),
            pltpu.SemaphoreType.DMA((len(held) + 1,)),
            pltpu.SemaphoreType.DMA((groups,)),
            pltpu.SemaphoreType.DMA,
            pltpu.SemaphoreType.DMA((3,)),
        ],
        compiler_params=params(16),
        cost_estimate=cost(150_000_000, 5_000_000),
        name="late_second",
    )(in_hbm(recv2), weight, *late_args, in_hbm(pieces))
    chips = parts // 2
    rows_shape = (steps * slots, columns)
    merge_args = (kept, swapped, late_kept, swap(late_sent))
    terms = pl.pallas_call(
        merge_rows,
        out_shape=[pltpu.HBM(rows_shape, f32)] * chips,
        in_specs=[HBM, HBM, ANY, HBM, ANY],
        out_specs=[HBM] * chips,
        scratch_shapes=[
            pltpu.VMEM(recv.shape, jnp.int32),
            *[pltpu.VMEM(v.shape, f32) for v in merge_args],
            pltpu.VMEM((chips, *rows_shape), f32),
            pltpu.SemaphoreType.DMA((5,)),
            pltpu.SemaphoreType.DMA((chips,)),
        ],
        compiler_params=params(16),
        cost_estimate=cost(2_000_000, 3_000_000),
        name="merge_rows",
    )(in_hbm(recv), in_hbm(kept), swapped, in_hbm(late_kept), merge_args[3])
    terms = [terms[0]] + [onward(terms[k], k) for k in range(1, chips)]
    new_states = pl.pallas_call(
        functools.partial(update_last, 0),
        out_shape=pltpu.HBM((slots, size, dim), f32),
        in_specs=[SMEM] + [HBM] * 4,
        out_specs=HBM,
        scratch_shapes=[
            pltpu.VMEM((groups, half, dim), f32),
            pltpu.VMEM((groups, half, dim), f32),
            pltpu.VMEM(xs_late.shape, f32),
            pltpu.VMEM((groups, 2 * steps, half), f32),
            pltpu.SemaphoreType.DMA((2,)),
            pltpu.SemaphoreType.DMA((groups,)),
            pltpu.SemaphoreType.DMA((groups,)),
        ],
        input_output_aliases={4: 0},
        compiler_params=params(16),
        cost_estimate=cost(32_000_000, 2 * groups * half * dim * 4),
        name="update_last",
    )(recv, in_hbm(recv2), late_args[0], in_hbm(u_last), new_states)

    layer_out = pl.pallas_call(
        finish_rows,
        out_shape=shape((steps, slots, columns), jnp.bfloat16),
        in_specs=[SMEM, HBM] + [ANY] * (chips - 1),
        out_specs=VMEM,
        scratch_shapes=[
            *[pltpu.VMEM(rows_shape, f32)] * chips,
            pltpu.SemaphoreType.DMA((chips,)),
        ],
        compiler_params=params(16),
        cost_estimate=cost(1_000_000, 1_000_000),
        name="finish_rows",
    )(live_count, in_hbm(terms[0]), *terms[1:])
    return (
        step_major(layer_out),
        new_states.reshape(states.shape),
        step_major(ntq),
        step_major(ntk),
        step_major(ntv),
    )


def solution(mesh):
    by_head = P(None, "head")
    by_both = P("group", None, "head")
    return jax.shard_map(
        shards,
        mesh=mesh,
        in_specs=(
            P("group", None, None),
            *([by_head] * 9),
            P("head"),
            P("head"),
            P(),
            P("head", None),
            P("group", "head", None, None),
            by_both,
            by_both,
            by_both,
            P("group", None, None),
            P("group", None, None),
            P("group"),
        ),
        out_specs=(
            by_both,
            P("group", "head", None, None),
            by_both,
            by_both,
            by_both,
        ),
        check_vma=False,
    )
```

```python
import functools

import jax
import jax.numpy as jnp
from jax import lax
from jax.experimental import pallas as pl
from jax.experimental.pallas import tpu as pltpu
from jax.sharding import PartitionSpec as P

SMEM = pl.BlockSpec(memory_space=pltpu.SMEM)
VMEM = pl.BlockSpec(memory_space=pltpu.VMEM)
HBM = pl.BlockSpec(memory_space=pltpu.HBM)
ANY = pl.BlockSpec(memory_space=pl.ANY)
LANES = 128


def params(mib):
    return pltpu.CompilerParams(vmem_limit_bytes=mib * 1024 * 1024)


def cost(flops, moved):
    return pl.CostEstimate(flops=flops, bytes_accessed=moved, transcendentals=0)


def in_hbm(v):
    return pltpu.with_memory_space_constraint(v, pltpu.HBM)


def in_vmem(v):
    return pltpu.with_memory_space_constraint(v, pltpu.VMEM)


def wait_all(ref, sem):
    pltpu.make_async_copy(ref, ref, sem).wait()


def load(refs, bufs, sems):
    copies = [
        pltpu.make_async_copy(ref, buf, sems.at[n]) for n, (ref, buf) in enumerate(zip(refs, bufs))
    ]
    for copy in copies:
        copy.start()
    return copies


def exact(a, b):
    return jnp.dot(a, b, precision=lax.Precision.HIGHEST, preferred_element_type=jnp.float32)


def exact_t(a, b):
    return lax.dot_general(
        a, b, (((0,), (0,)), ((), ())),
        precision=lax.Precision.HIGHEST, preferred_element_type=jnp.float32,
    )


def one_hot(slots, ids):
    hit = lax.broadcasted_iota(jnp.int32, (slots, ids.shape[1]), 0) == ids
    return hit.astype(jnp.float32)


def split(v):
    high = v.astype(jnp.bfloat16)
    return high, (v - high.astype(jnp.float32)).astype(jnp.bfloat16)


def pack(
    send, ids_ref, states, tq, tk, tv, out1, out2,
    buf, bq, bk, bv, ids, rows, tail_sems, in_sems, sems,
):
    groups, slots, size = send.shape[1], states.shape[0], states.shape[1]
    rest = out2.shape[1]
    lower = size - rest
    extra = rows.shape[1]
    held = (bq, bk, bv)
    tails = load((tq, tk, tv, ids_ref), (bq, bk, bv, ids), tail_sems)

    def second(g, carry):
        slot = jnp.maximum(send[1, g], 0)
        pltpu.make_async_copy(
            states.at[slot, pl.ds(lower, rest)], buf.at[g], in_sems.at[g]
        ).start()
        pltpu.make_async_copy(
            states.at[slot, pl.ds(0, lower)], out1.at[g, pl.ds(size, lower)], sems.at[0]
        ).start()
        return carry

    def first(g, carry):
        slot = jnp.maximum(send[0, g], 0)
        pltpu.make_async_copy(
            states.at[slot], out1.at[g, pl.ds(0, size)], sems.at[0]
        ).start()
        return carry

    lax.fori_loop(0, groups, second, 0, unroll=8)
    lax.fori_loop(0, groups, first, 0, unroll=8)

    def move(g, carry):
        pltpu.make_async_copy(
            states.at[0, pl.ds(lower, rest)], buf.at[g], in_sems.at[g]
        ).wait()
        pltpu.make_async_copy(buf.at[g], out2.at[g], sems.at[1]).start()
        return carry

    lax.fori_loop(0, groups, move, 0, unroll=4)
    for copy in tails:
        copy.wait()
    for c in range(2):
        pick = one_hot(slots, ids[c : c + 1, :])
        at = c * (extra // 2)
        for j in range(tq.shape[0]):
            for ref in held:
                chosen = exact_t(pick, ref[j])
                for g in range(ref.shape[2] // LANES):
                    rows[:, at, :] = chosen[:, g * LANES : (g + 1) * LANES]
                    at += 1
    pltpu.make_async_copy(rows, out1.at[:, pl.ds(size + lower, extra)], sems.at[0]).start()
    wait_all(out1, sems.at[0])
    wait_all(out2, sems.at[1])


def prepare(
    ids, live, recv, tq, tk, tv, pq, pk, pv, pg, pw, pd, cq, ck, cv, pace, bias,
    xt, xs, v_ref, rates, xt_late, xs_late, v_late, g_late, rates_late, live_late,
    ntq, ntk, ntv, bq, bk, bv, rows, gate, sems,
):
    held = (bq, bk, bv)
    copies = [
        pltpu.make_async_copy(ref, dst, sems.at[n])
        for n, (ref, dst) in enumerate(zip((tq, tk, tv), held))
    ]
    extra = rows.shape[1]
    copies.append(
        pltpu.make_async_copy(recv.at[:, pl.ds(recv.shape[1] - extra, extra)], rows, sems.at[3])
    )
    copies.append(pltpu.make_async_copy(pg, gate, sems.at[4]))
    for copy in copies:
        copy.start()
    taps, slots = tq.shape[0], tq.shape[1]
    puts = [one_hot(slots, ids[c : c + 1, :]) for c in range(2)]
    put = jnp.concatenate(puts, axis=1)
    arrived = jnp.sum(put, axis=1, keepdims=True) > 0.0
    late = puts[1]
    steps = pq.shape[0]
    is_live = lax.broadcasted_iota(jnp.int32, (slots, 1), 0) < live[0]
    heads = pw.shape[2]
    for t in range(steps):
        x = pd[t] + bias[...]
        soft = jnp.maximum(x, 0.0) + jnp.log1p(jnp.exp(-jnp.abs(x)))
        rates[t, :, 0:heads] = jnp.exp(-pace[...] * soft)
        rates[t, :, heads : 2 * heads] = jax.nn.sigmoid(pw[t])
        rates_late[t] = exact_t(late, rates[t])
    live_late[...] = exact_t(
        late, jnp.broadcast_to(is_live.astype(jnp.float32), (slots, LANES))
    )
    for copy in copies:
        copy.wait()
    for t in range(steps):
        g_late[t] = exact_t(late, gate[t])
    moved = {n: [] for n in range(3)}
    at = 0
    for j in range(taps):
        for n, ref in enumerate(held):
            groups = ref.shape[2] // LANES
            sent = [
                jnp.concatenate([rows[:, at + c + g, :] for g in range(groups)], axis=1)
                for c in (0, extra // 2)
            ]
            at += groups
            sent = exact(put, jnp.concatenate(sent, axis=0))
            moved[n].append(jnp.where(arrived, sent, ref[j]))

    def conv(before, proj, kernel, new):
        kernel = kernel[...].astype(jnp.float32)
        window = before + [proj[t] for t in range(steps)]
        outs = []
        for t in range(steps):
            mixed = window[t] * kernel[0:1, :]
            for j in range(1, taps + 1):
                mixed = mixed + window[t + j] * kernel[j : j + 1, :]
            outs.append(mixed * jax.nn.sigmoid(mixed))
        for j in range(taps):
            new[j] = jnp.where(is_live, window[steps + j], window[j])
        return outs

    def unit(v, scale):
        parts = []
        for h in range(v.shape[1] // LANES):
            part = v[:, h * LANES : (h + 1) * LANES]
            total = jnp.sum(part * part, axis=1, keepdims=True)
            parts.append(part * (lax.rsqrt(total + 1e-06) * scale))
        return jnp.concatenate(parts, axis=1)

    queries = [unit(v, LANES**-0.5) for v in conv(moved[0], pq, cq, ntq)]
    keys = [unit(v, 1.0) for v in conv(moved[1], pk, ck, ntk)]
    for n, v in enumerate(keys + queries):
        xt[n] = v
        xs[:, n, :] = v
        v = exact_t(late, v)
        xt_late[n] = v
        xs_late[:, n, :] = v
    for t, v in enumerate(conv(moved[2], pv, cv, ntv)):
        v_ref[t] = v
        v_late[t] = exact_t(late, v)


def solve(halves, is_live, xt, v_ref, gate, rates, gain, normed, u_ref, pr):
    dim = LANES
    steps = v_ref.shape[0]
    slots = v_ref.shape[1]
    heads = rates.shape[2] // 2
    inner = lambda a, b: jnp.sum(a * b, axis=1, keepdims=True)
    for n, half in enumerate(halves):
        key_lanes = pl.ds(half * dim, dim)
        keys = [xt[t, :, key_lanes] for t in range(steps)]
        queries = [xt[steps + t, :, key_lanes] for t in range(steps)]
        kk = {(s, t): inner(keys[s], keys[t]) for t in range(steps) for s in range(t)}
        kq = {(s, t): inner(keys[s], queries[t]) for t in range(steps) for s in range(t + 1)}
        for h in range(2):
            head = 2 * half + h
            lanes = pl.ds((2 * n + h) * dim, dim)
            wide = pl.ds(head * dim, dim)
            fall = [rates[t, :, head : head + 1] for t in range(steps)]
            rate = [rates[t, :, heads + head : heads + head + 1] for t in range(steps)]
            ratio = {}
            for s in range(steps):
                for t in range(s + 1, steps):
                    ratio[s, t] = fall[t] if t == s + 1 else ratio[s, t - 1] * fall[t]
            total = [fall[0]]
            for t in range(1, steps):
                total.append(total[-1] * fall[t])
            us = []
            for t in range(steps):
                gap = v_ref[t, :, wide] - total[t] * pr[:, t, lanes]
                for s in range(t):
                    gap = gap - (ratio[s, t] * kk[s, t]) * us[s]
                us.append(gap * rate[t])
                out = total[t] * pr[:, steps + t, lanes]
                for s in range(t + 1):
                    weight = kq[s, t] if s == t else ratio[s, t] * kq[s, t]
                    out = out + weight * us[s]
                mean = jnp.mean(out * out, axis=1, keepdims=True)
                z = gate[t, :, wide]
                out = out * lax.rsqrt(mean + 1e-06) * gain[...] * (z * jax.nn.sigmoid(z))
                normed[t, :, lanes] = out.astype(normed.dtype)
            for s in range(steps):
                last = us[s] if s == steps - 1 else ratio[s, steps - 1] * us[s]
                u_ref[:, s, lanes] = jnp.where(is_live, last, 0.0)
            u_ref[:, steps, lanes] = jnp.broadcast_to(
                jnp.where(is_live, total[-1], 1.0), (slots, dim)
            )


def products(halves, xs, buf, pr, wait):
    dim = LANES
    batch = 8 // len(halves)

    def some(k, carry):
        for i in range(batch):
            wait(k * batch + i)
        for i in range(batch):
            r = k * batch + i
            for n, half in enumerate(halves):
                state = jnp.concatenate(
                    [buf[r, pl.ds((2 * n + h) * dim, dim), :] for h in range(2)], axis=1
                )
                high, low = split(state)
                both = jnp.concatenate(split(xs[r, :, pl.ds(half * dim, dim)]), axis=0)
                a = jnp.dot(both, high, preferred_element_type=jnp.float32)
                a = a + jnp.dot(both, low, preferred_element_type=jnp.float32)
                rows = both.shape[0] // 2
                pr[r, :, pl.ds(2 * n * dim, 2 * dim)] = a[0:rows] + a[rows:]
        return carry

    lax.fori_loop(0, buf.shape[0] // batch, some, 0)


def sources(ids, src):
    groups = ids.shape[1]

    def clear(r, carry):
        src[r] = -1
        return carry

    lax.fori_loop(0, src.shape[0], clear, 0, unroll=8)
    for c in range(2):

        def put(g, carry, c=c):
            @pl.when(ids[c, g] >= 0)
            def _():
                src[ids[c, g]] = g if c == 0 else -2

            return carry

        lax.fori_loop(0, groups, put, 0, unroll=4)


def fetch(src, states, recv, buf, sems):
    slots, size = states.shape[0], states.shape[1]

    def start(r, carry):
        @pl.when(src[r] >= 0)
        def _():
            pltpu.make_async_copy(
                recv.at[src[r], pl.ds(0, size)], buf.at[r], sems.at[r]
            ).start()

        @pl.when(src[r] < 0)
        def _():
            pltpu.make_async_copy(states.at[r], buf.at[r], sems.at[r]).start()

        return carry

    lax.fori_loop(0, slots, start, 0)


def early_rows(
    ids, live, states, recv, weight_ref, s0, s1, s2, s3, s4, s5,
    sent, kept, new_states, h0, h1, h2, h3, h4, h5,
    src, buf, new, pr, u_ref, normed, weight,
    small_sems, sems, out_sems, weight_sem,
):
    slots, size = buf.shape[0], buf.shape[1]
    halves = tuple(range(size // (2 * LANES)))
    held = (h0, h1, h2, h3, h4, h5)
    xs, xt, v_ref, gate, rates, gain = held
    copies = load((s0, s1, s2, s3, s4, s5), held, small_sems)
    sources(ids, src)
    fetch(src, states, recv, buf, sems)
    for copy in copies:
        copy.wait()
    weight_copy = pltpu.make_async_copy(weight_ref, weight, weight_sem)
    weight_copy.start()
    wait = lambda r: pltpu.make_async_copy(states.at[0], buf.at[r], sems.at[r]).wait()
    products(halves, xs, buf, pr, wait)
    is_live = lax.broadcasted_iota(jnp.int32, (slots, 1), 0) < live[0]
    solve(halves, is_live, xt, v_ref, gate, rates, gain, normed, u_ref, pr)
    batch = 4

    def some(k, carry):
        for i in range(batch):
            for n in halves:
                renew(n, n, xs, u_ref, buf, new, k * batch + i)
        for i in range(batch):
            r = k * batch + i

            @pl.when(src[r] >= -1)
            def _():
                pltpu.make_async_copy(new.at[r], new_states.at[r], out_sems.at[r]).start()

        return carry

    lax.fori_loop(0, slots // batch, some, 0)
    rows = jnp.concatenate([normed[t] for t in range(normed.shape[0])], axis=0)
    columns = sent.shape[2]
    core = lax.rem(lax.axis_index("head"), 2)
    weight_copy.wait()
    for out, c in ((sent, 1 - core), (kept, core)):
        for j in range(sent.shape[0]):
            at = pl.multiple_of((2 * j + c) * columns, columns)
            out[j] = jnp.dot(
                rows, weight[:, pl.ds(at, columns)], preferred_element_type=jnp.float32
            )

    def finish(r, carry):
        @pl.when(src[r] >= -1)
        def _():
            pltpu.make_async_copy(new.at[r], new_states.at[r], out_sems.at[r]).wait()

        return carry

    lax.fori_loop(0, slots, finish, 0)


def late_share(half, weight_ref, smalls, work, buf, wait):
    pr, u_ref, normed, weight, weight_sem = work
    size = buf.shape[1]
    weight_copy = pltpu.make_async_copy(
        weight_ref.at[pl.ds(half * size, size)], weight, weight_sem
    )
    weight_copy.start()
    xs, xt, v_ref, gate, rates, live, gain = smalls
    products((half,), xs, buf, pr, wait)
    is_live = live[:, 0:1] > 0.5
    solve((half,), is_live, xt, v_ref, gate, rates, gain, normed, u_ref, pr)
    rows = jnp.concatenate([normed[t] for t in range(normed.shape[0])], axis=0)
    weight_copy.wait()
    return rows


def late_update(half, ids, xs, u, buf, new, out, sems, wait):
    count, size = buf.shape[0], buf.shape[1]
    rows = pl.ds(half * size, size)
    batch = 8

    def some(k, carry):
        for j in range(batch):
            wait(k * batch + j)
        for j in range(batch):
            renew(half, 0, xs, u, buf, new, k * batch + j)
        for j in range(batch):
            i = k * batch + j

            @pl.when(ids[1, i] >= 0)
            def _():
                pltpu.make_async_copy(
                    new.at[i], out.at[ids[1, i], rows], sems.at[i]
                ).start()

        return carry

    lax.fori_loop(0, count // batch, some, 0)

    def finish(i, carry):
        @pl.when(ids[1, i] >= 0)
        def _():
            pltpu.make_async_copy(new.at[i], out.at[0, rows], sems.at[i]).wait()

        return carry

    lax.fori_loop(0, count, finish, 0)


def late_first(
    base, ids, recv, weight_ref, s0, s1, s2, s3, s4, s5, s6, before, out, new_states,
    buf, pr, u_ref, normed, weight, new, share, sems, weight_sem, out_sems, share_sem,
):
    count, size = buf.shape[0], buf.shape[1]

    def copy(i):
        return pltpu.make_async_copy(recv.at[i, pl.ds(base, size)], buf.at[i], sems.at[i])

    def start(i, carry):
        copy(i).start()
        return carry

    lax.fori_loop(0, count, start, 0, unroll=8)
    work = (pr, u_ref, normed, weight, weight_sem)
    smalls = (s0, s1, s2, s3, s4, s5, s6)
    rows = late_share(0, weight_ref, smalls, work, buf, lambda i: copy(i).wait())
    columns = out.shape[2]
    for p in range(out.shape[0]):
        share[p] = jnp.dot(
            rows, weight[:, pl.ds(p * columns, columns)], preferred_element_type=jnp.float32
        )
    share_copy = pltpu.make_async_copy(share, out, share_sem)
    share_copy.start()
    late_update(0, ids, s0, u_ref, buf, new, new_states, out_sems, lambda i: None)
    share_copy.wait()


def late_second(
    recv, weight_ref, s0, s1, s2, s3, s4, s5, s6, other_ref, sent, kept, u_ref,
    pr, normed, weight, other, weight_sem, other_sem,
):
    other_copy = pltpu.make_async_copy(other_ref, other, other_sem)
    other_copy.start()
    work = (pr, u_ref, normed, weight, weight_sem)
    smalls = (s0, s1, s2, s3, s4, s5, s6)
    rows = late_share(1, weight_ref, smalls, work, recv, lambda i: None)
    other_copy.wait()
    columns = sent.shape[2]
    core = lax.rem(lax.axis_index("head"), 2)
    for out, c in ((sent, 1 - core), (kept, core)):
        for j in range(sent.shape[0]):
            p = 2 * j + c
            at = pl.multiple_of(p * columns, columns)
            out[j] = other[p] + jnp.dot(
                rows, weight[:, pl.ds(at, columns)], preferred_element_type=jnp.float32
            )


def renew(half, place, xs, u, buf, new, r):
    dim = LANES
    steps = xs.shape[1] // 2
    wide = lambda v: v.astype(jnp.float32)
    k_high, k_low = split(xs[r, 0:steps, pl.ds(half * dim, dim)])
    rows = u[r, :, pl.ds(2 * place * dim, 2 * dim)]
    u_high, u_low = split(rows[0:steps])
    left = jnp.concatenate([wide(k_high), wide(k_high), wide(k_low), wide(k_low)], axis=0)
    right = jnp.concatenate([wide(u_high), wide(u_low), wide(u_high), wide(u_low)], axis=0)
    change = jnp.dot(
        left.T.astype(jnp.bfloat16),
        right.astype(jnp.bfloat16),
        preferred_element_type=jnp.float32,
    )
    for h in range(2):
        at = pl.ds((2 * place + h) * dim, dim)
        lanes = slice(h * dim, (h + 1) * dim)
        new[r, at, :] = buf[r, at, :] * rows[steps : steps + 1, lanes] + change[:, lanes]


def update_last(ids, recv, xs, u, before, out, new, out_sems):
    late_update(1, ids, xs, u, recv, new, out, out_sems, lambda i: None)


def merge_rows(ids, early_kept, early_got, late_kept, late_got, o0, o1, o2, o3):
    outs = (o0, o1, o2, o3)
    chips = len(outs)
    chip = lax.axis_index("head") // 2
    count = ids.shape[1]
    steps = late_kept.shape[1] // count
    slots = early_kept.shape[1] // steps
    put = one_hot(slots, ids[1:2, :])
    arrived = jnp.sum(put, axis=1, keepdims=True) > 0.0
    for k in range(chips):
        j = lax.rem(chip + k, chips)
        for t in range(steps):
            rows = pl.ds(t * slots, slots)
            few = pl.ds(t * count, count)
            late = exact(put, late_kept[j, few, :] + late_got[j, few, :])
            early = early_kept[j, rows, :] + early_got[j, rows, :]
            outs[k][rows, :] = jnp.where(arrived, late, early)


def finish_rows(live, t0, t1, t2, t3, out):
    steps, slots = out.shape[0], out.shape[1]
    is_live = lax.broadcasted_iota(jnp.int32, (slots, 1), 0) < live[0]
    for t in range(steps):
        rows = pl.ds(t * slots, slots)
        total = (t0[rows, :] + t1[rows, :]) + (t2[rows, :] + t3[rows, :])
        out[t] = jnp.where(is_live, total, 0.0).astype(out.dtype)


def swap(v):
    parts = lax.axis_size("head")
    return lax.ppermute(v, "head", [(i, i ^ 1) for i in range(parts)])


def onward(v, k):
    parts = lax.axis_size("head")
    return lax.ppermute(v, "head", [(i, (i + 2 * k) % parts) for i in range(parts)])


def shards(
    hidden_in, w_query, w_key, w_value, w_gate_z, w_write, w_decay,
    conv_query, conv_key, conv_value, decay_rate, dt_bias, norm_gain, w_out,
    states, tail_query, tail_key, tail_value, send_slot, recv_slot, live_count,
):
    slots, steps, width = hidden_in.shape
    heads, dim = states.shape[1], states.shape[2]
    f32 = jnp.float32
    shape = jax.ShapeDtypeStruct
    size = heads * dim
    half = size // 2
    old = states.reshape(slots, size, dim)
    step_major = lambda v: jnp.transpose(v, (1, 0, 2))
    tails = [step_major(t) for t in (tail_query, tail_key, tail_value)]
    taps = tails[0].shape[0]
    extra = 2 * taps * sum(t.shape[2] for t in tails) // LANES
    send = jnp.transpose(send_slot[0], (1, 0))
    groups = send.shape[1]

    first_shape = (groups, size + half + extra, LANES)
    second_shape = (groups, half, LANES)

    def exchange(v):
        return lax.all_to_all(v, "group", split_axis=0, concat_axis=0, tiled=True)

    def first_exchange(send, send_ref, old, *tails):
        out1, out2 = pl.pallas_call(
            pack,
            out_shape=[pltpu.VMEM(first_shape, f32), pltpu.HBM(second_shape, f32)],
            in_specs=[SMEM] + [HBM] * 5,
            out_specs=[VMEM, HBM],
            scratch_shapes=[
                pltpu.VMEM((groups, half, LANES), f32),
                *[pltpu.VMEM(t.shape, f32) for t in tails],
                pltpu.VMEM(send.shape, jnp.int32),
                pltpu.VMEM((groups, extra, LANES), f32),
                pltpu.SemaphoreType.DMA((4,)),
                pltpu.SemaphoreType.DMA((groups,)),
                pltpu.SemaphoreType.DMA((2,)),
            ],
            compiler_params=params(24),
            cost_estimate=cost(0, 4 * groups * size * LANES * 4),
            name="pack",
        )(send, in_hbm(send_ref), in_hbm(old), *[in_hbm(t) for t in tails])
        return exchange(out1), out2

    def no_exchange(*_):
        return jnp.zeros(first_shape, f32), jnp.zeros(second_shape, f32)

    tie = lax.optimization_barrier
    recv1, out2 = lax.cond(
        live_count[0] >= 0, first_exchange, no_exchange, send, send, old, *tails
    )
    recv1, out2 = tie((recv1, out2))
    recv2 = exchange(out2)

    recv = jnp.transpose(recv_slot[0], (1, 0))
    flat_hidden = step_major(hidden_in).reshape(steps * slots, width)

    def project(weight):
        product = jnp.dot(flat_hidden, weight, preferred_element_type=f32)
        return product.reshape(steps, slots, weight.shape[1])

    pq, pk, pv, pg = (project(w) for w in (w_query, w_key, w_value, w_gate_z))
    pw, pd = project(w_write), project(w_decay)
    key_width, value_width = pq.shape[2], pv.shape[2]
    (
        xt, xs, values, rates, xt_late, xs_late, v_late, g_late, rates_late, live_late,
        ntq, ntk, ntv,
    ) = pl.pallas_call(
        prepare,
        out_shape=[
            pltpu.HBM((2 * steps, slots, key_width), f32),
            pltpu.HBM((slots, 2 * steps, key_width), f32),
            pltpu.HBM((steps, slots, value_width), f32),
            pltpu.HBM((steps, slots, 2 * heads), f32),
            pltpu.VMEM((2 * steps, groups, key_width), f32),
            pltpu.VMEM((groups, 2 * steps, key_width), f32),
            pltpu.VMEM((steps, groups, value_width), f32),
            pltpu.VMEM((steps, groups, value_width), f32),
            pltpu.VMEM((steps, groups, 2 * heads), f32),
            pltpu.VMEM((groups, LANES), f32),
            *[pltpu.HBM(t.shape, f32) for t in tails],
        ],
        in_specs=[VMEM, SMEM] + [HBM] * 4 + [VMEM] * 3 + [HBM] + [VMEM] * 7,
        out_specs=[VMEM] * 13,
        scratch_shapes=[
            *[pltpu.VMEM(t.shape, f32) for t in tails],
            pltpu.VMEM((groups, extra, LANES), f32),
            pltpu.VMEM(pg.shape, f32),
            pltpu.SemaphoreType.DMA((5,)),
        ],
        compiler_params=params(16),
        cost_estimate=cost(2_000_000, 4_000_000),
        name="prepare",
    )(
        recv, live_count, in_hbm(recv1), *[in_hbm(t) for t in tails], pq, pk, pv, in_hbm(pg), pw, pd,
        conv_query, conv_key, conv_value,
        decay_rate.reshape(1, heads), dt_bias.reshape(1, heads),
    )
    gain = norm_gain.reshape(1, dim)

    parts = lax.axis_size("head")
    columns = width // parts
    weight = in_hbm(w_out)
    early_args = [in_hbm(v) for v in (xs, xt, values, pg, rates, gain)]
    early_shape = (parts // 2, steps * slots, columns)
    sent, kept, new_states = pl.pallas_call(
        early_rows,
        out_shape=[
            pltpu.VMEM(early_shape, f32),
            pltpu.VMEM(early_shape, f32),
            pltpu.HBM((slots, size, dim), f32),
        ],
        in_specs=[SMEM, SMEM] + [HBM] * 9,
        out_specs=[VMEM, VMEM, HBM],
        scratch_shapes=[
            *[pltpu.VMEM(v.shape, f32) for v in early_args],
            pltpu.SMEM((slots,), jnp.int32),
            pltpu.VMEM((slots, size, dim), f32),
            pltpu.VMEM((slots, size, dim), f32),
            pltpu.VMEM((slots, 2 * steps, size), f32),
            pltpu.VMEM((slots, 2 * steps, size), f32),
            pltpu.VMEM((steps, slots, size), jnp.bfloat16),
            pltpu.VMEM((size, width), jnp.bfloat16),
            pltpu.SemaphoreType.DMA((6,)),
            pltpu.SemaphoreType.DMA((slots,)),
            pltpu.SemaphoreType.DMA((slots,)),
            pltpu.SemaphoreType.DMA,
        ],
        compiler_params=params(32),
        cost_estimate=cost(500_000_000, 22_000_000),
        name="early_rows",
    )(recv, live_count, in_hbm(old), in_hbm(recv1), weight, *early_args)
    swapped = swap(sent)

    late_args = [
        in_vmem(v) for v in (xs_late, xt_late, v_late, g_late, rates_late, live_late, gain)
    ]
    pieces_shape = (parts, steps * groups, columns)
    work = [
        pltpu.VMEM((groups, 2 * steps, half), f32),
        pltpu.VMEM((groups, 2 * steps, half), f32),
        pltpu.VMEM((steps, groups, half), jnp.bfloat16),
        pltpu.VMEM((half, width), jnp.bfloat16),
    ]
    pieces, new_states = pl.pallas_call(
        functools.partial(late_first, size),
        out_shape=[pltpu.HBM(pieces_shape, f32), pltpu.HBM((slots, size, dim), f32)],
        in_specs=[SMEM, HBM, HBM] + [VMEM] * 7 + [HBM],
        out_specs=[HBM, HBM],
        scratch_shapes=[
            pltpu.VMEM((groups, half, dim), f32),
            *work,
            pltpu.VMEM((groups, half, dim), f32),
            pltpu.VMEM(pieces_shape, f32),
            pltpu.SemaphoreType.DMA((groups,)),
            pltpu.SemaphoreType.DMA,
            pltpu.SemaphoreType.DMA((groups,)),
            pltpu.SemaphoreType.DMA,
        ],
        input_output_aliases={10: 1},
        compiler_params=params(16),
        cost_estimate=cost(200_000_000, 8_000_000),
        name="late_first",
    )(recv, in_hbm(recv1), weight, *late_args, new_states)
    recv2, new_states = tie((recv2, new_states))
    recv2 = in_vmem(recv2)
    late_shape = (parts // 2, steps * groups, columns)
    late_sent, late_kept, u_last = pl.pallas_call(
        late_second,
        out_shape=[
            pltpu.VMEM(late_shape, f32),
            pltpu.VMEM(late_shape, f32),
            pltpu.VMEM((groups, 2 * steps, half), f32),
        ],
        in_specs=[VMEM, HBM] + [VMEM] * 7 + [HBM],
        out_specs=[VMEM] * 3,
        scratch_shapes=[
            work[0],
            *work[2:],
            pltpu.VMEM(pieces_shape, f32),
            pltpu.SemaphoreType.DMA,
            pltpu.SemaphoreType.DMA,
        ],
        compiler_params=params(16),
        cost_estimate=cost(150_000_000, 5_000_000),
        name="late_second",
    )(recv2, weight, *late_args, in_hbm(pieces))
    chips = parts // 2
    rows_shape = (steps * slots, columns)
    terms = pl.pallas_call(
        merge_rows,
        out_shape=[pltpu.VMEM(rows_shape, f32)] * chips,
        in_specs=[VMEM] * 5,
        out_specs=[VMEM] * chips,
        compiler_params=params(16),
        cost_estimate=cost(2_000_000, 3_000_000),
        name="merge_rows",
    )(recv, in_vmem(kept), swapped, in_vmem(late_kept), swap(late_sent))
    terms = [terms[0]] + [onward(terms[k], k) for k in range(1, chips)]
    new_states = pl.pallas_call(
        update_last,
        out_shape=pltpu.HBM((slots, size, dim), f32),
        in_specs=[SMEM] + [VMEM] * 3 + [HBM],
        out_specs=HBM,
        scratch_shapes=[
            pltpu.VMEM((groups, half, dim), f32),
            pltpu.SemaphoreType.DMA((groups,)),
        ],
        input_output_aliases={4: 0},
        compiler_params=params(16),
        cost_estimate=cost(32_000_000, 2 * groups * half * dim * 4),
        name="update_last",
    )(recv, recv2, late_args[0], in_vmem(u_last), new_states)

    layer_out = pl.pallas_call(
        finish_rows,
        out_shape=shape((steps, slots, columns), jnp.bfloat16),
        in_specs=[SMEM] + [VMEM] * chips,
        out_specs=VMEM,
        compiler_params=params(16),
        cost_estimate=cost(1_000_000, 1_000_000),
        name="finish_rows",
    )(live_count, in_vmem(terms[0]), *terms[1:])
    return (
        step_major(layer_out),
        new_states.reshape(states.shape),
        step_major(ntq),
        step_major(ntk),
        step_major(ntv),
    )


def solution(mesh):
    by_head = P(None, "head")
    by_both = P("group", None, "head")
    return jax.shard_map(
        shards,
        mesh=mesh,
        in_specs=(
            P("group", None, None),
            *([by_head] * 9),
            P("head"),
            P("head"),
            P(),
            P("head", None),
            P("group", "head", None, None),
            by_both,
            by_both,
            by_both,
            P("group", None, None),
            P("group", None, None),
            P("group"),
        ),
        out_specs=(
            by_both,
            P("group", "head", None, None),
            by_both,
            by_both,
            by_both,
        ),
        check_vma=False,
    )
```

```python
import functools

import jax
import jax.numpy as jnp
from jax import lax
from jax.experimental import pallas as pl
from jax.experimental.pallas import tpu as pltpu
from jax.sharding import PartitionSpec as P

SMEM = pl.BlockSpec(memory_space=pltpu.SMEM)
VMEM = pl.BlockSpec(memory_space=pltpu.VMEM)
HBM = pl.BlockSpec(memory_space=pltpu.HBM)
ANY = pl.BlockSpec(memory_space=pl.ANY)
LANES = 128


def params(mib):
    return pltpu.CompilerParams(vmem_limit_bytes=mib * 1024 * 1024)


def cost(flops, moved):
    return pl.CostEstimate(flops=flops, bytes_accessed=moved, transcendentals=0)


def in_hbm(v):
    return pltpu.with_memory_space_constraint(v, pltpu.HBM)


def in_vmem(v):
    return pltpu.with_memory_space_constraint(v, pltpu.VMEM)


def wait_all(ref, sem):
    pltpu.make_async_copy(ref, ref, sem).wait()


def load(refs, bufs, sems):
    copies = [
        pltpu.make_async_copy(ref, buf, sems.at[n]) for n, (ref, buf) in enumerate(zip(refs, bufs))
    ]
    for copy in copies:
        copy.start()
    return copies


def exact(a, b):
    return jnp.dot(a, b, precision=lax.Precision.HIGHEST, preferred_element_type=jnp.float32)


def exact_t(a, b):
    return lax.dot_general(
        a, b, (((0,), (0,)), ((), ())),
        precision=lax.Precision.HIGHEST, preferred_element_type=jnp.float32,
    )


def one_hot(slots, ids):
    hit = lax.broadcasted_iota(jnp.int32, (slots, ids.shape[1]), 0) == ids
    return hit.astype(jnp.float32)


def split(v):
    high = v.astype(jnp.bfloat16)
    return high, (v - high.astype(jnp.float32)).astype(jnp.bfloat16)


def pack(
    send, ids_ref, states, tq, tk, tv, out1, out2,
    buf, bq, bk, bv, ids, rows, tail_sems, in_sems, sems,
):
    groups, slots, size = send.shape[1], states.shape[0], states.shape[1]
    rest = out2.shape[1]
    lower = size - rest
    extra = rows.shape[1]
    held = (bq, bk, bv)
    tails = load((tq, tk, tv, ids_ref), (bq, bk, bv, ids), tail_sems)

    def upper(g, carry):
        slot = jnp.maximum(send[1, g], 0)
        pltpu.make_async_copy(
            states.at[slot, pl.ds(lower, rest)], buf.at[g], in_sems.at[g]
        ).start()
        return carry

    def second(g, carry):
        slot = jnp.maximum(send[1, g], 0)
        pltpu.make_async_copy(
            states.at[slot, pl.ds(0, lower)], out1.at[g, pl.ds(size, lower)], sems.at[0]
        ).start()
        return carry

    def first(g, carry):
        slot = jnp.maximum(send[0, g], 0)
        pltpu.make_async_copy(
            states.at[slot], out1.at[g, pl.ds(0, size)], sems.at[0]
        ).start()
        return carry

    lax.fori_loop(0, groups, upper, 0, unroll=8)
    lax.fori_loop(0, groups, first, 0, unroll=8)
    lax.fori_loop(0, groups, second, 0, unroll=8)

    def move(g, carry):
        pltpu.make_async_copy(
            states.at[0, pl.ds(lower, rest)], buf.at[g], in_sems.at[g]
        ).wait()
        pltpu.make_async_copy(buf.at[g], out2.at[g], sems.at[1]).start()
        return carry

    lax.fori_loop(0, groups, move, 0, unroll=4)
    for copy in tails:
        copy.wait()
    pick = jnp.concatenate([one_hot(slots, ids[c : c + 1, :]) for c in range(2)], axis=1)
    table = jnp.concatenate([ref[j] for j in range(tq.shape[0]) for ref in held], axis=1)
    chosen = exact_t(pick, table)
    for at in range(extra // 2):
        part = chosen[:, at * LANES : (at + 1) * LANES]
        rows[:, at, :] = part[0:groups]
        rows[:, extra // 2 + at, :] = part[groups:]
    pltpu.make_async_copy(rows, out1.at[:, pl.ds(size + lower, extra)], sems.at[0]).start()
    wait_all(out1, sems.at[0])
    wait_all(out2, sems.at[1])


def prepare(
    ids, live, recv, tq, tk, tv, pq, pk, pv, pg, pw, pd, cq, ck, cv, pace, bias,
    xt, xs, v_ref, rates, xt_late, xs_late, v_late, g_late, rates_late, live_late,
    ntq, ntk, ntv, bq, bk, bv, rows, gate, sems,
):
    held = (bq, bk, bv)
    copies = [
        pltpu.make_async_copy(ref, dst, sems.at[n])
        for n, (ref, dst) in enumerate(zip((tq, tk, tv), held))
    ]
    extra = rows.shape[1]
    copies.append(
        pltpu.make_async_copy(recv.at[:, pl.ds(recv.shape[1] - extra, extra)], rows, sems.at[3])
    )
    copies.append(pltpu.make_async_copy(pg, gate, sems.at[4]))
    for copy in copies:
        copy.start()
    taps, slots = tq.shape[0], tq.shape[1]
    puts = [one_hot(slots, ids[c : c + 1, :]) for c in range(2)]
    put = jnp.concatenate(puts, axis=1)
    arrived = jnp.sum(put, axis=1, keepdims=True) > 0.0
    late = puts[1]
    steps = pq.shape[0]
    is_live = lax.broadcasted_iota(jnp.int32, (slots, 1), 0) < live[0]
    heads = pw.shape[2]
    for t in range(steps):
        x = pd[t] + bias[...]
        soft = jnp.maximum(x, 0.0) + jnp.log1p(jnp.exp(-jnp.abs(x)))
        rates[t, :, 0:heads] = jnp.exp(-pace[...] * soft)
        rates[t, :, heads : 2 * heads] = jax.nn.sigmoid(pw[t])
        rates_late[t] = exact_t(late, rates[t])
    live_late[...] = exact_t(
        late, jnp.broadcast_to(is_live.astype(jnp.float32), (slots, LANES))
    )
    for copy in copies:
        copy.wait()
    for t in range(steps):
        g_late[t] = exact_t(late, gate[t])
    moved = {n: [] for n in range(3)}
    at = 0
    for j in range(taps):
        for n, ref in enumerate(held):
            groups = ref.shape[2] // LANES
            sent = [
                jnp.concatenate([rows[:, at + c + g, :] for g in range(groups)], axis=1)
                for c in (0, extra // 2)
            ]
            at += groups
            sent = exact(put, jnp.concatenate(sent, axis=0))
            moved[n].append(jnp.where(arrived, sent, ref[j]))

    def conv(before, proj, kernel, new):
        kernel = kernel[...].astype(jnp.float32)
        window = before + [proj[t] for t in range(steps)]
        outs = []
        for t in range(steps):
            mixed = window[t] * kernel[0:1, :]
            for j in range(1, taps + 1):
                mixed = mixed + window[t + j] * kernel[j : j + 1, :]
            outs.append(mixed * jax.nn.sigmoid(mixed))
        for j in range(taps):
            new[j] = jnp.where(is_live, window[steps + j], window[j])
        return outs

    def unit(v, scale):
        parts = []
        for h in range(v.shape[1] // LANES):
            part = v[:, h * LANES : (h + 1) * LANES]
            total = jnp.sum(part * part, axis=1, keepdims=True)
            parts.append(part * (lax.rsqrt(total + 1e-06) * scale))
        return jnp.concatenate(parts, axis=1)

    queries = [unit(v, LANES**-0.5) for v in conv(moved[0], pq, cq, ntq)]
    keys = [unit(v, 1.0) for v in conv(moved[1], pk, ck, ntk)]
    for n, v in enumerate(keys + queries):
        xt[n] = v
        xs[:, n, :] = v
        v = exact_t(late, v)
        xt_late[n] = v
        xs_late[:, n, :] = v
    for t, v in enumerate(conv(moved[2], pv, cv, ntv)):
        v_ref[t] = v
        v_late[t] = exact_t(late, v)


def solve(halves, is_live, xt, v_ref, gate, rates, gain, normed, u_ref, pr):
    dim = LANES
    steps = v_ref.shape[0]
    slots = v_ref.shape[1]
    heads = rates.shape[2] // 2
    inner = lambda a, b: jnp.sum(a * b, axis=1, keepdims=True)
    for n, half in enumerate(halves):
        key_lanes = pl.ds(half * dim, dim)
        keys = [xt[t, :, key_lanes] for t in range(steps)]
        queries = [xt[steps + t, :, key_lanes] for t in range(steps)]
        kk = {(s, t): inner(keys[s], keys[t]) for t in range(steps) for s in range(t)}
        kq = {(s, t): inner(keys[s], queries[t]) for t in range(steps) for s in range(t + 1)}
        for h in range(2):
            head = 2 * half + h
            lanes = pl.ds((2 * n + h) * dim, dim)
            wide = pl.ds(head * dim, dim)
            fall = [rates[t, :, head : head + 1] for t in range(steps)]
            rate = [rates[t, :, heads + head : heads + head + 1] for t in range(steps)]
            ratio = {}
            for s in range(steps):
                for t in range(s + 1, steps):
                    ratio[s, t] = fall[t] if t == s + 1 else ratio[s, t - 1] * fall[t]
            total = [fall[0]]
            for t in range(1, steps):
                total.append(total[-1] * fall[t])
            us = []
            for t in range(steps):
                gap = v_ref[t, :, wide] - total[t] * pr[:, t, lanes]
                for s in range(t):
                    gap = gap - (ratio[s, t] * kk[s, t]) * us[s]
                us.append(gap * rate[t])
                out = total[t] * pr[:, steps + t, lanes]
                for s in range(t + 1):
                    weight = kq[s, t] if s == t else ratio[s, t] * kq[s, t]
                    out = out + weight * us[s]
                mean = jnp.mean(out * out, axis=1, keepdims=True)
                z = gate[t, :, wide]
                out = out * lax.rsqrt(mean + 1e-06) * gain[...] * (z * jax.nn.sigmoid(z))
                normed[t, :, lanes] = out.astype(normed.dtype)
            for s in range(steps):
                last = us[s] if s == steps - 1 else ratio[s, steps - 1] * us[s]
                u_ref[:, s, lanes] = jnp.where(is_live, last, 0.0)
            u_ref[:, steps, lanes] = jnp.broadcast_to(
                jnp.where(is_live, total[-1], 1.0), (slots, dim)
            )


def products(halves, xs, buf, pr, wait):
    dim = LANES
    batch = 16 // len(halves) if buf.shape[0] == 16 else 8 // len(halves)

    def some(k, carry):
        for i in range(batch):
            wait(k * batch + i)
        for i in range(batch):
            r = k * batch + i
            for n, half in enumerate(halves):
                state = jnp.concatenate(
                    [buf[r, pl.ds((2 * n + h) * dim, dim), :] for h in range(2)], axis=1
                )
                high, low = split(state)
                both = jnp.concatenate(split(xs[r, :, pl.ds(half * dim, dim)]), axis=0)
                a = jnp.dot(both, high, preferred_element_type=jnp.float32)
                a = a + jnp.dot(both, low, preferred_element_type=jnp.float32)
                rows = both.shape[0] // 2
                pr[r, :, pl.ds(2 * n * dim, 2 * dim)] = a[0:rows] + a[rows:]
        return carry

    lax.fori_loop(0, buf.shape[0] // batch, some, 0)


def sources(ids, src):
    groups = ids.shape[1]

    def clear(r, carry):
        src[r] = -1
        return carry

    lax.fori_loop(0, src.shape[0], clear, 0, unroll=8)
    for c in range(2):

        def put(g, carry, c=c):
            @pl.when(ids[c, g] >= 0)
            def _():
                src[ids[c, g]] = g if c == 0 else -2

            return carry

        lax.fori_loop(0, groups, put, 0, unroll=4)


def fetch(src, states, recv, buf, sems):
    slots, size = states.shape[0], states.shape[1]

    def start(r, carry):
        @pl.when(src[r] >= 0)
        def _():
            pltpu.make_async_copy(
                recv.at[src[r], pl.ds(0, size)], buf.at[r], sems.at[r]
            ).start()

        @pl.when(src[r] < 0)
        def _():
            pltpu.make_async_copy(states.at[r], buf.at[r], sems.at[r]).start()

        return carry

    lax.fori_loop(0, slots, start, 0)


def early_rows(
    ids, live, states, recv, weight_ref, s0, s1, s2, s3, s4, s5,
    sent, kept, new_states, h0, h1, h2, h3, h4, h5,
    src, buf, new, pr, u_ref, normed, weight,
    small_sems, sems, out_sems, weight_sem,
):
    slots, size = buf.shape[0], buf.shape[1]
    halves = tuple(range(size // (2 * LANES)))
    held = (h0, h1, h2, h3, h4, h5)
    xs, xt, v_ref, gate, rates, gain = held
    copies = load((s0, s1, s2, s3, s4, s5), held, small_sems)
    sources(ids, src)
    fetch(src, states, recv, buf, sems)
    for copy in copies:
        copy.wait()
    weight_copy = pltpu.make_async_copy(weight_ref, weight, weight_sem)
    weight_copy.start()
    wait = lambda r: pltpu.make_async_copy(states.at[0], buf.at[r], sems.at[r]).wait()
    products(halves, xs, buf, pr, wait)
    is_live = lax.broadcasted_iota(jnp.int32, (slots, 1), 0) < live[0]
    solve(halves, is_live, xt, v_ref, gate, rates, gain, normed, u_ref, pr)
    batch = 4

    def some(k, carry):
        for i in range(batch):
            for n in halves:
                renew(n, n, xs, u_ref, buf, new, k * batch + i)
        for i in range(batch):
            r = k * batch + i

            @pl.when(src[r] >= -1)
            def _():
                pltpu.make_async_copy(new.at[r], new_states.at[r], out_sems.at[r]).start()

        return carry

    lax.fori_loop(0, slots // batch, some, 0)
    rows = jnp.concatenate([normed[t] for t in range(normed.shape[0])], axis=0)
    columns = sent.shape[2]
    core = lax.rem(lax.axis_index("head"), 2)
    weight_copy.wait()
    for out, c in ((sent, 1 - core), (kept, core)):
        for j in range(sent.shape[0]):
            at = pl.multiple_of((2 * j + c) * columns, columns)
            out[j] = jnp.dot(
                rows, weight[:, pl.ds(at, columns)], preferred_element_type=jnp.float32
            )

    def finish(r, carry):
        @pl.when(src[r] >= -1)
        def _():
            pltpu.make_async_copy(new.at[r], new_states.at[r], out_sems.at[r]).wait()

        return carry

    lax.fori_loop(0, slots, finish, 0)


def late_share(half, weight_ref, smalls, work, buf, wait):
    pr, u_ref, normed, weight, weight_sem = work
    size = buf.shape[1]
    weight_copy = pltpu.make_async_copy(
        weight_ref.at[pl.ds(half * size, size)], weight, weight_sem
    )
    weight_copy.start()
    xs, xt, v_ref, gate, rates, live, gain = smalls
    products((half,), xs, buf, pr, wait)
    is_live = live[:, 0:1] > 0.5
    solve((half,), is_live, xt, v_ref, gate, rates, gain, normed, u_ref, pr)
    rows = jnp.concatenate([normed[t] for t in range(normed.shape[0])], axis=0)
    weight_copy.wait()
    return rows


def late_update(half, ids, xs, u, buf, new, out, sems, wait):
    count, size = buf.shape[0], buf.shape[1]
    rows = pl.ds(half * size, size)
    batch = 8

    def some(k, carry):
        for j in range(batch):
            wait(k * batch + j)
        for j in range(batch):
            renew(half, 0, xs, u, buf, new, k * batch + j)
        for j in range(batch):
            i = k * batch + j

            @pl.when(ids[1, i] >= 0)
            def _():
                pltpu.make_async_copy(
                    new.at[i], out.at[ids[1, i], rows], sems.at[i]
                ).start()

        return carry

    lax.fori_loop(0, count // batch, some, 0)

    def finish(i, carry):
        @pl.when(ids[1, i] >= 0)
        def _():
            pltpu.make_async_copy(new.at[i], out.at[0, rows], sems.at[i]).wait()

        return carry

    lax.fori_loop(0, count, finish, 0)


def late_first(
    base, ids, recv, weight_ref, s0, s1, s2, s3, s4, s5, s6, before, out, new_states,
    buf, pr, u_ref, normed, weight, new, share, sems, weight_sem, out_sems, share_sem,
):
    count, size = buf.shape[0], buf.shape[1]

    def copy(i):
        return pltpu.make_async_copy(recv.at[i, pl.ds(base, size)], buf.at[i], sems.at[i])

    def start(i, carry):
        copy(i).start()
        return carry

    lax.fori_loop(0, count, start, 0, unroll=8)
    work = (pr, u_ref, normed, weight, weight_sem)
    smalls = (s0, s1, s2, s3, s4, s5, s6)
    rows = late_share(0, weight_ref, smalls, work, buf, lambda i: copy(i).wait())
    columns = out.shape[2]
    for p in range(out.shape[0]):
        share[p] = jnp.dot(
            rows, weight[:, pl.ds(p * columns, columns)], preferred_element_type=jnp.float32
        )
    share_copy = pltpu.make_async_copy(share, out, share_sem)
    share_copy.start()
    late_update(0, ids, s0, u_ref, buf, new, new_states, out_sems, lambda i: None)
    share_copy.wait()


def late_second(
    recv, weight_ref, s0, s1, s2, s3, s4, s5, s6, other_ref, sent, kept, u_ref,
    pr, normed, weight, other, weight_sem, other_sem,
):
    other_copy = pltpu.make_async_copy(other_ref, other, other_sem)
    other_copy.start()
    work = (pr, u_ref, normed, weight, weight_sem)
    smalls = (s0, s1, s2, s3, s4, s5, s6)
    rows = late_share(1, weight_ref, smalls, work, recv, lambda i: None)
    other_copy.wait()
    columns = sent.shape[2]
    core = lax.rem(lax.axis_index("head"), 2)
    for out, c in ((sent, 1 - core), (kept, core)):
        for j in range(sent.shape[0]):
            p = 2 * j + c
            at = pl.multiple_of(p * columns, columns)
            out[j] = other[p] + jnp.dot(
                rows, weight[:, pl.ds(at, columns)], preferred_element_type=jnp.float32
            )


def renew(half, place, xs, u, buf, new, r):
    dim = LANES
    steps = xs.shape[1] // 2
    wide = lambda v: v.astype(jnp.float32)
    k_high, k_low = split(xs[r, 0:steps, pl.ds(half * dim, dim)])
    rows = u[r, :, pl.ds(2 * place * dim, 2 * dim)]
    u_high, u_low = split(rows[0:steps])
    left = jnp.concatenate([wide(k_high), wide(k_high), wide(k_low), wide(k_low)], axis=0)
    right = jnp.concatenate([wide(u_high), wide(u_low), wide(u_high), wide(u_low)], axis=0)
    change = jnp.dot(
        left.T.astype(jnp.bfloat16),
        right.astype(jnp.bfloat16),
        preferred_element_type=jnp.float32,
    )
    for h in range(2):
        at = pl.ds((2 * place + h) * dim, dim)
        lanes = slice(h * dim, (h + 1) * dim)
        new[r, at, :] = buf[r, at, :] * rows[steps : steps + 1, lanes] + change[:, lanes]


def update_last(ids, recv, xs, u, before, out, new, out_sems):
    late_update(1, ids, xs, u, recv, new, out, out_sems, lambda i: None)


def merge_rows(ids, early_kept, early_got, late_kept, late_got, o0, o1, o2, o3):
    outs = (o0, o1, o2, o3)
    chips = len(outs)
    chip = lax.axis_index("head") // 2
    count = ids.shape[1]
    steps = late_kept.shape[1] // count
    slots = early_kept.shape[1] // steps
    put = one_hot(slots, ids[1:2, :])
    arrived = jnp.sum(put, axis=1, keepdims=True) > 0.0
    for k in range(chips):
        j = lax.rem(chip + k, chips)
        few = [pl.ds(t * count, count) for t in range(steps)]
        late = [late_kept[j, at, :] + late_got[j, at, :] for at in few]
        late = exact(put, jnp.concatenate(late, axis=1))
        columns = o0.shape[1]
        for t in range(steps):
            rows = pl.ds(t * slots, slots)
            early = early_kept[j, rows, :] + early_got[j, rows, :]
            placed = late[:, t * columns : (t + 1) * columns]
            outs[k][rows, :] = jnp.where(arrived, placed, early)


def finish_rows(live, t0, t1, t2, t3, out):
    steps, slots = out.shape[0], out.shape[1]
    is_live = lax.broadcasted_iota(jnp.int32, (slots, 1), 0) < live[0]
    for t in range(steps):
        rows = pl.ds(t * slots, slots)
        total = (t0[rows, :] + t1[rows, :]) + (t2[rows, :] + t3[rows, :])
        out[t] = jnp.where(is_live, total, 0.0).astype(out.dtype)


def swap(v):
    parts = lax.axis_size("head")
    return lax.ppermute(v, "head", [(i, i ^ 1) for i in range(parts)])


def onward(v, k):
    parts = lax.axis_size("head")
    return lax.ppermute(v, "head", [(i, (i + 2 * k) % parts) for i in range(parts)])


def shards(
    hidden_in, w_query, w_key, w_value, w_gate_z, w_write, w_decay,
    conv_query, conv_key, conv_value, decay_rate, dt_bias, norm_gain, w_out,
    states, tail_query, tail_key, tail_value, send_slot, recv_slot, live_count,
):
    slots, steps, width = hidden_in.shape
    heads, dim = states.shape[1], states.shape[2]
    f32 = jnp.float32
    shape = jax.ShapeDtypeStruct
    size = heads * dim
    half = size // 2
    old = states.reshape(slots, size, dim)
    step_major = lambda v: jnp.transpose(v, (1, 0, 2))
    tails = [step_major(t) for t in (tail_query, tail_key, tail_value)]
    taps = tails[0].shape[0]
    extra = 2 * taps * sum(t.shape[2] for t in tails) // LANES
    send = jnp.transpose(send_slot[0], (1, 0))
    groups = send.shape[1]

    first_shape = (groups, size + half + extra, LANES)
    second_shape = (groups, half, LANES)

    def exchange(v):
        return lax.all_to_all(v, "group", split_axis=0, concat_axis=0, tiled=True)

    def first_exchange(send, send_ref, old, *tails):
        out1, out2 = pl.pallas_call(
            pack,
            out_shape=[pltpu.VMEM(first_shape, f32), pltpu.HBM(second_shape, f32)],
            in_specs=[SMEM] + [HBM] * 5,
            out_specs=[VMEM, HBM],
            scratch_shapes=[
                pltpu.VMEM((groups, half, LANES), f32),
                *[pltpu.VMEM(t.shape, f32) for t in tails],
                pltpu.VMEM(send.shape, jnp.int32),
                pltpu.VMEM((groups, extra, LANES), f32),
                pltpu.SemaphoreType.DMA((4,)),
                pltpu.SemaphoreType.DMA((groups,)),
                pltpu.SemaphoreType.DMA((2,)),
            ],
            compiler_params=params(24),
            cost_estimate=cost(0, 4 * groups * size * LANES * 4),
            name="pack",
        )(send, in_hbm(send_ref), in_hbm(old), *[in_hbm(t) for t in tails])
        return exchange(out1), out2

    def no_exchange(*_):
        return jnp.zeros(first_shape, f32), jnp.zeros(second_shape, f32)

    tie = lax.optimization_barrier
    recv1, out2 = lax.cond(
        lax.axis_index("group") < lax.axis_size("group"),
        first_exchange, no_exchange, send, send, old, *tails,
    )
    recv1, out2 = tie((recv1, out2))
    recv2 = exchange(out2)

    recv = jnp.transpose(recv_slot[0], (1, 0))
    flat_hidden = step_major(hidden_in).reshape(steps * slots, width)

    def project(weight):
        product = jnp.dot(flat_hidden, weight, preferred_element_type=f32)
        return product.reshape(steps, slots, weight.shape[1])

    pq, pk, pv, pg = (project(w) for w in (w_query, w_key, w_value, w_gate_z))
    pw, pd = project(w_write), project(w_decay)
    key_width, value_width = pq.shape[2], pv.shape[2]
    (
        xt, xs, values, rates, xt_late, xs_late, v_late, g_late, rates_late, live_late,
        ntq, ntk, ntv,
    ) = pl.pallas_call(
        prepare,
        out_shape=[
            pltpu.HBM((2 * steps, slots, key_width), f32),
            pltpu.HBM((slots, 2 * steps, key_width), f32),
            pltpu.HBM((steps, slots, value_width), f32),
            pltpu.HBM((steps, slots, 2 * heads), f32),
            pltpu.VMEM((2 * steps, groups, key_width), f32),
            pltpu.VMEM((groups, 2 * steps, key_width), f32),
            pltpu.VMEM((steps, groups, value_width), f32),
            pltpu.VMEM((steps, groups, value_width), f32),
            pltpu.VMEM((steps, groups, 2 * heads), f32),
            pltpu.VMEM((groups, LANES), f32),
            *[pltpu.HBM(t.shape, f32) for t in tails],
        ],
        in_specs=[VMEM, SMEM] + [HBM] * 4 + [VMEM] * 3 + [HBM] + [VMEM] * 7,
        out_specs=[VMEM] * 13,
        scratch_shapes=[
            *[pltpu.VMEM(t.shape, f32) for t in tails],
            pltpu.VMEM((groups, extra, LANES), f32),
            pltpu.VMEM(pg.shape, f32),
            pltpu.SemaphoreType.DMA((5,)),
        ],
        compiler_params=params(16),
        cost_estimate=cost(2_000_000, 4_000_000),
        name="prepare",
    )(
        recv, live_count, in_hbm(recv1), *[in_hbm(t) for t in tails], pq, pk, pv, in_hbm(pg), pw, pd,
        conv_query, conv_key, conv_value,
        decay_rate.reshape(1, heads), dt_bias.reshape(1, heads),
    )
    gain = norm_gain.reshape(1, dim)

    parts = lax.axis_size("head")
    columns = width // parts
    weight = in_hbm(w_out)
    early_args = [in_hbm(v) for v in (xs, xt, values, pg, rates, gain)]
    early_shape = (parts // 2, steps * slots, columns)
    sent, kept, new_states = pl.pallas_call(
        early_rows,
        out_shape=[
            pltpu.VMEM(early_shape, f32),
            pltpu.VMEM(early_shape, f32),
            pltpu.HBM((slots, size, dim), f32),
        ],
        in_specs=[SMEM, SMEM] + [HBM] * 9,
        out_specs=[VMEM, VMEM, HBM],
        scratch_shapes=[
            *[pltpu.VMEM(v.shape, f32) for v in early_args],
            pltpu.SMEM((slots,), jnp.int32),
            pltpu.VMEM((slots, size, dim), f32),
            pltpu.VMEM((slots, size, dim), f32),
            pltpu.VMEM((slots, 2 * steps, size), f32),
            pltpu.VMEM((slots, 2 * steps, size), f32),
            pltpu.VMEM((steps, slots, size), jnp.bfloat16),
            pltpu.VMEM((size, width), jnp.bfloat16),
            pltpu.SemaphoreType.DMA((6,)),
            pltpu.SemaphoreType.DMA((slots,)),
            pltpu.SemaphoreType.DMA((slots,)),
            pltpu.SemaphoreType.DMA,
        ],
        compiler_params=params(32),
        cost_estimate=cost(500_000_000, 22_000_000),
        name="early_rows",
    )(recv, live_count, in_hbm(old), in_hbm(recv1), weight, *early_args)
    swapped = swap(sent)

    late_args = [
        in_vmem(v) for v in (xs_late, xt_late, v_late, g_late, rates_late, live_late, gain)
    ]
    pieces_shape = (parts, steps * groups, columns)
    work = [
        pltpu.VMEM((groups, 2 * steps, half), f32),
        pltpu.VMEM((groups, 2 * steps, half), f32),
        pltpu.VMEM((steps, groups, half), jnp.bfloat16),
        pltpu.VMEM((half, width), jnp.bfloat16),
    ]
    pieces, new_states = pl.pallas_call(
        functools.partial(late_first, size),
        out_shape=[pltpu.HBM(pieces_shape, f32), pltpu.HBM((slots, size, dim), f32)],
        in_specs=[SMEM, HBM, HBM] + [VMEM] * 7 + [HBM],
        out_specs=[HBM, HBM],
        scratch_shapes=[
            pltpu.VMEM((groups, half, dim), f32),
            *work,
            pltpu.VMEM((groups, half, dim), f32),
            pltpu.VMEM(pieces_shape, f32),
            pltpu.SemaphoreType.DMA((groups,)),
            pltpu.SemaphoreType.DMA,
            pltpu.SemaphoreType.DMA((groups,)),
            pltpu.SemaphoreType.DMA,
        ],
        input_output_aliases={10: 1},
        compiler_params=params(16),
        cost_estimate=cost(200_000_000, 8_000_000),
        name="late_first",
    )(recv, in_hbm(recv1), weight, *late_args, new_states)
    recv2, new_states = tie((recv2, new_states))
    recv2 = in_vmem(recv2)
    late_shape = (parts // 2, steps * groups, columns)
    late_sent, late_kept, u_last = pl.pallas_call(
        late_second,
        out_shape=[
            pltpu.VMEM(late_shape, f32),
            pltpu.VMEM(late_shape, f32),
            pltpu.VMEM((groups, 2 * steps, half), f32),
        ],
        in_specs=[VMEM, HBM] + [VMEM] * 7 + [HBM],
        out_specs=[VMEM] * 3,
        scratch_shapes=[
            work[0],
            *work[2:],
            pltpu.VMEM(pieces_shape, f32),
            pltpu.SemaphoreType.DMA,
            pltpu.SemaphoreType.DMA,
        ],
        compiler_params=params(16),
        cost_estimate=cost(150_000_000, 5_000_000),
        name="late_second",
    )(recv2, weight, *late_args, in_hbm(pieces))
    chips = parts // 2
    rows_shape = (steps * slots, columns)
    terms = pl.pallas_call(
        merge_rows,
        out_shape=[pltpu.VMEM(rows_shape, f32)] * chips,
        in_specs=[VMEM] * 5,
        out_specs=[VMEM] * chips,
        compiler_params=params(16),
        cost_estimate=cost(2_000_000, 3_000_000),
        name="merge_rows",
    )(recv, in_vmem(kept), swapped, in_vmem(late_kept), swap(late_sent))
    terms = [terms[0]] + [onward(terms[k], k) for k in range(1, chips)]
    new_states = pl.pallas_call(
        update_last,
        out_shape=pltpu.HBM((slots, size, dim), f32),
        in_specs=[SMEM] + [VMEM] * 3 + [HBM],
        out_specs=HBM,
        scratch_shapes=[
            pltpu.VMEM((groups, half, dim), f32),
            pltpu.SemaphoreType.DMA((groups,)),
        ],
        input_output_aliases={4: 0},
        compiler_params=params(16),
        cost_estimate=cost(32_000_000, 2 * groups * half * dim * 4),
        name="update_last",
    )(recv, recv2, late_args[0], in_vmem(u_last), new_states)

    layer_out = pl.pallas_call(
        finish_rows,
        out_shape=shape((steps, slots, columns), jnp.bfloat16),
        in_specs=[SMEM] + [VMEM] * chips,
        out_specs=VMEM,
        compiler_params=params(16),
        cost_estimate=cost(1_000_000, 1_000_000),
        name="finish_rows",
    )(live_count, in_vmem(terms[0]), *terms[1:])
    return (
        step_major(layer_out),
        new_states.reshape(states.shape),
        step_major(ntq),
        step_major(ntk),
        step_major(ntv),
    )


def solution(mesh):
    by_head = P(None, "head")
    by_both = P("group", None, "head")
    return jax.shard_map(
        shards,
        mesh=mesh,
        in_specs=(
            P("group", None, None),
            *([by_head] * 9),
            P("head"),
            P("head"),
            P(),
            P("head", None),
            P("group", "head", None, None),
            by_both,
            by_both,
            by_both,
            P("group", None, None),
            P("group", None, None),
            P("group"),
        ),
        out_specs=(
            by_both,
            P("group", "head", None, None),
            by_both,
            by_both,
            by_both,
        ),
        check_vma=False,
    )
```

```python
import functools

import jax
import jax.numpy as jnp
from jax import lax
from jax.experimental import pallas as pl
from jax.experimental.pallas import tpu as pltpu
from jax.sharding import PartitionSpec as P

SMEM = pl.BlockSpec(memory_space=pltpu.SMEM)
VMEM = pl.BlockSpec(memory_space=pltpu.VMEM)
HBM = pl.BlockSpec(memory_space=pltpu.HBM)
ANY = pl.BlockSpec(memory_space=pl.ANY)
LANES = 128


def params(mib):
    return pltpu.CompilerParams(vmem_limit_bytes=mib * 1024 * 1024)


def cost(flops, moved):
    return pl.CostEstimate(flops=flops, bytes_accessed=moved, transcendentals=0)


def in_hbm(v):
    return pltpu.with_memory_space_constraint(v, pltpu.HBM)


def in_vmem(v):
    return pltpu.with_memory_space_constraint(v, pltpu.VMEM)


def wait_all(ref, sem):
    pltpu.make_async_copy(ref, ref, sem).wait()


def load(refs, bufs, sems):
    copies = [
        pltpu.make_async_copy(ref, buf, sems.at[n]) for n, (ref, buf) in enumerate(zip(refs, bufs))
    ]
    for copy in copies:
        copy.start()
    return copies


def exact(a, b):
    return jnp.dot(a, b, precision=lax.Precision.HIGHEST, preferred_element_type=jnp.float32)


def exact_t(a, b):
    return lax.dot_general(
        a, b, (((0,), (0,)), ((), ())),
        precision=lax.Precision.HIGHEST, preferred_element_type=jnp.float32,
    )


def one_hot(slots, ids):
    hit = lax.broadcasted_iota(jnp.int32, (slots, ids.shape[1]), 0) == ids
    return hit.astype(jnp.float32)


def split(v):
    high = v.astype(jnp.bfloat16)
    return high, (v - high.astype(jnp.float32)).astype(jnp.bfloat16)


def pack(
    send, ids_ref, states, tq, tk, tv, out1, out2,
    buf, bq, bk, bv, ids, rows, tail_sems, in_sems, sems,
):
    groups, slots, size = send.shape[1], states.shape[0], states.shape[1]
    rest = out2.shape[1]
    lower = size - rest
    extra = rows.shape[1]
    held = (bq, bk, bv)
    tails = load((tq, tk, tv, ids_ref), (bq, bk, bv, ids), tail_sems)

    def upper(g, carry):
        slot = jnp.maximum(send[1, g], 0)
        pltpu.make_async_copy(
            states.at[slot, pl.ds(lower, rest)], buf.at[g], in_sems.at[g]
        ).start()
        return carry

    def second(g, carry):
        slot = jnp.maximum(send[1, g], 0)
        pltpu.make_async_copy(
            states.at[slot, pl.ds(0, lower)], out1.at[g, pl.ds(size, lower)], sems.at[0]
        ).start()
        return carry

    def first(g, carry):
        slot = jnp.maximum(send[0, g], 0)
        pltpu.make_async_copy(
            states.at[slot], out1.at[g, pl.ds(0, size)], sems.at[0]
        ).start()
        return carry

    lax.fori_loop(0, groups, upper, 0, unroll=8)
    lax.fori_loop(0, groups, first, 0, unroll=8)
    lax.fori_loop(0, groups, second, 0, unroll=8)

    def move(g, carry):
        pltpu.make_async_copy(
            states.at[0, pl.ds(lower, rest)], buf.at[g], in_sems.at[g]
        ).wait()
        pltpu.make_async_copy(buf.at[g], out2.at[g], sems.at[1]).start()
        return carry

    lax.fori_loop(0, groups, move, 0, unroll=4)
    for copy in tails:
        copy.wait()
    pick = jnp.concatenate([one_hot(slots, ids[c : c + 1, :]) for c in range(2)], axis=1)
    table = jnp.concatenate([ref[j] for j in range(tq.shape[0]) for ref in held], axis=1)
    chosen = exact_t(pick, table)
    for at in range(extra // 2):
        part = chosen[:, at * LANES : (at + 1) * LANES]
        rows[:, at, :] = part[0:groups]
        rows[:, extra // 2 + at, :] = part[groups:]
    pltpu.make_async_copy(rows, out1.at[:, pl.ds(size + lower, extra)], sems.at[0]).start()
    wait_all(out1, sems.at[0])
    wait_all(out2, sems.at[1])


def prepare(
    ids, live, recv, tq, tk, tv, pq, pk, pv, pg, pw, pd, cq, ck, cv, pace, bias,
    xt, xs, v_ref, rates, xt_late, xs_late, v_late, g_late, rates_late, live_late,
    ntq, ntk, ntv, bq, bk, bv, rows, gate, sems,
):
    held = (bq, bk, bv)
    copies = [
        pltpu.make_async_copy(ref, dst, sems.at[n])
        for n, (ref, dst) in enumerate(zip((tq, tk, tv), held))
    ]
    extra = rows.shape[1]
    copies.append(
        pltpu.make_async_copy(recv.at[:, pl.ds(recv.shape[1] - extra, extra)], rows, sems.at[3])
    )
    copies.append(pltpu.make_async_copy(pg, gate, sems.at[4]))
    for copy in copies:
        copy.start()
    taps, slots = tq.shape[0], tq.shape[1]
    puts = [one_hot(slots, ids[c : c + 1, :]) for c in range(2)]
    put = jnp.concatenate(puts, axis=1)
    arrived = jnp.sum(put, axis=1, keepdims=True) > 0.0
    late = puts[1]
    steps = pq.shape[0]
    is_live = lax.broadcasted_iota(jnp.int32, (slots, 1), 0) < live[0]
    heads = pw.shape[2]
    for t in range(steps):
        x = pd[t] + bias[...]
        soft = jnp.maximum(x, 0.0) + jnp.log1p(jnp.exp(-jnp.abs(x)))
        rates[t, :, 0:heads] = jnp.exp(-pace[...] * soft)
        rates[t, :, heads : 2 * heads] = jax.nn.sigmoid(pw[t])
        rates_late[t] = exact_t(late, rates[t])
    live_late[...] = exact_t(
        late, jnp.broadcast_to(is_live.astype(jnp.float32), (slots, LANES))
    )
    for copy in copies:
        copy.wait()
    for t in range(steps):
        g_late[t] = exact_t(late, gate[t])
    moved = {n: [] for n in range(3)}
    at = 0
    for j in range(taps):
        for n, ref in enumerate(held):
            groups = ref.shape[2] // LANES
            sent = [
                jnp.concatenate([rows[:, at + c + g, :] for g in range(groups)], axis=1)
                for c in (0, extra // 2)
            ]
            at += groups
            sent = exact(put, jnp.concatenate(sent, axis=0))
            moved[n].append(jnp.where(arrived, sent, ref[j]))

    def conv(before, proj, kernel, new):
        kernel = kernel[...].astype(jnp.float32)
        window = before + [proj[t] for t in range(steps)]
        outs = []
        for t in range(steps):
            mixed = window[t] * kernel[0:1, :]
            for j in range(1, taps + 1):
                mixed = mixed + window[t + j] * kernel[j : j + 1, :]
            outs.append(mixed * jax.nn.sigmoid(mixed))
        for j in range(taps):
            new[j] = jnp.where(is_live, window[steps + j], window[j])
        return outs

    def unit(v, scale):
        parts = []
        for h in range(v.shape[1] // LANES):
            part = v[:, h * LANES : (h + 1) * LANES]
            total = jnp.sum(part * part, axis=1, keepdims=True)
            parts.append(part * (lax.rsqrt(total + 1e-06) * scale))
        return jnp.concatenate(parts, axis=1)

    queries = [unit(v, LANES**-0.5) for v in conv(moved[0], pq, cq, ntq)]
    keys = [unit(v, 1.0) for v in conv(moved[1], pk, ck, ntk)]
    for n, v in enumerate(keys + queries):
        xt[n] = v
        xs[:, n, :] = v
        v = exact_t(late, v)
        xt_late[n] = v
        xs_late[:, n, :] = v
    for t, v in enumerate(conv(moved[2], pv, cv, ntv)):
        v_ref[t] = v
        v_late[t] = exact_t(late, v)


def solve(halves, is_live, xt, v_ref, gate, rates, gain, normed, u_ref, pr):
    dim = LANES
    steps = v_ref.shape[0]
    slots = v_ref.shape[1]
    heads = rates.shape[2] // 2
    inner = lambda a, b: jnp.sum(a * b, axis=1, keepdims=True)
    for n, half in enumerate(halves):
        key_lanes = pl.ds(half * dim, dim)
        keys = [xt[t, :, key_lanes] for t in range(steps)]
        queries = [xt[steps + t, :, key_lanes] for t in range(steps)]
        kk = {(s, t): inner(keys[s], keys[t]) for t in range(steps) for s in range(t)}
        kq = {(s, t): inner(keys[s], queries[t]) for t in range(steps) for s in range(t + 1)}
        for h in range(2):
            head = 2 * half + h
            lanes = pl.ds((2 * n + h) * dim, dim)
            wide = pl.ds(head * dim, dim)
            fall = [rates[t, :, head : head + 1] for t in range(steps)]
            rate = [rates[t, :, heads + head : heads + head + 1] for t in range(steps)]
            ratio = {}
            for s in range(steps):
                for t in range(s + 1, steps):
                    ratio[s, t] = fall[t] if t == s + 1 else ratio[s, t - 1] * fall[t]
            total = [fall[0]]
            for t in range(1, steps):
                total.append(total[-1] * fall[t])
            us = []
            for t in range(steps):
                gap = v_ref[t, :, wide] - total[t] * pr[:, t, lanes]
                for s in range(t):
                    gap = gap - (ratio[s, t] * kk[s, t]) * us[s]
                us.append(gap * rate[t])
                out = total[t] * pr[:, steps + t, lanes]
                for s in range(t + 1):
                    weight = kq[s, t] if s == t else ratio[s, t] * kq[s, t]
                    out = out + weight * us[s]
                mean = jnp.mean(out * out, axis=1, keepdims=True)
                z = gate[t, :, wide]
                out = out * lax.rsqrt(mean + 1e-06) * gain[...] * (z * jax.nn.sigmoid(z))
                normed[t, :, lanes] = out.astype(normed.dtype)
            for s in range(steps):
                last = us[s] if s == steps - 1 else ratio[s, steps - 1] * us[s]
                u_ref[:, s, lanes] = jnp.where(is_live, last, 0.0)
            u_ref[:, steps, lanes] = jnp.broadcast_to(
                jnp.where(is_live, total[-1], 1.0), (slots, dim)
            )


def products(halves, xs, buf, pr, wait):
    dim = LANES
    batch = 16 // len(halves) if buf.shape[0] == 16 else 8 // len(halves)

    def some(k, carry):
        for i in range(batch):
            wait(k * batch + i)
        for i in range(batch):
            r = k * batch + i
            for n, half in enumerate(halves):
                state = jnp.concatenate(
                    [buf[r, pl.ds((2 * n + h) * dim, dim), :] for h in range(2)], axis=1
                )
                high, low = split(state)
                both = jnp.concatenate(split(xs[r, :, pl.ds(half * dim, dim)]), axis=0)
                a = jnp.dot(both, high, preferred_element_type=jnp.float32)
                a = a + jnp.dot(both, low, preferred_element_type=jnp.float32)
                rows = both.shape[0] // 2
                pr[r, :, pl.ds(2 * n * dim, 2 * dim)] = a[0:rows] + a[rows:]
        return carry

    lax.fori_loop(0, buf.shape[0] // batch, some, 0)


def sources(ids, src):
    groups = ids.shape[1]

    def clear(r, carry):
        src[r] = -1
        return carry

    lax.fori_loop(0, src.shape[0], clear, 0, unroll=8)
    for c in range(2):

        def put(g, carry, c=c):
            @pl.when(ids[c, g] >= 0)
            def _():
                src[ids[c, g]] = g if c == 0 else -2

            return carry

        lax.fori_loop(0, groups, put, 0, unroll=4)


def fetch(src, states, recv, buf, sems):
    slots, size = states.shape[0], states.shape[1]

    def start(r, carry):
        @pl.when(src[r] >= 0)
        def _():
            pltpu.make_async_copy(
                recv.at[src[r], pl.ds(0, size)], buf.at[r], sems.at[r]
            ).start()

        @pl.when(src[r] < 0)
        def _():
            pltpu.make_async_copy(states.at[r], buf.at[r], sems.at[r]).start()

        return carry

    lax.fori_loop(0, slots, start, 0)


def early_rows(
    ids, live, states, recv, weight_ref, s0, s1, s2, s3, s4, s5,
    sent, kept, new_states, h0, h1, h2, h3, h4, h5,
    src, buf, new, pr, u_ref, normed, weight,
    small_sems, sems, out_sems, weight_sem,
):
    slots, size = buf.shape[0], buf.shape[1]
    halves = tuple(range(size // (2 * LANES)))
    held = (h0, h1, h2, h3, h4, h5)
    xs, xt, v_ref, gate, rates, gain = held
    copies = load((s0, s1, s2, s3, s4, s5), held, small_sems)
    sources(ids, src)
    fetch(src, states, recv, buf, sems)
    for copy in copies:
        copy.wait()
    weight_copy = pltpu.make_async_copy(weight_ref, weight, weight_sem)
    weight_copy.start()
    wait = lambda r: pltpu.make_async_copy(states.at[0], buf.at[r], sems.at[r]).wait()
    products(halves, xs, buf, pr, wait)
    is_live = lax.broadcasted_iota(jnp.int32, (slots, 1), 0) < live[0]
    solve(halves, is_live, xt, v_ref, gate, rates, gain, normed, u_ref, pr)
    batch = 4

    def some(k, carry):
        for i in range(batch):
            for n in halves:
                renew(n, n, xs, u_ref, buf, new, k * batch + i)
        for i in range(batch):
            r = k * batch + i

            @pl.when(src[r] >= -1)
            def _():
                pltpu.make_async_copy(new.at[r], new_states.at[r], out_sems.at[r]).start()

        return carry

    lax.fori_loop(0, slots // batch, some, 0)
    rows = jnp.concatenate([normed[t] for t in range(normed.shape[0])], axis=0)
    columns = sent.shape[2]
    core = lax.rem(lax.axis_index("head"), 2)
    weight_copy.wait()
    for out, c in ((sent, 1 - core), (kept, core)):
        for j in range(sent.shape[0]):
            at = pl.multiple_of((2 * j + c) * columns, columns)
            out[j] = jnp.dot(
                rows, weight[:, pl.ds(at, columns)], preferred_element_type=jnp.float32
            )

    def finish(r, carry):
        @pl.when(src[r] >= -1)
        def _():
            pltpu.make_async_copy(new.at[r], new_states.at[r], out_sems.at[r]).wait()

        return carry

    lax.fori_loop(0, slots, finish, 0)


def late_share(half, weight_ref, smalls, work, buf, wait):
    pr, u_ref, normed, weight, weight_sem = work
    size = buf.shape[1]
    weight_copy = pltpu.make_async_copy(
        weight_ref.at[pl.ds(half * size, size)], weight, weight_sem
    )
    weight_copy.start()
    xs, xt, v_ref, gate, rates, live, gain = smalls
    products((half,), xs, buf, pr, wait)
    is_live = live[:, 0:1] > 0.5
    solve((half,), is_live, xt, v_ref, gate, rates, gain, normed, u_ref, pr)
    rows = jnp.concatenate([normed[t] for t in range(normed.shape[0])], axis=0)
    weight_copy.wait()
    return rows


def late_update(half, ids, xs, u, buf, new, out, sems, wait):
    count, size = buf.shape[0], buf.shape[1]
    rows = pl.ds(half * size, size)
    batch = 8

    def some(k, carry):
        for j in range(batch):
            wait(k * batch + j)
        for j in range(batch):
            renew(half, 0, xs, u, buf, new, k * batch + j)
        for j in range(batch):
            i = k * batch + j

            @pl.when(ids[1, i] >= 0)
            def _():
                pltpu.make_async_copy(
                    new.at[i], out.at[ids[1, i], rows], sems.at[i]
                ).start()

        return carry

    lax.fori_loop(0, count // batch, some, 0)

    def finish(i, carry):
        @pl.when(ids[1, i] >= 0)
        def _():
            pltpu.make_async_copy(new.at[i], out.at[0, rows], sems.at[i]).wait()

        return carry

    lax.fori_loop(0, count, finish, 0)


def late_first(
    base, ids, recv, weight_ref, s0, s1, s2, s3, s4, s5, s6, before, out, new_states,
    buf, pr, u_ref, normed, weight, new, share, sems, weight_sem, out_sems, share_sem,
):
    count, size = buf.shape[0], buf.shape[1]

    def copy(i):
        return pltpu.make_async_copy(recv.at[i, pl.ds(base, size)], buf.at[i], sems.at[i])

    def start(i, carry):
        copy(i).start()
        return carry

    lax.fori_loop(0, count, start, 0, unroll=8)
    work = (pr, u_ref, normed, weight, weight_sem)
    smalls = (s0, s1, s2, s3, s4, s5, s6)
    rows = late_share(0, weight_ref, smalls, work, buf, lambda i: copy(i).wait())
    columns = out.shape[2]
    for p in range(out.shape[0]):
        share[p] = jnp.dot(
            rows, weight[:, pl.ds(p * columns, columns)], preferred_element_type=jnp.float32
        )
    share_copy = pltpu.make_async_copy(share, out, share_sem)
    share_copy.start()
    late_update(0, ids, s0, u_ref, buf, new, new_states, out_sems, lambda i: None)
    share_copy.wait()


def late_second(
    recv, weight_ref, s0, s1, s2, s3, s4, s5, s6, other_ref, sent, kept, u_ref,
    pr, normed, weight, other, weight_sem, other_sem,
):
    other_copy = pltpu.make_async_copy(other_ref, other, other_sem)
    other_copy.start()
    work = (pr, u_ref, normed, weight, weight_sem)
    smalls = (s0, s1, s2, s3, s4, s5, s6)
    rows = late_share(1, weight_ref, smalls, work, recv, lambda i: None)
    other_copy.wait()
    columns = sent.shape[2]
    core = lax.rem(lax.axis_index("head"), 2)
    for out, c in ((sent, 1 - core), (kept, core)):
        for j in range(sent.shape[0]):
            p = 2 * j + c
            at = pl.multiple_of(p * columns, columns)
            out[j] = other[p] + jnp.dot(
                rows, weight[:, pl.ds(at, columns)], preferred_element_type=jnp.float32
            )


def renew(half, place, xs, u, buf, new, r):
    dim = LANES
    steps = xs.shape[1] // 2
    wide = lambda v: v.astype(jnp.float32)
    k_high, k_low = split(xs[r, 0:steps, pl.ds(half * dim, dim)])
    rows = u[r, :, pl.ds(2 * place * dim, 2 * dim)]
    u_high, u_low = split(rows[0:steps])
    left = jnp.concatenate([wide(k_high), wide(k_high), wide(k_low), wide(k_low)], axis=0)
    right = jnp.concatenate([wide(u_high), wide(u_low), wide(u_high), wide(u_low)], axis=0)
    change = jnp.dot(
        left.T.astype(jnp.bfloat16),
        right.astype(jnp.bfloat16),
        preferred_element_type=jnp.float32,
    )
    for h in range(2):
        at = pl.ds((2 * place + h) * dim, dim)
        lanes = slice(h * dim, (h + 1) * dim)
        new[r, at, :] = buf[r, at, :] * rows[steps : steps + 1, lanes] + change[:, lanes]


def update_last(ids, recv, xs, u, before, out, new, out_sems):
    late_update(1, ids, xs, u, recv, new, out, out_sems, lambda i: None)


def merge_rows(ids, early_kept, early_got, late_kept, late_got, o0, o1, o2, o3):
    outs = (o0, o1, o2, o3)
    chips = len(outs)
    chip = lax.axis_index("head") // 2
    count = ids.shape[1]
    steps = late_kept.shape[1] // count
    slots = early_kept.shape[1] // steps
    put = one_hot(slots, ids[1:2, :])
    arrived = jnp.sum(put, axis=1, keepdims=True) > 0.0
    for k in range(chips):
        j = lax.rem(chip + k, chips)
        few = [pl.ds(t * count, count) for t in range(steps)]
        late = [late_kept[j, at, :] + late_got[j, at, :] for at in few]
        late = exact(put, jnp.concatenate(late, axis=1))
        columns = o0.shape[1]
        for t in range(steps):
            rows = pl.ds(t * slots, slots)
            early = early_kept[j, rows, :] + early_got[j, rows, :]
            placed = late[:, t * columns : (t + 1) * columns]
            outs[k][rows, :] = jnp.where(arrived, placed, early)


def finish_rows(live, t0, t1, t2, t3, out):
    steps, slots = out.shape[0], out.shape[1]
    is_live = lax.broadcasted_iota(jnp.int32, (slots, 1), 0) < live[0]
    for t in range(steps):
        rows = pl.ds(t * slots, slots)
        total = (t0[rows, :] + t1[rows, :]) + (t2[rows, :] + t3[rows, :])
        out[t] = jnp.where(is_live, total, 0.0).astype(out.dtype)


def swap(v):
    parts = lax.axis_size("head")
    return lax.ppermute(v, "head", [(i, i ^ 1) for i in range(parts)])


def onward(v, k):
    parts = lax.axis_size("head")
    return lax.ppermute(v, "head", [(i, (i + 2 * k) % parts) for i in range(parts)])


def shards(
    hidden_in, w_query, w_key, w_value, w_gate_z, w_write, w_decay,
    conv_query, conv_key, conv_value, decay_rate, dt_bias, norm_gain, w_out,
    states, tail_query, tail_key, tail_value, send_slot, recv_slot, live_count,
):
    slots, steps, width = hidden_in.shape
    heads, dim = states.shape[1], states.shape[2]
    f32 = jnp.float32
    shape = jax.ShapeDtypeStruct
    size = heads * dim
    half = size // 2
    old = states.reshape(slots, size, dim)
    step_major = lambda v: jnp.transpose(v, (1, 0, 2))
    tails = [step_major(t) for t in (tail_query, tail_key, tail_value)]
    taps = tails[0].shape[0]
    extra = 2 * taps * sum(t.shape[2] for t in tails) // LANES
    send = jnp.transpose(send_slot[0], (1, 0))
    groups = send.shape[1]

    first_shape = (groups, size + half + extra, LANES)
    second_shape = (groups, half, LANES)

    def exchange(v):
        return lax.all_to_all(v, "group", split_axis=0, concat_axis=0, tiled=True)

    def first_exchange(send, send_ref, old, *tails):
        out1, out2 = pl.pallas_call(
            pack,
            out_shape=[pltpu.VMEM(first_shape, f32), pltpu.HBM(second_shape, f32)],
            in_specs=[SMEM] + [HBM] * 5,
            out_specs=[VMEM, HBM],
            scratch_shapes=[
                pltpu.VMEM((groups, half, LANES), f32),
                *[pltpu.VMEM(t.shape, f32) for t in tails],
                pltpu.VMEM(send.shape, jnp.int32),
                pltpu.VMEM((groups, extra, LANES), f32),
                pltpu.SemaphoreType.DMA((4,)),
                pltpu.SemaphoreType.DMA((groups,)),
                pltpu.SemaphoreType.DMA((2,)),
            ],
            compiler_params=params(24),
            cost_estimate=cost(0, 4 * groups * size * LANES * 4),
            name="pack",
        )(send, in_hbm(send_ref), in_hbm(old), *[in_hbm(t) for t in tails])
        return exchange(out1), out2

    def no_exchange(*_):
        return jnp.zeros(first_shape, f32), jnp.zeros(second_shape, f32)

    tie = lax.optimization_barrier
    recv1, out2 = lax.cond(
        lax.axis_index("group") < lax.axis_size("group"),
        first_exchange, no_exchange, send, send, old, *tails,
    )
    recv1, out2 = tie((recv1, out2))
    recv2 = exchange(out2)

    recv = jnp.transpose(recv_slot[0], (1, 0))
    flat_hidden = step_major(hidden_in).reshape(steps * slots, width)

    def project(weight):
        product = jnp.dot(flat_hidden, weight, preferred_element_type=f32)
        return product.reshape(steps, slots, weight.shape[1])

    pq, pk, pv, pg = (project(w) for w in (w_query, w_key, w_value, w_gate_z))
    pw, pd = project(w_write), project(w_decay)
    key_width, value_width = pq.shape[2], pv.shape[2]
    (
        xt, xs, values, rates, xt_late, xs_late, v_late, g_late, rates_late, live_late,
        ntq, ntk, ntv,
    ) = pl.pallas_call(
        prepare,
        out_shape=[
            pltpu.HBM((2 * steps, slots, key_width), f32),
            pltpu.HBM((slots, 2 * steps, key_width), f32),
            pltpu.HBM((steps, slots, value_width), f32),
            pltpu.HBM((steps, slots, 2 * heads), f32),
            pltpu.VMEM((2 * steps, groups, key_width), f32),
            pltpu.VMEM((groups, 2 * steps, key_width), f32),
            pltpu.VMEM((steps, groups, value_width), f32),
            pltpu.VMEM((steps, groups, value_width), f32),
            pltpu.VMEM((steps, groups, 2 * heads), f32),
            pltpu.VMEM((groups, LANES), f32),
            *[pltpu.HBM(t.shape, f32) for t in tails],
        ],
        in_specs=[VMEM, SMEM] + [HBM] * 4 + [VMEM] * 3 + [HBM] + [VMEM] * 7,
        out_specs=[VMEM] * 13,
        scratch_shapes=[
            *[pltpu.VMEM(t.shape, f32) for t in tails],
            pltpu.VMEM((groups, extra, LANES), f32),
            pltpu.VMEM(pg.shape, f32),
            pltpu.SemaphoreType.DMA((5,)),
        ],
        compiler_params=params(16),
        cost_estimate=cost(2_000_000, 4_000_000),
        name="prepare",
    )(
        recv, live_count, in_hbm(recv1), *[in_hbm(t) for t in tails], pq, pk, pv, in_hbm(pg), pw, pd,
        conv_query, conv_key, conv_value,
        decay_rate.reshape(1, heads), dt_bias.reshape(1, heads),
    )
    gain = norm_gain.reshape(1, dim)

    parts = lax.axis_size("head")
    columns = width // parts
    weight = in_hbm(w_out)
    early_args = [in_hbm(v) for v in (xs, xt, values, pg, rates, gain)]
    early_shape = (parts // 2, steps * slots, columns)
    sent, kept, new_states = pl.pallas_call(
        early_rows,
        out_shape=[
            pltpu.VMEM(early_shape, f32),
            pltpu.VMEM(early_shape, f32),
            pltpu.HBM((slots, size, dim), f32),
        ],
        in_specs=[SMEM, SMEM] + [HBM] * 9,
        out_specs=[VMEM, VMEM, HBM],
        scratch_shapes=[
            *[pltpu.VMEM(v.shape, f32) for v in early_args],
            pltpu.SMEM((slots,), jnp.int32),
            pltpu.VMEM((slots, size, dim), f32),
            pltpu.VMEM((slots, size, dim), f32),
            pltpu.VMEM((slots, 2 * steps, size), f32),
            pltpu.VMEM((slots, 2 * steps, size), f32),
            pltpu.VMEM((steps, slots, size), jnp.bfloat16),
            pltpu.VMEM((size, width), jnp.bfloat16),
            pltpu.SemaphoreType.DMA((6,)),
            pltpu.SemaphoreType.DMA((slots,)),
            pltpu.SemaphoreType.DMA((slots,)),
            pltpu.SemaphoreType.DMA,
        ],
        compiler_params=params(32),
        cost_estimate=cost(500_000_000, 22_000_000),
        name="early_rows",
    )(recv, live_count, in_hbm(old), in_hbm(recv1), weight, *early_args)
    swapped = swap(sent)

    late_args = [
        in_vmem(v) for v in (xs_late, xt_late, v_late, g_late, rates_late, live_late, gain)
    ]
    pieces_shape = (parts, steps * groups, columns)
    work = [
        pltpu.VMEM((groups, 2 * steps, half), f32),
        pltpu.VMEM((groups, 2 * steps, half), f32),
        pltpu.VMEM((steps, groups, half), jnp.bfloat16),
        pltpu.VMEM((half, width), jnp.bfloat16),
    ]
    pieces, new_states = pl.pallas_call(
        functools.partial(late_first, size),
        out_shape=[pltpu.HBM(pieces_shape, f32), pltpu.HBM((slots, size, dim), f32)],
        in_specs=[SMEM, HBM, HBM] + [VMEM] * 7 + [HBM],
        out_specs=[HBM, HBM],
        scratch_shapes=[
            pltpu.VMEM((groups, half, dim), f32),
            *work,
            pltpu.VMEM((groups, half, dim), f32),
            pltpu.VMEM(pieces_shape, f32),
            pltpu.SemaphoreType.DMA((groups,)),
            pltpu.SemaphoreType.DMA,
            pltpu.SemaphoreType.DMA((groups,)),
            pltpu.SemaphoreType.DMA,
        ],
        input_output_aliases={10: 1},
        compiler_params=params(16),
        cost_estimate=cost(200_000_000, 8_000_000),
        name="late_first",
    )(recv, in_hbm(recv1), weight, *late_args, new_states)
    recv2, new_states = tie((recv2, new_states))
    recv2 = in_vmem(recv2)
    late_shape = (parts // 2, steps * groups, columns)
    late_sent, late_kept, u_last = pl.pallas_call(
        late_second,
        out_shape=[
            pltpu.VMEM(late_shape, f32),
            pltpu.VMEM(late_shape, f32),
            pltpu.VMEM((groups, 2 * steps, half), f32),
        ],
        in_specs=[VMEM, HBM] + [VMEM] * 7 + [HBM],
        out_specs=[VMEM] * 3,
        scratch_shapes=[
            work[0],
            *work[2:],
            pltpu.VMEM(pieces_shape, f32),
            pltpu.SemaphoreType.DMA,
            pltpu.SemaphoreType.DMA,
        ],
        compiler_params=params(16),
        cost_estimate=cost(150_000_000, 5_000_000),
        name="late_second",
    )(recv2, weight, *late_args, in_hbm(pieces))
    chips = parts // 2
    rows_shape = (steps * slots, columns)
    terms = pl.pallas_call(
        merge_rows,
        out_shape=[pltpu.VMEM(rows_shape, f32)] * chips,
        in_specs=[VMEM] * 5,
        out_specs=[VMEM] * chips,
        compiler_params=params(16),
        cost_estimate=cost(2_000_000, 3_000_000),
        name="merge_rows",
    )(recv, in_vmem(kept), swapped, in_vmem(late_kept), swap(late_sent))
    far = sorted(range(1, chips), key=lambda k: -min(k, chips - k))
    arrived = {k: onward(terms[k], k) for k in far}
    terms = [terms[0]] + [arrived[k] for k in far]
    new_states = pl.pallas_call(
        update_last,
        out_shape=pltpu.HBM((slots, size, dim), f32),
        in_specs=[SMEM] + [VMEM] * 3 + [HBM],
        out_specs=HBM,
        scratch_shapes=[
            pltpu.VMEM((groups, half, dim), f32),
            pltpu.SemaphoreType.DMA((groups,)),
        ],
        input_output_aliases={4: 0},
        compiler_params=params(16),
        cost_estimate=cost(32_000_000, 2 * groups * half * dim * 4),
        name="update_last",
    )(recv, recv2, late_args[0], in_vmem(u_last), new_states)

    layer_out = pl.pallas_call(
        finish_rows,
        out_shape=shape((steps, slots, columns), jnp.bfloat16),
        in_specs=[SMEM] + [VMEM] * chips,
        out_specs=VMEM,
        compiler_params=params(16),
        cost_estimate=cost(1_000_000, 1_000_000),
        name="finish_rows",
    )(live_count, in_vmem(terms[0]), *terms[1:])
    return (
        step_major(layer_out),
        new_states.reshape(states.shape),
        step_major(ntq),
        step_major(ntk),
        step_major(ntv),
    )


def solution(mesh):
    by_head = P(None, "head")
    by_both = P("group", None, "head")
    return jax.shard_map(
        shards,
        mesh=mesh,
        in_specs=(
            P("group", None, None),
            *([by_head] * 9),
            P("head"),
            P("head"),
            P(),
            P("head", None),
            P("group", "head", None, None),
            by_both,
            by_both,
            by_both,
            P("group", None, None),
            P("group", None, None),
            P("group"),
        ),
        out_specs=(
            by_both,
            P("group", "head", None, None),
            by_both,
            by_both,
            by_both,
        ),
        check_vma=False,
    )
```
